128 devices in a mesh: wide: 16 (over y, z), narrow: 8 (over x, core).
Axes of the slice: x: 4, y: 4, z: 4, core: 2. Of those that a mesh axis runs over, the one named last changes fastest.
Arguments:
- token_ids: int32 [512, 2, 64], P(('wide', 'narrow')), may hold values from 0 to 501759, as said below
- lengths: int32 [512, 2], P(('wide', 'narrow')), may hold values from 16 to 64
- groups: int32 [512], P(('wide', 'narrow')), may hold values from 0 to 15
- table: bfloat16 [501760, 768], P(('wide', 'narrow')), may hold values from -6 to 6
- w_qkv: bfloat16 [1, 768, 2304], P(None, ('wide', 'narrow')), may hold values from -0.21875 to 0.21875
- w_out: bfloat16 [1, 768, 768], P(None, ('wide', 'narrow')), may hold values from -0.625 to 0.625
- w_up: bfloat16 [1, 768, 3072], P(None, ('wide', 'narrow')), may hold values from -0.21875 to 0.21875
- w_down: bfloat16 [1, 3072, 768], P(None, ('wide', 'narrow')), may hold values from -0.109375 to 0.109375
- gains: bfloat16 [1, 2, 768], P(None, None, ('wide', 'narrow')), may hold values from 0.5 to 1.5
- biases: bfloat16 [1, 10, 768], P(None, None, ('wide', 'narrow')), may hold values from -1.25 to 1.25
Outputs:
- loss_terms: float32 [512, 2], P(('wide', 'narrow'))
- token_grads: float32 [512, 2, 64, 768], P(('wide', 'narrow'))
- table_grads: float32 [501760, 768], P(('wide', 'narrow'))
- qkv_grads: float32 [1, 768, 2304], P(None, ('wide', 'narrow'))
- out_grads: float32 [1, 768, 768], P(None, ('wide', 'narrow'))
- up_grads: float32 [1, 768, 3072], P(None, ('wide', 'narrow'))
- down_grads: float32 [1, 3072, 768], P(None, ('wide', 'narrow'))
- gain_grads: float32 [1, 2, 768], P(None, None, ('wide', 'narrow'))
- bias_grads: float32 [1, 10, 768], P(None, None, ('wide', 'narrow'))
The draws below stay inside these ranges and needn't reach their ends.
Inputs may be any that keep to these rules, and one draw needn't show every extreme that they name: `token_ids`: split the ids into aligned blocks of 2 * 4 * 64 (the tokens of 4 pairs) and the vocabulary into shards of 3920 consecutive rows: no block has more than 8 ids in one shard, and in every draw one shard holds exactly 8 ids of every block.
All inputs are finite; a program needn't handle non-finite values.
Results may differ from the reference program's by a relative error of at most 0.0095.
Values may be sent and summed in bfloat16 or wider, within the bound.
A program may use at most 192 MiB of HBM per device.

```python
import math
import jax
import jax.numpy as jnp
import numpy as np
from jax import lax

D = 768
HEAD_DIM = 64
FF = 3072
SEQ = 64
LAYERS = 1
GROUPS = 16
VOCAB_DEV = 3920
PAIR_DEV = 4
PAIRS = 512
VOCAB = 501760
CAP = 8
DEVICES = 128


def draw_token_ids(key, part):
    key = jax.random.fold_in(key, 11)
    block_tokens = 2 * PAIR_DEV * SEQ
    slot_total = DEVICES * CAP
    block_total = PAIRS // PAIR_DEV
    first_key, second_key, third_key, fourth_key = jax.random.split(key, 4)
    forced_owner = jax.random.randint(first_key, (), 0, DEVICES)
    slot_index = jnp.arange(slot_total, dtype=jnp.int32)
    noise_vals = jax.random.randint(second_key, (block_total, slot_total), 0, 2 ** 18)
    slot_scores = noise_vals * slot_total + slot_index[None, :]
    slot_scores = jnp.where((slot_index // CAP == forced_owner)[None, :], slot_index[None, :] - slot_total, slot_scores)
    chosen = jnp.argsort(slot_scores, axis=1)[:, :block_tokens].astype(jnp.int32)
    order_noise = jax.random.randint(third_key, (block_total, block_tokens), 0, 2 ** 18)
    order_scores = order_noise * block_tokens + jnp.arange(block_tokens, dtype=jnp.int32)[None, :]
    order_perm = jnp.argsort(order_scores, axis=1)
    chosen = jnp.take_along_axis(chosen, order_perm, axis=1)
    owners = chosen // CAP
    within = jax.random.randint(fourth_key, (block_total, block_tokens), 0, VOCAB_DEV)
    return (owners * VOCAB_DEV + within).reshape(PAIRS, 2, SEQ).astype(jnp.int32)


def touch_ends(drawn, key, low, high):
    longest = drawn.shape.index(max(drawn.shape))
    spots = []
    for shift in (0, 1):
        where = [jax.random.randint(jax.random.fold_in(key, axis), (), 0, length) for axis, length in enumerate(drawn.shape)]
        where[longest] = (where[longest] + shift) % drawn.shape[longest]
        spots.append(tuple(where))
    return drawn.at[spots[0]].set(low).at[spots[1]].set(high)


def shard_levels(stream_key, shape, pieces, low, top_value):
    gain = 1.0
    for position, parts in pieces:
        heights = jax.random.uniform(jax.random.fold_in(jax.random.fold_in(stream_key, 6), position), (parts,), jnp.float32, low / len(pieces), top_value / len(pieces))
        gain = gain * jnp.repeat(jnp.exp(heights), shape[position] // parts).reshape((-1,) + (1,) * (len(shape) - 1 - position))
    return gain


def rank_table(number_of, lean):
    weights = [(1 << 20) // math.isqrt(rank ** lean) + 1 for rank in range(1, number_of + 1)]
    scale = 1 + sum(weights) // (1 << 30)
    return np.cumsum(np.array([max(1, weight // scale) for weight in weights]))


def skewed_ids(key, shape, count, lean):
    table = rank_table(count, lean)
    ticket = jax.random.randint(jax.random.fold_in(key, 1), shape, 0, int(table[count - 1]))
    rank = jnp.searchsorted(jnp.asarray(table, jnp.int32), ticket, side="right")
    return jax.random.permutation(jax.random.fold_in(key, 2), count)[rank].astype(jnp.int32)


def scatter_about(stream_key, extent, deviation, bound, cuts=(), kind=jnp.bfloat16):
    drawn = deviation * jax.random.normal(stream_key, extent, jnp.float32)
    if cuts:
        drawn = drawn * shard_levels(stream_key, extent, cuts, -0.22, 0.18)
    return jnp.clip(drawn, -bound, bound).astype(kind)


def setup_inputs(seed: int = 0) -> dict:
    key_of = jax.random.split(jax.random.key(seed), 11)
    return {
        "token_ids": draw_token_ids(jax.random.fold_in(key_of[10], 71), 0),
        "lengths": touch_ends(jax.random.randint(key_of[1], (PAIRS, 2), SEQ // 4, SEQ + 1), jax.random.fold_in(key_of[1], 1), SEQ // 4, SEQ).astype(jnp.int32),
        "groups": touch_ends(skewed_ids(key_of[2], (PAIRS,), GROUPS, 2), jax.random.fold_in(key_of[2], 3), 0, GROUPS - 1).astype(jnp.int32),
        "table": scatter_about(key_of[3], (VOCAB, D), 1.0, 6.0, ((0, 128),)),
        "w_qkv": scatter_about(key_of[4], (LAYERS, D, 3 * D), D ** -0.5, 0.21875, ((1, 128),)),
        "w_out": scatter_about(key_of[5], (LAYERS, D, D), (D // 8) ** -0.5, 0.625, ((1, 128),)),
        "w_up": scatter_about(key_of[6], (LAYERS, D, FF), D ** -0.5, 0.21875, ((1, 128),)),
        "w_down": scatter_about(key_of[7], (LAYERS, FF, D), FF ** -0.5, 0.109375, ((1, 128),)),
        "gains": jnp.clip(1.0 + 0.1 * jax.random.normal(key_of[8], (LAYERS, 2, D), jnp.float32), 0.5, 1.5).astype(jnp.bfloat16),
        "biases": scatter_about(key_of[9], (LAYERS, 10, D), 0.2, 1.25, ((2, 128),)),
    }


logit_scale = 10.0
margin = 0.3
norm_eps = 1e-12
pool_eps = 1e-06
far_low = -1e+30
highest = lax.Precision.HIGHEST

@jax.custom_vjp
def low(v):
    return lax.optimization_barrier(v.astype(jnp.bfloat16)).astype(jnp.float32)

@jax.custom_vjp
def low_back(v):
    return v

def low_keep(v):
    return (low(v), None)

def low_pass(kept, grad):
    return (grad,)

def back_keep(v):
    return (v, None)

def back_low(kept, grad):
    return (low(grad),)
low.defvjp(low_keep, low_pass)
low_back.defvjp(back_keep, back_low)

def layer_norm(inputs, gain_row, bias_row):
    centred = inputs - lax.optimization_barrier(jnp.mean(inputs, axis=-1, keepdims=True))
    inverse = lax.rsqrt(lax.optimization_barrier(jnp.mean(centred * centred, axis=-1, keepdims=True)) + norm_eps)
    return centred * inverse * gain_row + bias_row

def pooling(states, sent_lengths):
    token_mask = (jnp.arange(SEQ)[None, :] < sent_lengths[:, None]).astype(jnp.float32)
    mean_vec = lax.optimization_barrier(jnp.sum(states * token_mask[:, :, None], axis=1)) / sent_lengths.astype(jnp.float32)[:, None]
    return mean_vec * lax.rsqrt(lax.optimization_barrier(jnp.sum(mean_vec * mean_vec, axis=-1, keepdims=True)) + pool_eps)

def dense(left, right):
    return jnp.dot(left, right, precision=highest, preferred_element_type=jnp.float32)

def encoder_layer(hidden, key_ok, qkv_w, out_w, up_w, down_w, gain_rows, bias_rows):
    model_width = out_w.shape[1]
    sent_count = key_ok.shape[0]
    hidden_low = low(hidden)
    qkv_bias = jnp.concatenate([bias_rows[0], jnp.zeros_like(bias_rows[0]), bias_rows[1]])
    qkv_all = low_back(low(dense(hidden_low, qkv_w) + qkv_bias))
    qkv_parts = qkv_all.reshape(sent_count, SEQ, 3, model_width // HEAD_DIM, HEAD_DIM)
    scores = jnp.einsum('sqhd,skhd->shqk', qkv_parts[:, :, 0], qkv_parts[:, :, 1], precision=highest) * 0.125
    scores = jnp.where(key_ok[:, None, None, :], low_back(scores), far_low)
    attn_probs = jnp.exp(scores - jax.nn.logsumexp(scores, axis=-1, keepdims=True))
    context = jnp.einsum('shqk,skhd->sqhd', low(attn_probs), qkv_parts[:, :, 2], precision=highest)
    context = low_back(low(context.reshape(-1, model_width)))
    attended = low_back(dense(context, out_w) + bias_rows[2])
    norm_one = layer_norm(hidden + attended, gain_rows[0], bias_rows[3])
    pre_act = low_back(dense(low(norm_one), up_w) + bias_rows[6:].reshape(-1))
    act_low = low(jax.nn.gelu(pre_act, approximate=False))
    ffn_out = low_back(dense(act_low, down_w) + bias_rows[4])
    return layer_norm(norm_one + ffn_out, gain_rows[1], bias_rows[5])

def reference(token_ids, lengths, groups, table, w_qkv, w_out, w_up, w_down, gains, biases):
    flat_ids = token_ids.reshape(-1).astype(jnp.int32)
    sent_lengths = lengths.reshape(-1)
    sent_total = sent_lengths.shape[0]
    block_sents = min(sent_total, 4096 // SEQ)
    block_count = sent_total // block_sents
    key_ok = jnp.arange(SEQ)[None, :] < sent_lengths[:, None]

    def forward(table_f, qkv_f, out_f, up_f, down_f, gain_f, bias_f, offset_f):
        embedded = low_back(jnp.take(table_f, flat_ids, axis=0)) + offset_f
        model_width = embedded.shape[1]

        def block_fn(inputs):
            hidden, block_ok, block_lengths = inputs
            for layer_at in range(LAYERS):
                hidden = encoder_layer(hidden, block_ok, qkv_f[layer_at], out_f[layer_at], up_f[layer_at], down_f[layer_at], gain_f[layer_at], bias_f[layer_at])
            return pooling(hidden.reshape(-1, SEQ, model_width), block_lengths)
        pooled = lax.map(jax.checkpoint(block_fn), (embedded.reshape(block_count, block_sents * SEQ, model_width), key_ok.reshape(block_count, block_sents, SEQ), sent_lengths.reshape(block_count, block_sents)))
        pooled = pooled.reshape(-1, 2, model_width)
        source = pooled[:, 0]
        target = pooled[:, 1]
        pair_total = source.shape[0]
        raw = logit_scale * dense(source, target.T) - logit_scale * margin * jnp.eye(pair_total, dtype=jnp.float32)
        live = groups[:, None] == groups[None, :]
        masked = jnp.where(live, raw, far_low)
        diagonal = logit_scale * lax.optimization_barrier(jnp.sum(source * target, axis=1)) - logit_scale * margin
        row_lse = jax.nn.logsumexp(masked, axis=1)
        col_lse = jax.nn.logsumexp(masked, axis=0)
        terms = jnp.stack([row_lse - diagonal, col_lse - diagonal], axis=1)
        return (jnp.sum(terms) / (2.0 * pair_total), terms)
    zero_offset = jnp.zeros((flat_ids.shape[0], table.shape[1]), jnp.float32)
    total_loss, back_fn, loss_terms = jax.vjp(forward, table.astype(jnp.float32), w_qkv.astype(jnp.float32), w_out.astype(jnp.float32), w_up.astype(jnp.float32), w_down.astype(jnp.float32), gains.astype(jnp.float32), biases.astype(jnp.float32), zero_offset, has_aux=True)
    grads = back_fn(jnp.ones_like(total_loss))
    token_grads = grads[7].reshape(token_ids.shape + (table.shape[1],))
    return (loss_terms, token_grads, grads[0], grads[1], grads[2], grads[3], grads[4], grads[5], grads[6])
```

```python
import functools

import jax
import jax.numpy as jnp
from jax import lax
from jax.experimental import pallas as pl
from jax.experimental.pallas import tpu as pltpu
from jax.sharding import PartitionSpec as P

HEAD_DIM = 64
SEQ = 64
LAYERS = 1


logit_scale = 10.0
margin = 0.3
norm_eps = 1e-12
pool_eps = 1e-06
far_low = -1e30


MESH = pl.DeviceIdType.MESH
RING = 4
ORDERS = ((0, 1, 2), (1, 2, 0), (2, 0, 1))
UNIT = 48


def where_am_i():
    wide = lax.axis_index("wide")
    narrow = lax.axis_index("narrow")
    return [narrow // 2, wide // RING, wide % RING], narrow % 2


def device_at(spot, core):
    return (spot[1] * RING + spot[2], spot[0] * 2 + core)


def moved(spot, dim, by):
    there = list(spot)
    there[dim] = (spot[dim] + by) % RING
    return there


def block_of(ref, part, core, order, spans):
    return ref.at[(part, core, order) + tuple(pl.ds(*spans[d]) for d in range(3))]


def greet(spot, core):
    barrier = pltpu.get_barrier_semaphore()
    others = [(moved(spot, d, by), core) for d in range(3) for by in (1, -1)] + [(spot, 1 - core)]
    for there, c in others:
        pl.semaphore_signal(barrier, inc=1, device_id=device_at(there, c), device_id_type=MESH)
    pl.semaphore_wait(barrier, len(others))


def gather_kernel(rounds, own_ref, out_ref, send_sem, recv_sem, local_sem):
    spot, core = where_am_i()
    sent = []
    greet(spot, core)

    def push(r, o, event, spans, there, c=None, src=None):
        c = core if c is None else c
        dst = block_of(out_ref, r, core, o, spans)
        copy = pltpu.make_async_remote_copy(
            src_ref=dst if src is None else src,
            dst_ref=dst,
            send_sem=send_sem.at[r, o, event],
            recv_sem=recv_sem.at[r, o, event],
            device_id=device_at(there, c),
            device_id_type=MESH,
        )
        copy.start()
        sent.append(copy)

    def landed(r, o, event, spans, c=None):
        c = core if c is None else c
        dst = block_of(out_ref, r, c, o, spans)
        pltpu.make_async_copy(dst, dst, recv_sem.at[r, o, event]).wait()

    def spans_for(o, phase, at, half=None):
        order = ORDERS[o]
        spans = {}
        for k, d in enumerate(order):
            if k < phase:
                spans[d] = (0, RING)
            elif k == phase:
                spans[d] = (at, 1)
            else:
                spans[d] = (spot[d], 1)
        if half is not None:
            spans[order[0]] = (2 * half, 2)
        return spans

    every = [(r, o) for r in range(rounds) for o in range(3)]
    locals_ = []
    for r, o in every:
        d = ORDERS[o][0]
        here = spans_for(o, 0, spot[d])
        mine = block_of(out_ref, r, core, o, here)
        src = own_ref.at[r, o]
        copy = pltpu.make_async_copy(src, mine, local_sem.at[r, o])
        copy.start()
        locals_.append(copy)
        push(r, o, 0, here, moved(spot, d, 1), src=src)
        push(r, o, 1, here, moved(spot, d, -1), src=src)
    for r, o in every:
        d = ORDERS[o][0]
        before = spans_for(o, 0, (spot[d] - 1) % RING)
        landed(r, o, 0, before)
        push(r, o, 2, before, moved(spot, d, 1))

    def spread(r, o, phase):
        d = ORDERS[o][phase]
        here = spans_for(o, phase, spot[d])
        first = 3 + 4 * (phase - 1)
        push(r, o, first, here, moved(spot, d, 1))
        push(r, o, first + 1, here, moved(spot, d, -1))

    def share(r, o, event, spans):
        push(r, o, event, spans, spot, 1 - core)

    def relay(r, o, phase):
        d = ORDERS[o][phase]
        first = 3 + 4 * (phase - 1)
        left, right = (spot[d] - 1) % RING, (spot[d] + 1) % RING
        landed(r, o, first, spans_for(o, phase, left))
        push(r, o, first + 2, spans_for(o, phase, left, 0), moved(spot, d, 1))
        landed(r, o, first + 1, spans_for(o, phase, right))
        push(r, o, first + 3, spans_for(o, phase, right, 1), moved(spot, d, -1))
        share(r, o, 11 + 3 * (phase - 1) + 1, spans_for(o, phase, left))
        share(r, o, 11 + 3 * (phase - 1) + 2, spans_for(o, phase, right))

    def finish(r, o, phase):
        d = ORDERS[o][phase]
        first = 3 + 4 * (phase - 1)
        across = (spot[d] + 2) % RING
        landed(r, o, first + 2, spans_for(o, phase, across, 0))
        landed(r, o, first + 3, spans_for(o, phase, across, 1))
        share(r, o, 11 + 3 * (phase - 1) + 3, spans_for(o, phase, across))

    for (r, o), copy in zip(every, locals_):
        d = ORDERS[o][0]
        landed(r, o, 1, spans_for(o, 0, (spot[d] + 1) % RING))
        landed(r, o, 2, spans_for(o, 0, (spot[d] + 2) % RING))
        copy.wait()
        spread(r, o, 1)
        share(r, o, 11, spans_for(o, 1, spot[ORDERS[o][1]]))
    for r, o in every:
        relay(r, o, 1)
    for r, o in every:
        finish(r, o, 1)
        spread(r, o, 2)
    for r in range(rounds):
        for o in range(3):
            relay(r, o, 2)
        for o in range(3):
            finish(r, o, 2)
    for r, o in every:
        for phase in (1, 2):
            d = ORDERS[o][phase]
            if phase == 1:
                landed(r, o, 11, spans_for(o, 1, spot[d]), 1 - core)
            base = 11 + 3 * (phase - 1)
            landed(r, o, base + 1, spans_for(o, phase, (spot[d] - 1) % RING), 1 - core)
            landed(r, o, base + 2, spans_for(o, phase, (spot[d] + 1) % RING), 1 - core)
            landed(r, o, base + 3, spans_for(o, phase, (spot[d] + 2) % RING), 1 - core)
    for copy in sent:
        copy.wait_send()


def gather_units(own, collective_id, name, space=pl.ANY):
    rounds, _, rows, _ = own.shape
    return pl.pallas_call(
        functools.partial(gather_kernel, rounds),
        out_shape=jax.ShapeDtypeStruct((rounds, 2, 3, RING, RING, RING, rows, 128), own.dtype),
        in_specs=[pl.BlockSpec(memory_space=pltpu.VMEM)],
        out_specs=pl.BlockSpec(memory_space=space),
        scratch_shapes=[
            pltpu.SemaphoreType.DMA((rounds, 3, 18)),
            pltpu.SemaphoreType.DMA((rounds, 3, 18)),
            pltpu.SemaphoreType.DMA((rounds, 3)),
        ],
        compiler_params=pltpu.CompilerParams(
            collective_id=collective_id,
            has_side_effects=True,
            vmem_limit_bytes=60 * 1024 * 1024,
        ),
        name=name,
    )(own.reshape(rounds, 3, 1, 1, 1, rows, 128))


def reduce_kernel(part_ref, out_ref, d2d, *rest):
    bufs, (send_sem, recv_sem) = rest[:-2], rest[-2:]
    spot, core = where_am_i()
    sent = []
    greet(spot, core)
    every = [(r, o) for r in range(3) for o in range(3)]

    def copy_to(src, dst, r, o, event, there, c):
        copy = pltpu.make_async_remote_copy(
            src_ref=src,
            dst_ref=dst,
            send_sem=send_sem.at[r, o, event],
            recv_sem=recv_sem.at[r, o, event],
            device_id=device_at(there, c),
            device_id_type=MESH,
        )
        copy.start()
        sent.append(copy)

    def landed(dst, r, o, event):
        pltpu.make_async_copy(dst, dst, recv_sem.at[r, o, event]).wait()

    def spans_for(o, phase, at, half=None):
        order = ORDERS[o]
        spans = {}
        for k, d in enumerate(order):
            if k < phase:
                spans[d] = (spot[d], 1)
            elif k == phase:
                spans[d] = (at, 1)
            else:
                spans[d] = (0, RING)
        if half is not None:
            spans[order[phase + 1]] = (2 * half, 2)
        return spans

    def mine(r, o, spans):
        return block_of(part_ref, r, core, o, spans)

    def slot(r, o, phase, which):
        return bufs[(o * 3 + phase) * 2 + which // 2].at[r, which % 2]

    def add_into(into, others):
        sizes = into.shape[:3]
        total = sizes[0] * sizes[1] * sizes[2]

        def one(i, _):
            at = (i // (sizes[1] * sizes[2]), i // sizes[2] % sizes[1], i % sizes[2])
            value = into[at].astype(jnp.float32)
            for other in others:
                value = value + other[at].astype(jnp.float32)
            into[at] = value.astype(jnp.bfloat16)
            return 0

        lax.fori_loop(0, total, one, 0)

    whole = {d: (0, RING) for d in range(3)}

    def first(r, o, phase):
        d = ORDERS[o][phase]
        across = (spot[d] + 2) % RING
        event = 1 + 4 * phase
        if phase < 2:
            for half, by in ((0, 1), (1, -1)):
                copy_to(mine(r, o, spans_for(o, phase, across, half)), slot(r, o, phase, half), r, o, event + half, moved(spot, d, by), core)
        else:
            copy_to(mine(r, o, spans_for(o, phase, across)), slot(r, o, phase, 0), r, o, event, moved(spot, d, 1), core)

    def second(r, o, phase):
        d = ORDERS[o][phase]
        event = 1 + 4 * phase
        for half, by in ((0, 1), (1, -1)):
            at = (spot[d] + by) % RING
            if phase < 2 or half == 0:
                view = slot(r, o, phase, half)
                landed(view, r, o, event + half)
                add_into(mine(r, o, spans_for(o, phase, at, half if phase < 2 else None)), [view])
            copy_to(mine(r, o, spans_for(o, phase, at)), slot(r, o, phase, 2 + half), r, o, event + 2 + half, moved(spot, d, by), core)

    def third(r, o, phase):
        d = ORDERS[o][phase]
        event = 1 + 4 * phase
        a, b = slot(r, o, phase, 2), slot(r, o, phase, 3)
        landed(a, r, o, event + 2)
        landed(b, r, o, event + 3)
        here = mine(r, o, spans_for(o, phase, spot[d]))
        if phase < 2:
            add_into(here, [a, b])
        else:
            total = here[0, 0, 0].astype(jnp.float32) + a[0, 0, 0].astype(jnp.float32)
            out_ref[r, o] = total + b[0, 0, 0].astype(jnp.float32)

    rounds = (2, 1, 0)
    for r in rounds:
        for o in range(3):
            copy_to(block_of(part_ref, r, 1 - core, o, whole), d2d.at[r, o], r, o, 0, spot, 1 - core)
    for r in rounds:
        for o in range(3):
            landed(d2d.at[r, o], r, o, 0)
            add_into(mine(r, o, whole), [d2d.at[r, o]])
            first(r, o, 0)
    for phase in range(3):
        for r in rounds:
            for o in range(3):
                second(r, o, phase)
        for r in rounds:
            for o in range(3):
                third(r, o, phase)
                if phase < 2:
                    first(r, o, phase + 1)
    for copy in sent:
        copy.wait_send()


def reduce_grads(parts):
    bf = jnp.bfloat16
    bufs = []
    for o in range(3):
        for phase in range(3):
            order = ORDERS[o]
            sizes = [RING] * 3
            for k in range(phase + 1):
                sizes[order[k]] = 1
            half = list(sizes)
            if phase < 2:
                half[order[phase + 1]] = 2
            for s in (half, sizes):
                bufs.append(pltpu.VMEM((3, 2, *s, UNIT, 128), bf))
    return pl.pallas_call(
        reduce_kernel,
        out_shape=jax.ShapeDtypeStruct((3, 3, UNIT, 128), jnp.float32),
        in_specs=[pl.BlockSpec(memory_space=pltpu.VMEM)],
        out_specs=pl.BlockSpec(memory_space=pltpu.VMEM),
        scratch_shapes=[
            pltpu.VMEM((3, 3, RING, RING, RING, UNIT, 128), bf),
            *bufs,
            pltpu.SemaphoreType.DMA((3, 3, 13)),
            pltpu.SemaphoreType.DMA((3, 3, 13)),
        ],
        compiler_params=pltpu.CompilerParams(
            collective_id=2, has_side_effects=True, vmem_limit_bytes=62 * 1024 * 1024
        ),
        name="reduce_grads",
    )(parts)


def layer_norm(inputs, gain_row, bias_row):
    centred = inputs - jnp.mean(inputs, axis=-1, keepdims=True)
    inverse = lax.rsqrt(jnp.mean(centred * centred, axis=-1, keepdims=True) + norm_eps)
    return centred * inverse * gain_row + bias_row


def pooling(states, sent_lengths):
    token_mask = (jnp.arange(SEQ)[None, :] < sent_lengths[:, None]).astype(jnp.float32)
    mean_vec = (
        jnp.sum(states * token_mask[:, :, None], axis=1) / sent_lengths.astype(jnp.float32)[:, None]
    )
    return mean_vec * lax.rsqrt(jnp.sum(mean_vec * mean_vec, axis=-1, keepdims=True) + pool_eps)


def gelu_exact(inputs):
    return jax.nn.gelu(inputs, approximate=False)


def contract_rows(first_part, second_part):
    return lax.dot_general(
        first_part, second_part, (((0,), (0,)), ((), ())), preferred_element_type=jnp.float32
    )


def contract_cols(first_part, second_part):
    return lax.dot_general(
        first_part, second_part, (((1,), (1,)), ((), ())), preferred_element_type=jnp.float32
    )


def exact_rows(first_part, second_part):
    return lax.dot_general(
        first_part,
        second_part,
        (((0,), (0,)), ((), ())),
        precision=lax.Precision.HIGHEST,
        preferred_element_type=jnp.float32,
    )


def exact_cols(first_part, second_part):
    return lax.dot_general(
        first_part,
        second_part,
        (((1,), (1,)), ((), ())),
        precision=lax.Precision.HIGHEST,
        preferred_element_type=jnp.float32,
    )


def exact_dot(first_part, second_part):
    return jnp.dot(
        first_part, second_part, precision=lax.Precision.HIGHEST, preferred_element_type=jnp.float32
    )


def split_heads(qkv_low, sent_count, model_width):
    qkv_parts = qkv_low.reshape(sent_count, SEQ, 3, model_width // HEAD_DIM, HEAD_DIM)
    return (qkv_parts[:, :, 0], qkv_parts[:, :, 1], qkv_parts[:, :, 2])


def masked_scores(query, key_part, key_ok):
    scores = (
        jnp.einsum("sqhd,skhd->shqk", query, key_part, preferred_element_type=jnp.float32) * 0.125
    )
    return jnp.where(key_ok[:, None, None, :], scores, far_low)


def layer_forward(hidden, layer_params, key_ok):
    qkv_w, out_w, up_w, down_w, gain_rows, bias_rows = layer_params
    gain_rows = gain_rows.astype(jnp.float32)
    bias_rows = bias_rows.astype(jnp.float32)
    model_width = out_w.shape[1]
    sent_count = key_ok.shape[0]
    hidden_low = hidden.astype(jnp.bfloat16)
    qkv_bias = jnp.concatenate([bias_rows[0], jnp.zeros_like(bias_rows[0]), bias_rows[1]])
    qkv_low = (jnp.dot(hidden_low, qkv_w, preferred_element_type=jnp.float32) + qkv_bias).astype(
        jnp.bfloat16
    )
    query, key_part, value_part = split_heads(qkv_low, sent_count, model_width)
    scores = masked_scores(query, key_part, key_ok)
    score_peak = jnp.max(scores, axis=-1, keepdims=True)
    score_lse = score_peak + jnp.log(jnp.sum(jnp.exp(scores - score_peak), axis=-1, keepdims=True))
    attn_probs = jnp.exp(scores - score_lse)
    context = jnp.einsum(
        "shqk,skhd->sqhd",
        attn_probs.astype(jnp.bfloat16),
        value_part,
        preferred_element_type=jnp.float32,
    )
    context_low = context.reshape(-1, model_width).astype(jnp.bfloat16)
    resid_one = hidden + (
        jnp.dot(context_low, out_w, preferred_element_type=jnp.float32) + bias_rows[2]
    )
    norm_one = layer_norm(resid_one, gain_rows[0], bias_rows[3])
    norm_low = norm_one.astype(jnp.bfloat16)
    pre_act = jnp.dot(norm_low, up_w, preferred_element_type=jnp.float32) + bias_rows[6:].reshape(
        -1
    )
    act_low = gelu_exact(pre_act).astype(jnp.bfloat16)
    resid_two = norm_one + (
        jnp.dot(act_low, down_w, preferred_element_type=jnp.float32) + bias_rows[4]
    )
    output = layer_norm(resid_two, gain_rows[1], bias_rows[5])
    return (
        output,
        (
            hidden_low,
            qkv_low,
            score_lse,
            context_low,
            resid_one,
            norm_low,
            pre_act,
            act_low,
            resid_two,
        ),
    )


def layer_backward(grad_out, layer_params, saved, key_ok):
    qkv_w, out_w, up_w, down_w, gain_rows, bias_rows = layer_params
    gain_rows = gain_rows.astype(jnp.float32)
    bias_rows = bias_rows.astype(jnp.float32)
    (
        hidden_low,
        qkv_low,
        score_lse,
        context_low,
        resid_one,
        norm_low,
        pre_act,
        act_low,
        resid_two,
    ) = saved
    model_width = out_w.shape[1]
    sent_count = key_ok.shape[0]
    second_back = jax.vjp(layer_norm, resid_two, gain_rows[1], bias_rows[5])[1]
    d_resid_two, d_gain_two, d_shift_two = second_back(grad_out)
    d_ffn = d_resid_two.astype(jnp.bfloat16)
    d_down = contract_rows(act_low, d_ffn)
    gelu_back = jax.vjp(gelu_exact, pre_act)[1]
    d_pre = gelu_back(contract_cols(d_ffn, down_w))[0].astype(jnp.bfloat16)
    d_up = contract_rows(norm_low, d_pre)
    d_norm_one = d_resid_two + contract_cols(d_pre, up_w)
    first_back = jax.vjp(layer_norm, resid_one, gain_rows[0], bias_rows[3])[1]
    d_resid_one, d_gain_one, d_shift_one = first_back(d_norm_one)
    d_attn = d_resid_one.astype(jnp.bfloat16)
    d_out = contract_rows(context_low, d_attn)
    d_context = contract_cols(d_attn, out_w).astype(jnp.bfloat16)
    d_context = d_context.reshape(sent_count, SEQ, model_width // HEAD_DIM, HEAD_DIM)
    query, key_part, value_part = split_heads(qkv_low, sent_count, model_width)
    attn_probs = jnp.exp(masked_scores(query, key_part, key_ok) - score_lse)
    d_value = jnp.einsum(
        "shqk,sqhd->skhd",
        attn_probs.astype(jnp.bfloat16),
        d_context,
        preferred_element_type=jnp.float32,
    )
    d_probs = jnp.einsum(
        "sqhd,skhd->shqk", d_context, value_part, preferred_element_type=jnp.float32
    )
    d_scores = attn_probs * (d_probs - jnp.sum(attn_probs * d_probs, axis=-1, keepdims=True))
    d_scores = d_scores.astype(jnp.bfloat16)
    d_query = (
        jnp.einsum("shqk,skhd->sqhd", d_scores, key_part, preferred_element_type=jnp.float32)
        * 0.125
    )
    d_key = (
        jnp.einsum("shqk,sqhd->skhd", d_scores, query, preferred_element_type=jnp.float32) * 0.125
    )
    d_qkv = (
        jnp.stack([d_query, d_key, d_value], axis=2)
        .reshape(-1, 3 * model_width)
        .astype(jnp.bfloat16)
    )
    d_qkv_w = contract_rows(hidden_low, d_qkv)
    d_hidden = d_resid_one + contract_cols(d_qkv, qkv_w)
    column_sums = jnp.sum(d_qkv.astype(jnp.float32), axis=0)
    d_gains = jnp.stack([d_gain_one, d_gain_two])
    vector_rows = jnp.stack(
        [
            column_sums[:model_width],
            column_sums[2 * model_width :],
            jnp.sum(d_attn.astype(jnp.float32), axis=0),
            d_shift_one,
            jnp.sum(d_ffn.astype(jnp.float32), axis=0),
            d_shift_two,
        ]
    )
    up_rows = jnp.sum(d_pre.astype(jnp.float32), axis=0).reshape(4, model_width)
    d_biases = jnp.concatenate([vector_rows, up_rows])
    return (d_hidden, (d_qkv_w, d_out, d_up, d_down, d_gains, d_biases))


def own_units(w_qkv, w_out, w_up, w_down, core):
    first = jnp.concatenate([w_qkv, w_out], axis=1)
    both = jnp.stack([first, w_up]).reshape(2, 6, 2, 3, RING, 128)
    out_going = both.transpose(4, 2, 0, 3, 1, 5).reshape(8, 2, 3, 6, 128)
    rows = lax.all_to_all(out_going, "narrow", split_axis=0, concat_axis=0, tiled=True)
    units = rows.transpose(1, 2, 0, 3, 4).reshape(2, 3, UNIT, 128)
    halves = w_down.reshape(24, 2, 3, 128).transpose(1, 2, 0, 3)
    keep = lax.dynamic_index_in_dim(halves, core, 0, keepdims=False)
    give = lax.dynamic_index_in_dim(halves, 1 - core, 0, keepdims=False)
    got = swapped(give)
    low_rows = jnp.where(core == 0, keep, got)
    high_rows = jnp.where(core == 0, got, keep)
    down = jnp.concatenate([low_rows, high_rows], axis=1)
    return jnp.concatenate([units, down[None]], axis=0)


def swapped(value):
    return lax.ppermute(value, "narrow", [(i, i ^ 1) for i in range(8)])


def whole_weights(gathered):
    first, up = (
        gathered[r].transpose(3, 4, 5, 0, 1, 2, 6).reshape(768, 3072) for r in range(2)
    )
    down = gathered[2].transpose(3, 4, 2, 5, 0, 1, 6).reshape(3072, 768)
    return first[:, :2304], first[:, 2304:], up, down


def as_units(d_qkv, d_out, d_up, d_down):
    first = jnp.concatenate([d_qkv, d_out], axis=1)
    shape = (RING, RING, UNIT, 2, 3, RING, 128)
    parts = [m.reshape(shape).transpose(3, 4, 5, 0, 1, 2, 6) for m in (first, d_up)]
    down = d_down.reshape(RING, RING, RING, UNIT, 2, 3, 128).transpose(4, 5, 2, 0, 1, 3, 6)
    return jnp.stack(parts + [down]).astype(jnp.bfloat16)


def own_rows(reduced, core):
    out_going = reduced[:2].reshape(2, 3, 8, 6, 128).transpose(2, 0, 1, 3, 4)
    rows = lax.all_to_all(out_going, "narrow", split_axis=0, concat_axis=0, tiled=True)
    rows = rows.reshape(RING, 2, 2, 3, 6, 128).transpose(2, 4, 1, 3, 0, 5).reshape(2, 6, 3072)
    halves = reduced[2].reshape(3, 2, 24, 128).transpose(1, 0, 2, 3)
    keep = lax.dynamic_index_in_dim(halves, core, 0, keepdims=False)
    give = lax.dynamic_index_in_dim(halves, 1 - core, 0, keepdims=False)
    got = swapped(give)
    low_cols = jnp.where(core == 0, keep, got)
    high_cols = jnp.where(core == 0, got, keep)
    down = jnp.concatenate([low_cols, high_cols]).transpose(1, 0, 2).reshape(24, 768)
    return rows[0, :, :2304], rows[0, :, 2304:], rows[1], down


def shards(token_ids, lengths, groups, table, w_qkv, w_out, w_up, w_down, gains, biases):
    pair_count = token_ids.shape[0]
    sent_count = 2 * pair_count
    vocab_rows = table.shape[0]
    model_width = table.shape[1]
    flat_ids = token_ids.reshape(-1)
    token_count = flat_ids.shape[0]
    device_total = lax.axis_size(("wide", "narrow"))
    rank_at = lax.axis_index(("wide", "narrow"))
    slot_cap = max(2, 2 * token_count // device_total)
    owner_of = flat_ids // vocab_rows
    local_of = flat_ids - owner_of * vocab_rows
    owner_hits = (owner_of[:, None] == jnp.arange(device_total)[None, :]).astype(jnp.int32)
    rank_in = jnp.sum(jnp.cumsum(owner_hits, axis=0) * owner_hits, axis=1) - 1
    slot_of = owner_of * slot_cap + rank_in
    id_slots = jnp.full((device_total * slot_cap,), -1, jnp.int32).at[slot_of].set(local_of)
    id_slots = id_slots.reshape(device_total, slot_cap)
    asked = lax.all_to_all(id_slots, ("wide", "narrow"), split_axis=0, concat_axis=0, tiled=True)
    valid = asked >= 0
    found = jnp.take(table, jnp.clip(asked, 0, vocab_rows - 1), axis=0)
    found = jnp.where(valid[..., None], found, jnp.zeros((), table.dtype))
    returned = lax.all_to_all(found, ("wide", "narrow"), split_axis=0, concat_axis=0, tiled=True)
    hidden = returned.reshape(-1, model_width)[slot_of].astype(jnp.float32)
    sent_lengths = lengths.reshape(-1)
    key_ok = jnp.arange(SEQ)[None, :] < sent_lengths[:, None]

    core = lax.axis_index("narrow") % 2
    everywhere = ("wide", "narrow")
    all_groups = lax.all_gather(groups, everywhere, axis=0, tiled=True)
    vectors = lax.all_gather(
        jnp.concatenate([gains[0], biases[0]]), everywhere, axis=1, tiled=True
    )
    own = own_units(w_qkv[0], w_out[0], w_up[0], w_down[0], core)
    gathered = gather_units(own, 1, "gather_weights")
    layer_params = whole_weights(gathered) + (vectors[:2], vectors[2:])
    hidden, saved = layer_forward(hidden, layer_params, key_ok)
    states = hidden.reshape(sent_count, SEQ, model_width)
    pooled, pool_back = jax.vjp(lambda inner_states: pooling(inner_states, sent_lengths), states)
    gathered_rows = gather_units(pooled.reshape(1, 3, 16, 128), 3, "gather_pooled")
    pair_rows = gathered_rows[0].transpose(3, 4, 2, 0, 1, 5, 6).reshape(-1, 2, model_width)
    source, target = pair_rows[:, 0], pair_rows[:, 1]
    total_pairs = pair_count * device_total
    pair_weight = 1.0 / (2.0 * total_pairs)
    diagonal = logit_scale * jnp.sum(source * target, axis=1) - logit_scale * margin
    same_pair = jnp.eye(total_pairs, dtype=jnp.float32)
    raw = logit_scale * exact_cols(source, target) - logit_scale * margin * same_pair
    live = all_groups[:, None] == all_groups[None, :]
    masked = jnp.where(live, raw, far_low)
    row_lse = jax.nn.logsumexp(masked, axis=1)
    col_lse = jax.nn.logsumexp(masked, axis=0)
    mix = (
        pair_weight * (jnp.exp(masked - row_lse[:, None]) + jnp.exp(masked - col_lse[None, :]))
        - 2.0 * pair_weight * same_pair
    )
    begin = rank_at * pair_count
    own_mix = lax.dynamic_slice_in_dim(mix, begin, pair_count, 0)
    own_cols = lax.dynamic_slice_in_dim(mix, begin, pair_count, 1)
    source_grad = logit_scale * exact_dot(own_mix, target)
    target_grad = logit_scale * exact_rows(own_cols, source)
    terms = jnp.stack([row_lse - diagonal, col_lse - diagonal], axis=1)
    loss_terms = lax.dynamic_slice_in_dim(terms, begin, pair_count, 0)
    pooled_grad = jnp.stack([source_grad, target_grad], axis=1).reshape(sent_count, model_width)
    d_hidden = pool_back(pooled_grad)[0].reshape(token_count, model_width)
    d_hidden, layer_grads = layer_backward(d_hidden, layer_params, saved, key_ok)
    reduced = reduce_grads(as_units(*layer_grads[:4]))
    d_matrices = own_rows(reduced, core)
    d_vectors = lax.psum(jnp.concatenate(layer_grads[4:]), everywhere)
    d_vectors = lax.dynamic_slice_in_dim(d_vectors, rank_at * 6, 6, 1)
    sent_rows = d_hidden.astype(jnp.bfloat16)
    grad_slots = (
        jnp.zeros((device_total * slot_cap, model_width), jnp.bfloat16).at[slot_of].set(sent_rows)
    )
    grad_slots = grad_slots.reshape(device_total, slot_cap, model_width)
    arrived = lax.all_to_all(
        grad_slots, ("wide", "narrow"), split_axis=0, concat_axis=0, tiled=True
    )
    target_slot = jnp.where(asked >= 0, asked, vocab_rows).reshape(-1)
    table_grads = (
        jnp.zeros((vocab_rows, model_width), jnp.float32)
        .at[target_slot]
        .add(arrived.reshape(-1, model_width).astype(jnp.float32), mode="drop")
    )
    token_grads = d_hidden.reshape(pair_count, 2, SEQ, model_width)
    return (
        loss_terms,
        token_grads,
        table_grads,
        d_matrices[0][None],
        d_matrices[1][None],
        d_matrices[2][None],
        d_matrices[3][None],
        d_vectors[None, :2],
        d_vectors[None, 2:],
    )


def solution(mesh):
    in_specs = (
        P(("wide", "narrow"), None, None),
        P(("wide", "narrow"), None),
        P(("wide", "narrow")),
        P(("wide", "narrow"), None),
        P(None, ("wide", "narrow"), None),
        P(None, ("wide", "narrow"), None),
        P(None, ("wide", "narrow"), None),
        P(None, ("wide", "narrow"), None),
        P(None, None, ("wide", "narrow")),
        P(None, None, ("wide", "narrow")),
    )
    out_specs = (
        P(("wide", "narrow"), None),
        P(("wide", "narrow"), None, None, None),
        P(("wide", "narrow"), None),
        P(None, ("wide", "narrow"), None),
        P(None, ("wide", "narrow"), None),
        P(None, ("wide", "narrow"), None),
        P(None, ("wide", "narrow"), None),
        P(None, None, ("wide", "narrow")),
        P(None, None, ("wide", "narrow")),
    )
    return jax.shard_map(shards, mesh=mesh, in_specs=in_specs, out_specs=out_specs, check_vma=False)
```

```python
import functools

import jax
import jax.numpy as jnp
from jax import lax
from jax.experimental import pallas as pl
from jax.experimental.pallas import tpu as pltpu
from jax.sharding import PartitionSpec as P

HEAD_DIM = 64
SEQ = 64


logit_scale = 10.0
margin = 0.3
norm_eps = 1e-12
pool_eps = 1e-06
far_low = -1e30


MESH = pl.DeviceIdType.MESH
RING = 4
ORDERS = ((0, 1, 2), (1, 2, 0), (2, 0, 1))
UNIT = 48


def where_am_i():
    wide = lax.axis_index("wide")
    narrow = lax.axis_index("narrow")
    return [narrow // 2, wide // RING, wide % RING], narrow % 2


def device_at(spot, core):
    return (spot[1] * RING + spot[2], spot[0] * 2 + core)


def moved(spot, dim, by):
    there = list(spot)
    there[dim] = (spot[dim] + by) % RING
    return there


def block_of(ref, part, core, order, spans):
    return ref.at[(part, core, order) + tuple(pl.ds(*spans[d]) for d in range(3))]


def greet(spot, core):
    barrier = pltpu.get_barrier_semaphore()
    others = [(moved(spot, d, by), core) for d in range(3) for by in (1, -1)] + [(spot, 1 - core)]
    for there, c in others:
        pl.semaphore_signal(barrier, inc=1, device_id=device_at(there, c), device_id_type=MESH)
    pl.semaphore_wait(barrier, len(others))


class Gather:
    def __init__(self, out, send_sem, recv_sem, spot, core, dims):
        self.out, self.send_sem, self.recv_sem = out, send_sem, recv_sem
        self.spot, self.core, self.dims = spot, core, dims
        self.sent = []

    def block(self, r, o, spans, core):
        return self.out.at[(r, core, o) + tuple(pl.ds(*spans[d]) for d in self.dims)]

    def push(self, r, o, event, spans, there, core=None, src=None):
        dst = self.block(r, o, spans, self.core)
        copy = pltpu.make_async_remote_copy(
            src_ref=dst if src is None else src,
            dst_ref=dst,
            send_sem=self.send_sem.at[r, o, event],
            recv_sem=self.recv_sem.at[r, o, event],
            device_id=device_at(there, self.core if core is None else core),
            device_id_type=MESH,
        )
        copy.start()
        self.sent.append(copy)

    def landed(self, r, o, event, spans, core=None):
        dst = self.block(r, o, spans, self.core if core is None else core)
        pltpu.make_async_copy(dst, dst, self.recv_sem.at[r, o, event]).wait()

    def spans(self, o, phase, at, half=None):
        order = ORDERS[o]
        spans = {}
        for k, d in enumerate(order):
            if k < phase:
                spans[d] = (0, RING)
            elif k == phase:
                spans[d] = (at, 1)
            else:
                spans[d] = (self.spot[d], 1)
        if half is not None:
            spans[order[0]] = (2 * half, 2)
        return spans

    def ring(self, o, phase):
        d = ORDERS[o][phase]
        v = self.spot[d]
        up, down = moved(self.spot, d, 1), moved(self.spot, d, -1)
        return v, (v - 1) % RING, (v + 1) % RING, (v + 2) % RING, up, down

    def begin(self, r, o, src):
        v, low, high, far, up, down = self.ring(o, 0)
        here = self.spans(o, 0, v)
        self.push(r, o, 0, here, up, src=src)
        self.push(r, o, 1, here, down, src=src)

    def pass_on(self, r, o):
        v, low, high, far, up, down = self.ring(o, 0)
        self.landed(r, o, 0, self.spans(o, 0, low))
        self.push(r, o, 2, self.spans(o, 0, low), up)

    def first_done(self, r, o):
        v, low, high, far, up, down = self.ring(o, 0)
        self.landed(r, o, 1, self.spans(o, 0, high))
        self.landed(r, o, 2, self.spans(o, 0, far))
        self.share(r, o, 11, self.spans(o, 1, self.spot[ORDERS[o][1]]))

    def share(self, r, o, event, spans):
        self.push(r, o, event, spans, self.spot, 1 - self.core)

    def spread(self, r, o, phase):
        v, low, high, far, up, down = self.ring(o, phase)
        event = 3 + 4 * (phase - 1)
        here = self.spans(o, phase, v)
        self.push(r, o, event, here, up)
        self.push(r, o, event + 1, here, down)

    def relay(self, r, o, phase):
        v, low, high, far, up, down = self.ring(o, phase)
        event, shared = 3 + 4 * (phase - 1), 11 + 3 * (phase - 1)
        self.landed(r, o, event, self.spans(o, phase, low))
        self.push(r, o, event + 2, self.spans(o, phase, low, 0), up)
        self.landed(r, o, event + 1, self.spans(o, phase, high))
        self.push(r, o, event + 3, self.spans(o, phase, high, 1), down)
        self.share(r, o, shared + 1, self.spans(o, phase, low))
        self.share(r, o, shared + 2, self.spans(o, phase, high))

    def finish(self, r, o, phase):
        v, low, high, far, up, down = self.ring(o, phase)
        event, shared = 3 + 4 * (phase - 1), 11 + 3 * (phase - 1)
        self.landed(r, o, event + 2, self.spans(o, phase, far, 0))
        self.landed(r, o, event + 3, self.spans(o, phase, far, 1))
        self.share(r, o, shared + 3, self.spans(o, phase, far))

    def shared_done(self, r, o):
        other = 1 - self.core
        self.landed(r, o, 11, self.spans(o, 1, self.spot[ORDERS[o][1]]), other)
        for phase in (1, 2):
            v, low, high, far, up, down = self.ring(o, phase)
            shared = 11 + 3 * (phase - 1)
            for k, at in enumerate((low, high, far)):
                self.landed(r, o, shared + 1 + k, self.spans(o, phase, at), other)

    def drain(self):
        for copy in self.sent:
            copy.wait_send()


def mm(a, b):
    return jnp.dot(a, b, preferred_element_type=jnp.float32)


def mm_nt(a, b):
    return lax.dot_general(a, b, (((1,), (1,)), ((), ())), preferred_element_type=jnp.float32)


def mm_tn(a, b):
    return lax.dot_general(a, b, (((0,), (0,)), ((), ())), preferred_element_type=jnp.float32)


def head_mask():
    row = lax.broadcasted_iota(jnp.int32, (256, 256), 0) // HEAD_DIM
    col = lax.broadcasted_iota(jnp.int32, (256, 256), 1) // HEAD_DIM
    return row == col


def spread_heads(part, mask):
    four = jnp.concatenate([part] * 4, axis=0)
    return jnp.where(mask, four, jnp.zeros((), four.dtype))


def gather_heads(wide_part, mask):
    kept = jnp.where(mask, wide_part, 0.0)
    return (kept[:64] + kept[64:128]) + (kept[128:192] + kept[192:])


def panel(w, r, n2):
    c, o, x = n2 // 6, n2 // 2 % 3, n2 % 2 * 2
    pair = [w[r, c, o, x + k].reshape(768, 128) for k in range(2)]
    return jnp.concatenate(pair, axis=1)


def down_panel(w, cb, y):
    c, o = cb // 3, cb % 3
    return jnp.concatenate([w[2, c, o, x, y, z] for z in range(RING) for x in range(RING)], axis=0)


def split_low(value):
    high = value.astype(jnp.bfloat16)
    return high, (value - high.astype(jnp.float32)).astype(jnp.bfloat16)


def forward_kernel(
    lens_ref, own_ref, tile_ref, x_ref,
    w_out, vec_out, h1_out, h2_out, inv_out, nl_out, act_out, gp_out, qkv_out, prob_out, ctx_out, dpool_out, loss_out,
    w, vecs, tiles, h1, h2, inv, nl, act, gp, qkv, prob, ctx, resid, pooled, rnorm, pool_own, pool_swap, pool_all,
    left3, right3, stats,
    send_sem, recv_sem, local_sem, pool_send, pool_recv, tile_send, tile_recv, swap_sem, load_sem, save_sem,
):
    spot, core = where_am_i()
    bf, f32 = jnp.bfloat16, jnp.float32
    greet(spot, core)
    g = Gather(w_out, send_sem, recv_sem, spot, core, (0, 1, 2))
    every = [(r, o) for r in range(3) for o in range(3)]
    keep = []
    for r, o in every:
        here = g.spans(o, 0, spot[ORDERS[o][0]])
        copy = pltpu.make_async_copy(own_ref.at[r, o], g.block(r, o, here, core), local_sem.at[r, o])
        copy.start()
        keep.append(copy)
        g.begin(r, o, own_ref.at[r, o])
    tiles[pl.ds(spot[1], 1), pl.ds(spot[2], 1)] = tile_ref[...]
    tile_sent = []

    def tile_push(event, at, there):
        ref = tiles.at[at]
        copy = pltpu.make_async_remote_copy(
            src_ref=ref, dst_ref=ref, send_sem=tile_send.at[event], recv_sem=tile_recv.at[event],
            device_id=device_at(there, core), device_id_type=MESH,
        )
        copy.start()
        tile_sent.append(copy)

    def tile_landed(event, at):
        ref = tiles.at[at]
        pltpu.make_async_copy(ref, ref, tile_recv.at[event]).wait()

    def tile_at(phase, v):
        return (pl.ds(v, 1), pl.ds(spot[2], 1)) if phase == 0 else (pl.ds(0, RING), pl.ds(v, 1))

    def tile_step(phase, step):
        d = phase + 1
        v = spot[d]
        up, down = moved(spot, d, 1), moved(spot, d, -1)
        if step == 0:
            tile_push(3 * phase, tile_at(phase, v), up)
            tile_push(3 * phase + 1, tile_at(phase, v), down)
        elif step == 1:
            tile_landed(3 * phase, tile_at(phase, (v - 1) % RING))
            tile_push(3 * phase + 2, tile_at(phase, (v - 1) % RING), up)
        else:
            tile_landed(3 * phase + 1, tile_at(phase, (v + 1) % RING))
            tile_landed(3 * phase + 2, tile_at(phase, (v + 2) % RING))

    tile_step(0, 0)
    for r, o in every:
        g.pass_on(r, o)
    tile_step(0, 1)
    for (r, o), copy in zip(every, keep):
        copy.wait()
        g.first_done(r, o)
        g.spread(r, o, 1)
    tile_step(0, 2)
    tile_step(1, 0)
    for r, o in every:
        g.relay(r, o, 1)
    tile_step(1, 1)
    for r, o in every:
        g.finish(r, o, 1)
        g.spread(r, o, 2)
    tile_step(1, 2)

    row_at = lax.broadcasted_iota(jnp.int32, (128, 768), 0)
    col_at = lax.broadcasted_iota(jnp.int32, (128, 768), 1)
    all_vec = jnp.zeros((16, 768), f32)
    all_grp = jnp.zeros((16, 512), f32)
    for slab in range(16):
        part = tiles[slab // RING, slab % RING]
        pick = (col_at == row_at + UNIT * slab) & (row_at < UNIT)
        all_vec = all_vec + mm(part, pick.astype(bf))
        pick = (col_at == row_at + 32 * slab) & (row_at < 32)
        all_grp = all_grp + mm(part, pick[:, :512].astype(bf))
    vecs[...] = all_vec
    group_row = all_grp[12:13]
    saves = []

    def save(scratch, out, at):
        copy = pltpu.make_async_copy(scratch, out, save_sem.at[at])
        copy.start()
        saves.append(copy)

    def load(r, o, c):
        return pltpu.make_async_copy(w_out.at[r, c, o], w.at[r, c, o], load_sem.at[r, c, o])

    def arrive(r):
        for o in range(3):
            g.relay(r, o, 2)
        for o in range(3):
            g.finish(r, o, 2)
            load(r, o, core).start()

    def arrived(r):
        for o in range(3):
            g.shared_done(r, o)
            load(r, o, 1 - core).start()
        for o in range(3):
            load(r, o, 0).wait()
            load(r, o, 1).wait()

    save(vecs, vec_out, 0)
    arrive(0)
    arrived(0)
    mask = head_mask()

    def qkv_step(n2, _):
        kind, p = n2 // 3, n2 % 3
        rows = vecs[2:4, :]
        bias = jnp.where(kind == 0, rows[0:1], jnp.where(kind == 2, rows[1:2], 0.0))
        bias = jnp.where(p == 0, bias[:, :256], jnp.where(p == 1, bias[:, 256:512], bias[:, 512:]))
        qkv[n2] = (mm(x_ref[...], panel(w, 0, n2)) + bias).astype(bf)
        return 0

    lax.fori_loop(0, 9, qkv_step, 0)
    save(qkv, qkv_out, 1)
    arrive(1)

    def attend(s, _):
        rows = pl.ds(pl.multiple_of(s * SEQ, SEQ), SEQ)
        slot = lax.broadcasted_iota(jnp.int32, (SEQ, 256), 0)
        live = slot < lens_ref[s]
        for p in range(3):
            query, key_part, value = qkv[p, rows, :], qkv[3 + p, rows, :], qkv[6 + p, rows, :]
            scores = mm_nt(key_part, spread_heads(query, mask)) * 0.125
            scores = jnp.where(live, scores, far_low)
            powers = jnp.exp(scores - jnp.max(scores, axis=0, keepdims=True))
            probs = powers / jnp.sum(powers, axis=0, keepdims=True)
            prob[s, p] = probs
            ctx[p, rows, :] = gather_heads(mm_tn(probs.astype(bf), value), mask).astype(bf)
        return 0

    lax.fori_loop(0, 8, attend, 0)
    save(prob, prob_out, 2)
    save(ctx, ctx_out, 3)
    context = jnp.concatenate([ctx[0], ctx[1], ctx[2]], axis=1)
    for p in range(3):
        resid[:, 256 * p : 256 * p + 256] = mm(context, panel(w, 0, 9 + p))

    def norm_one_step(s, _):
        rows = pl.ds(pl.multiple_of(s * SEQ, SEQ), SEQ)
        value = x_ref[rows, :].astype(f32) + (resid[rows, :] + vecs[4:5, :])
        centred = value - jnp.mean(value, axis=1, keepdims=True)
        inverse = lax.rsqrt(jnp.mean(centred * centred, axis=1, keepdims=True) + norm_eps)
        scaled = centred * inverse
        h1[rows, :] = scaled
        inv[0, rows, :] = jnp.broadcast_to(inverse, (SEQ, 128))
        normed = scaled * vecs[0:1, :] + vecs[5:6, :]
        nl[rows, :] = normed.astype(bf)
        resid[rows, :] = normed + vecs[6:7, :]
        return 0

    lax.fori_loop(0, 8, norm_one_step, 0)
    save(h1, h1_out, 4)
    save(nl, nl_out, 5)
    arrived(1)
    arrive(2)

    def up_step(n2, _):
        weight = panel(w, 1, n2)
        q, p = n2 // 3, n2 % 3
        rows = vecs[8:12, :]
        bias = jnp.where(q == 0, rows[0:1], jnp.where(q == 1, rows[1:2], jnp.where(q == 2, rows[2:3], rows[3:4])))
        bias = jnp.where(p == 0, bias[:, :256], jnp.where(p == 1, bias[:, 256:512], bias[:, 512:]))
        for half in range(4):
            part = pl.ds(128 * half, 128)
            pre = mm(nl[part, :], weight) + bias
            upper = 0.5 + 0.5 * lax.erf(pre * 0.7071067811865476)
            act[n2, part, :] = (pre * upper).astype(bf)
            gp[n2, part, :] = upper + pre * (jnp.exp(-0.5 * pre * pre) * 0.3989422804014327)
        return 0

    lax.fori_loop(0, 12, up_step, 0)
    save(act, act_out, 6)
    save(gp, gp_out, 7)
    arrived(2)

    def down_step(y, _):
        hidden = jnp.concatenate([act[3 * y], act[3 * y + 1], act[3 * y + 2]], axis=1)
        for p in range(3):
            weight = jnp.concatenate([down_panel(w, 2 * p, y), down_panel(w, 2 * p + 1, y)], axis=1)
            cols = slice(256 * p, 256 * p + 256)
            resid[:, cols] = resid[:, cols] + mm(hidden, weight)
        return 0

    lax.fori_loop(0, RING, down_step, 0)

    def norm_two_step(s, _):
        rows = pl.ds(pl.multiple_of(s * SEQ, SEQ), SEQ)
        value = resid[rows, :]
        centred = value - jnp.mean(value, axis=1, keepdims=True)
        inverse = lax.rsqrt(jnp.mean(centred * centred, axis=1, keepdims=True) + norm_eps)
        scaled = centred * inverse
        h2[rows, :] = scaled
        inv[1, rows, :] = jnp.broadcast_to(inverse, (SEQ, 128))
        state = scaled * vecs[1:2, :] + vecs[7:8, :]
        live = lax.broadcasted_iota(jnp.int32, (SEQ, 768), 0) < lens_ref[s]
        mean_vec = jnp.sum(jnp.where(live, state, 0.0), axis=0, keepdims=True) / lens_ref[s].astype(f32)
        r = lax.rsqrt(jnp.sum(mean_vec * mean_vec, axis=1, keepdims=True) + pool_eps)
        pooled[s] = mean_vec * r
        rnorm[s] = jnp.broadcast_to(r, (1, 768))
        return 0

    lax.fori_loop(0, 8, norm_two_step, 0)
    save(h2, h2_out, 8)
    save(inv, inv_out, 9)

    sources = jnp.concatenate([pooled[2 * i] for i in range(4)], axis=0)
    targets = jnp.concatenate([pooled[2 * i + 1] for i in range(4)], axis=0)
    first = core == 0
    pad = jnp.zeros((4, 768), f32)
    pool_own[0] = jnp.concatenate([jnp.where(first, targets, sources), pad], axis=0)
    swap = pltpu.make_async_remote_copy(
        src_ref=pool_own.at[0], dst_ref=pool_swap, send_sem=swap_sem.at[0], recv_sem=swap_sem.at[1],
        device_id=device_at(spot, 1 - core), device_id_type=MESH,
    )
    swap.start()
    swap.wait()
    got = pool_swap[0:4, :]
    kind = jnp.concatenate(
        [jnp.where(first, sources, got), jnp.where(first, got, targets)], axis=0
    )
    q = Gather(pool_all, pool_send, pool_recv, spot, core, (1, 2, 0))
    for o in range(3):
        unit = jnp.concatenate([kind[:, 256 * o : 256 * o + 128], kind[:, 256 * o + 128 : 256 * o + 256]], axis=0)
        here = (pl.ds(spot[1], 1), pl.ds(spot[2], 1), pl.ds(spot[0], 1))
        pool_all[(0, core, o) + here] = unit.reshape(1, 1, 1, 16, 128)
    for o in range(3):
        q.begin(0, o, None)
    for o in range(3):
        q.pass_on(0, o)
    for o in range(3):
        q.first_done(0, o)
        q.spread(0, o, 1)
    for o in range(3):
        q.relay(0, o, 1)
    for o in range(3):
        q.finish(0, o, 1)
        q.spread(0, o, 2)
    for o in range(3):
        q.relay(0, o, 2)
    for o in range(3):
        q.finish(0, o, 2)
    for o in range(3):
        q.shared_done(0, o)

    for k, out in ((0, left3), (1, right3)):
        for o in range(3):
            for h in range(2):
                block = pool_all[0, k, o, :, :, :, 8 * h : 8 * h + 8, :].reshape(512, 128)
                high, low = split_low(block)
                at = 256 * o + 128 * h
                parts = (high, high, low) if k == 0 else (high, low, high)
                for i in range(3):
                    out[:, 768 * i + at : 768 * i + at + 128] = parts[i]
    pair_row = lax.broadcasted_iota(jnp.int32, (512, 256), 0)
    pair_col = lax.broadcasted_iota(jnp.int32, (512, 256), 1)
    names = lax.broadcasted_iota(jnp.int32, (16, 512), 0).astype(f32)
    member = (names == group_row).astype(bf)

    def column_lse(rows3, cols3, into):
        for p in range(2):
            cut = slice(256 * p, 256 * p + 256)
            scores = logit_scale * mm_nt(rows3[...], cols3[cut, :])
            scores = scores - jnp.where(pair_row == pair_col + 256 * p, logit_scale * margin, 0.0)
            alike = mm_tn(member, member[:, cut]) > 0.5
            scores = jnp.where(alike, scores, far_low)
            peak = jnp.max(scores, axis=0, keepdims=True)
            total = jnp.sum(jnp.exp(scores - peak), axis=0, keepdims=True)
            stats[into : into + 1, cut] = peak + jnp.log(total)

    column_lse(left3, right3, 0)
    column_lse(right3, left3, 1)
    chip = (spot[1] * RING + spot[2]) * RING + spot[0]
    mine = pl.ds(pl.multiple_of(chip * 8, 8), 8)
    weight = 1.0 / 1024.0
    at_row = lax.broadcasted_iota(jnp.int32, (8, 512), 0) + chip * 8
    at_col = lax.broadcasted_iota(jnp.int32, (8, 512), 1)
    own_pair = at_row == at_col
    first_rows = (lax.broadcasted_iota(jnp.int32, (16, 8), 0).astype(f32)).astype(bf)
    pick = (lax.broadcasted_iota(jnp.int32, (8, 512), 1) == at_row).astype(bf)
    own_member = mm_nt(pick, member)
    alike = mm(own_member.astype(bf), member) > 0.5
    grads = []
    terms = []
    for k, (rows3, cols3) in enumerate(((left3, right3), (right3, left3))):
        block = pool_all[0, k, :, pl.ds(spot[1], 1), pl.ds(spot[2], 1), pl.ds(spot[0], 1)]
        cut = [block[o, 0, 0, 0, 8 * h : 8 * h + 8, :] for o in range(3) for h in range(2)]
        own8 = jnp.concatenate(cut, axis=1)
        high, low = split_low(own8)
        parts = (high, high, low) if k == 0 else (high, low, high)
        scores = logit_scale * mm_nt(jnp.concatenate(parts, axis=1), cols3[...])
        scores = scores - jnp.where(own_pair, logit_scale * margin, 0.0)
        diagonal = jnp.sum(jnp.where(own_pair, scores, 0.0), axis=1, keepdims=True)
        scores = jnp.where(alike, scores, far_low)
        peak = jnp.max(scores, axis=1, keepdims=True)
        lse = peak + jnp.log(jnp.sum(jnp.exp(scores - peak), axis=1, keepdims=True))
        other = stats[k : k + 1, :]
        mix = weight * (jnp.exp(scores - lse) + jnp.exp(scores - other))
        mix = mix - jnp.where(own_pair, 2.0 * weight, 0.0)
        mix_high, mix_low = split_low(mix)
        high_at, low_at = (0, 768) if k == 0 else (0, 1536)
        high_cols, low_cols = cols3[:, high_at : high_at + 768], cols3[:, low_at : low_at + 768]
        grad = mm(mix_high, high_cols) + mm(mix_high, low_cols) + mm(mix_low, high_cols)
        grads.append(logit_scale * jnp.where(first, grad[0:4], grad[4:8]))
        terms.append(jnp.where(first, (lse - diagonal)[0:4], (lse - diagonal)[4:8]))
    lane = lax.broadcasted_iota(jnp.int32, (4, 128), 1)
    both = jnp.where(lane == 0, terms[0], jnp.where(lane == 1, terms[1], 0.0))
    loss_out[...] = jnp.concatenate([both, jnp.zeros((4, 128), f32)], axis=0)
    for s in range(8):
        d_row = grads[s % 2][s // 2 : s // 2 + 1, :]
        row = pooled[s]
        inner = jnp.sum(row * d_row, axis=1, keepdims=True)
        dpool_out[s] = rnorm[s] * (d_row - row * inner) / lens_ref[s].astype(f32)
    g.drain()
    q.drain()
    for copy in tile_sent:
        copy.wait_send()
    for copy in saves:
        copy.wait()


def forward_pass(lens, own, tile, x):
    bf, f32 = jnp.bfloat16, jnp.float32
    shapes = [
        ((3, 2, 3, RING, RING, RING, UNIT, 128), bf),
        ((16, 768), f32),
        ((512, 768), f32),
        ((512, 768), f32),
        ((2, 512, 128), f32),
        ((512, 768), bf),
        ((12, 512, 256), bf),
        ((12, 512, 256), f32),
        ((9, 512, 256), bf),
        ((8, 3, SEQ, 256), f32),
        ((3, 512, 256), bf),
        ((8, 1, 768), f32),
        ((8, 128), f32),
    ]
    anywhere = pl.BlockSpec(memory_space=pl.ANY)
    vmem = pl.BlockSpec(memory_space=pltpu.VMEM)
    dma = pltpu.SemaphoreType.DMA
    return pl.pallas_call(
        forward_kernel,
        out_shape=[jax.ShapeDtypeStruct(*s) for s in shapes],
        in_specs=[pl.BlockSpec(memory_space=pltpu.SMEM), vmem, vmem, vmem],
        out_specs=[anywhere] * 11 + [vmem] * 2,
        scratch_shapes=[
            pltpu.VMEM(*shapes[0]),
            pltpu.VMEM(*shapes[1]),
            pltpu.VMEM((RING, RING, 16, 128), bf),
            *[pltpu.VMEM(*s) for s in shapes[2:11]],
            pltpu.VMEM((512, 768), f32),
            pltpu.VMEM((8, 1, 768), f32),
            pltpu.VMEM((8, 1, 768), f32),
            pltpu.VMEM((1, 8, 768), f32),
            pltpu.VMEM((8, 768), f32),
            pltpu.VMEM((1, 2, 3, RING, RING, RING, 16, 128), f32),
            pltpu.VMEM((512, 2304), bf),
            pltpu.VMEM((512, 2304), bf),
            pltpu.VMEM((8, 512), f32),
            dma((3, 3, 18)),
            dma((3, 3, 18)),
            dma((3, 3)),
            dma((1, 3, 18)),
            dma((1, 3, 18)),
            dma((6,)),
            dma((6,)),
            dma((2,)),
            dma((3, 2, 3)),
            dma((10,)),
        ],
        compiler_params=pltpu.CompilerParams(
            collective_id=1, has_side_effects=True, vmem_limit_bytes=60 * 1024 * 1024
        ),
        name="forward_pass",
    )(lens, own.reshape(3, 3, 1, 1, 1, UNIT, 128), tile.reshape(1, 1, 16, 128), x)


class Reduce:
    def __init__(self, parts, bufs, out, send_sem, recv_sem, spot, core):
        self.parts, self.bufs, self.out = parts, bufs, out
        self.send_sem, self.recv_sem = send_sem, recv_sem
        self.spot, self.core = spot, core
        self.sent = []

    def copy(self, src, dst, r, o, event, there, core):
        copy = pltpu.make_async_remote_copy(
            src_ref=src,
            dst_ref=dst,
            send_sem=self.send_sem.at[r, o, event],
            recv_sem=self.recv_sem.at[r, o, event],
            device_id=device_at(there, core),
            device_id_type=MESH,
        )
        copy.start()
        self.sent.append(copy)

    def landed(self, dst, r, o, event):
        pltpu.make_async_copy(dst, dst, self.recv_sem.at[r, o, event]).wait()

    def spans(self, o, phase, at, half=None):
        order = ORDERS[o]
        spans = {}
        for k, d in enumerate(order):
            if k < phase:
                spans[d] = (self.spot[d], 1)
            elif k == phase:
                spans[d] = (at, 1)
            else:
                spans[d] = (0, RING)
        if half is not None:
            spans[order[phase + 1]] = (2 * half, 2)
        return spans

    def mine(self, r, o, spans):
        return block_of(self.parts, r, self.core, o, spans)

    def slot(self, r, o, phase, which):
        return self.bufs[(o * 3 + phase) * 2 + which // 2].at[r, which % 2]

    def add_into(self, into, others):
        sizes = into.shape[:3]

        def one(i, _):
            at = (i // sizes[1], i % sizes[1])
            if len(others) == 1:
                into[at] = into[at] + others[0][at]
            else:
                value = into[at].astype(jnp.float32)
                for other in others:
                    value = value + other[at].astype(jnp.float32)
                into[at] = value.astype(jnp.bfloat16)
            return 0

        lax.fori_loop(0, sizes[0] * sizes[1], one, 0)

    def first(self, r, o, phase):
        d = ORDERS[o][phase]
        across = (self.spot[d] + 2) % RING
        event = 1 + 4 * phase
        if phase < 2:
            for half, by in ((0, 1), (1, -1)):
                src = self.mine(r, o, self.spans(o, phase, across, half))
                self.copy(src, self.slot(r, o, phase, half), r, o, event + half, moved(self.spot, d, by), self.core)
        else:
            src = self.mine(r, o, self.spans(o, phase, across))
            self.copy(src, self.slot(r, o, phase, 0), r, o, event, moved(self.spot, d, 1), self.core)

    def second(self, r, o, phase):
        d = ORDERS[o][phase]
        event = 1 + 4 * phase
        for half, by in ((0, 1), (1, -1)):
            at = (self.spot[d] + by) % RING
            if phase < 2 or half == 0:
                view = self.slot(r, o, phase, half)
                self.landed(view, r, o, event + half)
                self.add_into(self.mine(r, o, self.spans(o, phase, at, half if phase < 2 else None)), [view])
            src = self.mine(r, o, self.spans(o, phase, at))
            self.copy(src, self.slot(r, o, phase, 2 + half), r, o, event + 2 + half, moved(self.spot, d, by), self.core)

    def third(self, r, o, phase):
        d = ORDERS[o][phase]
        event = 1 + 4 * phase
        a, b = self.slot(r, o, phase, 2), self.slot(r, o, phase, 3)
        self.landed(a, r, o, event + 2)
        self.landed(b, r, o, event + 3)
        here = self.mine(r, o, self.spans(o, phase, self.spot[d]))
        if phase < 2:
            self.add_into(here, [a, b])
        else:
            total = here[0, 0, 0].astype(jnp.float32) + a[0, 0, 0].astype(jnp.float32)
            self.out[r, o] = total + b[0, 0, 0].astype(jnp.float32)


def reduce_buffers(rounds):
    bufs = []
    for o in range(3):
        for phase in range(3):
            order = ORDERS[o]
            sizes = [RING] * 3
            for k in range(phase + 1):
                sizes[order[k]] = 1
            half = list(sizes)
            if phase < 2:
                half[order[phase + 1]] = 2
            for s in (half, sizes):
                bufs.append(pltpu.VMEM((rounds, 2, *s, UNIT, 128), jnp.bfloat16))
    return bufs


def norm_back(grad, scaled, inverse, gain):
    e = grad * gain
    mean_e = jnp.mean(e, axis=1, keepdims=True)
    mean_eh = jnp.mean(e * scaled, axis=1, keepdims=True)
    return inverse * (e - mean_e - scaled * mean_eh)


def backward_kernel(
    lens_ref, vec_ref, dpool_ref, x_ref,
    w_in, h1_in, h2_in, inv_in, nl_in, act_in, gp_in, qkv_in, prob_in, ctx_in,
    token_out, low_out, red_out, vec_out,
    w, h1, h2, inv, nl, act, gp, qkv, prob, ctx, parts, d2d, d_res, d_low, turned, dvec, vec_slots, *rest,
):
    bufs = rest[:18]
    send_sem, recv_sem, swap_send, swap_recv, free_sem, vec_send, vec_recv, load_sem, gp_sem, w_sem = rest[18:]
    spot, core = where_am_i()
    bf, f32 = jnp.bfloat16, jnp.float32

    def load(src, dst, at):
        copy = pltpu.make_async_copy(src, dst, load_sem.at[at])
        copy.start()
        return copy

    def load_w(r, at):
        copy = pltpu.make_async_copy(w_in.at[r], w.at[at], w_sem.at[r])
        copy.start()
        return copy

    def load_gp(y, at):
        return pltpu.make_async_copy(gp_in.at[pl.ds(3 * y, 3)], gp.at[at], gp_sem.at[at])

    get_h2, get_inv = load(h2_in, h2, 0), load(inv_in, inv, 1)
    get_act = load(act_in, act, 2)
    get_w2 = load_w(2, 0)
    load_gp(0, 0).start()
    load_gp(1, 1).start()
    get_nl = load(nl_in, nl, 3)
    get_w1 = load_w(1, 1)
    get_h1, get_ctx = load(h1_in, h1, 4), load(ctx_in, ctx, 5)
    get_qkv, get_prob = load(qkv_in, qkv, 6), load(prob_in, prob, 7)
    greet(spot, core)
    red = Reduce(parts, bufs, red_out, send_sem, recv_sem, spot, core)
    swaps = {}

    def give(r):
        if r == 0:
            pl.semaphore_wait(free_sem, 1)
        for o in range(3):
            copy = pltpu.make_async_remote_copy(
                src_ref=parts.at[r, 1 - core, o], dst_ref=d2d.at[r % 2, o],
                send_sem=swap_send.at[r, o], recv_sem=swap_recv.at[r, o],
                device_id=device_at(spot, 1 - core), device_id_type=MESH,
            )
            copy.start()
            red.sent.append(copy)

    def take(r):
        for o in range(3):
            view = d2d.at[r % 2, o]
            pltpu.make_async_copy(view, view, swap_recv.at[r, o]).wait()
            red.add_into(parts.at[r, core, o], [view])
            red.first(r, o, 0)
        if r == 2:
            pl.semaphore_signal(free_sem, inc=1, device_id=device_at(spot, 1 - core), device_id_type=MESH)

    def second(r, phase):
        for o in range(3):
            red.second(r, o, phase)

    def third(r, phase):
        for o in range(3):
            red.third(r, o, phase)
            if phase < 2:
                red.first(r, o, phase + 1)

    dvec[0] = jnp.zeros((16, 768), f32)

    def add_vec(row, value):
        dvec[0, row : row + 1, :] = dvec[0, row : row + 1, :] + value

    def total(value):
        return jnp.sum(value, axis=0, keepdims=True)

    get_h2.wait()
    get_inv.wait()

    def norm_two_step(s, _):
        rows = pl.ds(pl.multiple_of(s * SEQ, SEQ), SEQ)
        live = lax.broadcasted_iota(jnp.int32, (SEQ, 768), 0) < lens_ref[s]
        grad = jnp.where(live, jnp.broadcast_to(dpool_ref[s], (SEQ, 768)), 0.0)
        scaled = h2[rows, :]
        inverse = inv[1, rows, 0:1]
        back = norm_back(grad, scaled, inverse, vec_ref[1:2, :])
        low = back.astype(bf)
        d_res[rows, :] = back
        d_low[rows, :] = low
        add_vec(1, total(grad * scaled))
        add_vec(7, total(grad))
        add_vec(6, total(low.astype(f32)))
        return 0

    lax.fori_loop(0, 8, norm_two_step, 0)
    get_act.wait()

    def down_step(y, _):
        hidden = jnp.concatenate([act[3 * y], act[3 * y + 1], act[3 * y + 2]], axis=1)
        turned[...] = hidden.T
        for p in range(3):
            block = mm(turned[...], d_low[:, 256 * p : 256 * p + 256]).astype(bf)
            for k in range(2):
                cb = 2 * p + k
                for z in range(RING):
                    for x in range(RING):
                        at = UNIT * (RING * z + x)
                        parts[2, cb // 3, cb % 3, x, y, z] = block[at : at + UNIT, 128 * k : 128 * k + 128]
        return 0

    lax.fori_loop(0, RING, down_step, 0)
    give(2)
    get_w2.wait()

    def pre_step(y, _):
        at = y % 2
        load_gp(y, at).wait()
        columns = [
            jnp.concatenate([w[0, cb // 3, cb % 3, x, y, z] for z in range(RING) for x in range(RING)], axis=0)
            for cb in range(6)
        ]
        weight = jnp.concatenate(columns, axis=1)
        for j in range(3):
            grad = mm_nt(d_low[...], weight[256 * j : 256 * j + 256, :]) * gp[at, j]
            low = grad.astype(bf)
            act[3 * y + j] = low
            cut = slice(256 * j, 256 * j + 256)
            dvec[0, pl.ds(8 + y, 1), cut] = total(low.astype(f32))

        @pl.when(y < 2)
        def _():
            load_gp(y + 2, at).start()

        return 0

    lax.fori_loop(0, RING, pre_step, 0)
    get_w0 = load_w(0, 0)
    take(2)
    get_nl.wait()
    turned_nl = nl[...].T
    turned[:, :] = turned_nl

    def up_step(n2, _):
        block = mm(turned[...], act[n2]).astype(bf)
        c, o, x = n2 // 6, n2 // 2 % 3, n2 % 2 * 2
        for k in range(2):
            parts[1, c, o, x + k] = block[:, 128 * k : 128 * k + 128].reshape(RING, RING, UNIT, 128)
        return 0

    lax.fori_loop(0, 12, up_step, 0)
    give(1)
    second(2, 0)
    get_w1.wait()

    def six_blocks(at, n):
        blocks = []
        for k in range(6):
            m = n + k
            blocks.append(w[at, m // 12, m // 4 % 3, m % 4].reshape(768, 128))
        return jnp.concatenate(blocks, axis=1)

    def up_back_step(t, _):
        low = jnp.concatenate([act[3 * t], act[3 * t + 1], act[3 * t + 2]], axis=1)
        weight = six_blocks(1, 6 * t)
        for p in range(3):
            cut = slice(256 * p, 256 * p + 256)
            d_res[:, cut] = d_res[:, cut] + mm_nt(low, weight[cut, :])
        return 0

    lax.fori_loop(0, RING, up_back_step, 0)
    take(1)
    third(2, 0)
    get_h1.wait()

    def norm_one_step(s, _):
        rows = pl.ds(pl.multiple_of(s * SEQ, SEQ), SEQ)
        grad, scaled = d_res[rows, :], h1[rows, :]
        back = norm_back(grad, scaled, inv[0, rows, 0:1], vec_ref[0:1, :])
        low = back.astype(bf)
        d_res[rows, :] = back
        d_low[rows, :] = low
        add_vec(0, total(grad * scaled))
        add_vec(5, total(grad))
        add_vec(4, total(low.astype(f32)))
        return 0

    lax.fori_loop(0, 8, norm_one_step, 0)
    second(1, 0)
    get_ctx.wait()
    turned[...] = jnp.concatenate([ctx[0], ctx[1], ctx[2]], axis=1).T
    get_w0.wait()
    weight = six_blocks(0, 18)
    for p in range(3):
        cut = slice(256 * p, 256 * p + 256)
        block = mm(turned[...], d_low[:, cut]).astype(bf)
        for k in range(2):
            n = 18 + 2 * p + k
            parts[0, n // 12, n // 4 % 3, n % 4] = block[:, 128 * k : 128 * k + 128].reshape(RING, RING, UNIT, 128)
        ctx[p] = mm_nt(d_low[...], weight[cut, :]).astype(bf)
    second(2, 1)
    third(1, 0)
    get_qkv.wait()
    get_prob.wait()
    mask = head_mask()

    def attend_back(s, _):
        rows = pl.ds(pl.multiple_of(s * SEQ, SEQ), SEQ)
        for p in range(3):
            query, key_part, value = qkv[p, rows, :], qkv[3 + p, rows, :], qkv[6 + p, rows, :]
            wide_grad = spread_heads(ctx[p, rows, :], mask)
            probs = prob[s, p]
            d_value = mm(probs.astype(bf), wide_grad)
            d_probs = mm_nt(value, wide_grad)
            centre = jnp.sum(probs * d_probs, axis=0, keepdims=True)
            d_scores = (probs * (d_probs - centre)).astype(bf)
            d_query = gather_heads(mm_tn(d_scores, key_part), mask) * 0.125
            d_key = mm(d_scores, spread_heads(query, mask)) * 0.125
            low_query, low_value = d_query.astype(bf), d_value.astype(bf)
            qkv[p, rows, :] = low_query
            qkv[3 + p, rows, :] = d_key.astype(bf)
            qkv[6 + p, rows, :] = low_value
            cut = slice(256 * p, 256 * p + 256)
            dvec[0, 2:3, cut] = dvec[0, 2:3, cut] + total(low_query.astype(f32))
            dvec[0, 3:4, cut] = dvec[0, 3:4, cut] + total(low_value.astype(f32))
        return 0

    lax.fori_loop(0, 8, attend_back, 0)
    vec_sent = []

    def vec_push(event, src, there, c):
        copy = pltpu.make_async_remote_copy(
            src_ref=src, dst_ref=vec_slots.at[event], send_sem=vec_send.at[event], recv_sem=vec_recv.at[event],
            device_id=device_at(there, c), device_id_type=MESH,
        )
        copy.start()
        vec_sent.append(copy)

    def vec_landed(event):
        ref = vec_slots.at[event]
        pltpu.make_async_copy(ref, ref, vec_recv.at[event]).wait()

    def vec_start(d):
        vec_push(1 + 3 * d, dvec.at[d + 1], moved(spot, d, 1), core)
        vec_push(2 + 3 * d, dvec.at[d + 1], moved(spot, d, -1), core)

    def vec_relay(d):
        vec_landed(1 + 3 * d)
        vec_push(3 + 3 * d, vec_slots.at[1 + 3 * d], moved(spot, d, 1), core)

    def vec_add(d):
        vec_landed(2 + 3 * d)
        vec_landed(3 + 3 * d)
        sides = vec_slots[1 + 3 * d] + vec_slots[2 + 3 * d]
        dvec[d + 2] = (dvec[d + 1] + sides) + vec_slots[3 + 3 * d]

    vec_push(0, dvec.at[0], spot, 1 - core)
    turned[...] = x_ref[...].T

    def qkv_step(n2, _):
        block = mm(turned[...], qkv[n2]).astype(bf)
        c, o, x = n2 // 6, n2 // 2 % 3, n2 % 2 * 2
        for k in range(2):
            parts[0, c, o, x + k] = block[:, 128 * k : 128 * k + 128].reshape(RING, RING, UNIT, 128)
        return 0

    lax.fori_loop(0, 9, qkv_step, 0)
    give(0)
    third(2, 1)
    second(1, 1)
    vec_landed(0)
    dvec[1] = dvec[0] + vec_slots[0]
    vec_start(0)

    def input_step(t, _):
        low = jnp.concatenate([qkv[3 * t], qkv[3 * t + 1], qkv[3 * t + 2]], axis=1)
        weight = six_blocks(0, 6 * t)
        for p in range(3):
            cut = slice(256 * p, 256 * p + 256)
            d_res[:, cut] = d_res[:, cut] + mm_nt(low, weight[cut, :])
        return 0

    lax.fori_loop(0, 3, input_step, 0)
    token_copy = pltpu.make_async_copy(d_res, token_out, load_sem.at[8])
    token_copy.start()
    d_low[...] = d_res[...].astype(bf)
    low_copy = pltpu.make_async_copy(d_low, low_out, load_sem.at[9])
    low_copy.start()
    take(0)
    vec_relay(0)
    third(1, 1)
    second(2, 2)
    vec_add(0)
    vec_start(1)
    second(0, 0)
    vec_relay(1)
    second(1, 2)
    third(2, 2)
    third(0, 0)
    vec_add(1)
    vec_start(2)
    second(0, 1)
    vec_relay(2)
    third(1, 2)
    third(0, 1)
    vec_add(2)
    vec_out[...] = dvec[4]
    second(0, 2)
    third(0, 2)
    token_copy.wait()
    low_copy.wait()
    for copy in red.sent + vec_sent:
        copy.wait_send()


def backward_pass(lens, vectors, d_pool, x, w, h1, h2, inv, nl, act, gp, qkv, prob, ctx):
    bf, f32 = jnp.bfloat16, jnp.float32
    anywhere = pl.BlockSpec(memory_space=pl.ANY)
    vmem = pl.BlockSpec(memory_space=pltpu.VMEM)
    dma = pltpu.SemaphoreType.DMA
    scratch = [
        pltpu.VMEM((2, *w.shape[1:]), bf),
        pltpu.VMEM(h1.shape, f32),
        pltpu.VMEM(h2.shape, f32),
        pltpu.VMEM(inv.shape, f32),
        pltpu.VMEM(nl.shape, bf),
        pltpu.VMEM(act.shape, bf),
        pltpu.VMEM((2, 3, 512, 256), f32),
        pltpu.VMEM(qkv.shape, bf),
        pltpu.VMEM(prob.shape, f32),
        pltpu.VMEM(ctx.shape, bf),
        pltpu.VMEM(w.shape, bf),
        pltpu.VMEM((2, *w.shape[2:]), bf),
        pltpu.VMEM((512, 768), f32),
        pltpu.VMEM((512, 768), bf),
        pltpu.VMEM((768, 512), bf),
        pltpu.VMEM((5, 16, 768), f32),
        pltpu.VMEM((10, 16, 768), f32),
        *reduce_buffers(3),
        dma((3, 3, 13)),
        dma((3, 3, 13)),
        dma((3, 3)),
        dma((3, 3)),
        pltpu.SemaphoreType.REGULAR,
        dma((10,)),
        dma((10,)),
        dma((10,)),
        dma((2,)),
        dma((3,)),
    ]
    return pl.pallas_call(
        backward_kernel,
        out_shape=[
            jax.ShapeDtypeStruct((512, 768), f32),
            jax.ShapeDtypeStruct((512, 768), bf),
            jax.ShapeDtypeStruct((3, 3, UNIT, 128), f32),
            jax.ShapeDtypeStruct((16, 768), f32),
        ],
        in_specs=[pl.BlockSpec(memory_space=pltpu.SMEM), vmem, vmem, vmem] + [anywhere] * 10,
        out_specs=[anywhere, anywhere, vmem, vmem],
        scratch_shapes=scratch,
        compiler_params=pltpu.CompilerParams(
            collective_id=2, has_side_effects=True, vmem_limit_bytes=63 * 1024 * 1024
        ),
        name="backward_pass",
    )(lens, vectors, d_pool, x, w, h1, h2, inv, nl, act, gp, qkv, prob, ctx)


def own_units(w_qkv, w_out, w_up, w_down, gains, biases, groups, core):
    first = jnp.concatenate([w_qkv, w_out], axis=1)
    both = jnp.stack([first, w_up]).reshape(2, 6, 2, 3, RING, 128)
    out_going = both.transpose(4, 2, 0, 3, 1, 5).reshape(8, 36, 128)
    extra = jnp.concatenate([gains.reshape(-1), biases.reshape(-1), groups.astype(jnp.bfloat16)])
    extra = jnp.broadcast_to(jnp.pad(extra, (0, 52))[None, None], (8, 1, 128))
    out_going = jnp.concatenate([out_going, extra], axis=1)
    rows = lax.all_to_all(out_going, "narrow", split_axis=0, concat_axis=0, tiled=True)
    units = rows[:, :36].reshape(8, 2, 3, 6, 128).transpose(1, 2, 0, 3, 4).reshape(2, 3, UNIT, 128)
    vectors = rows[:, 36, :72].reshape(8, 12, 6).transpose(1, 0, 2).reshape(12, UNIT)
    named = rows[:, 36, 72:76].reshape(1, 32)
    tile = jnp.concatenate(
        [jnp.pad(vectors, ((0, 0), (0, 80))), jnp.pad(named, ((0, 3), (0, 96)))], axis=0
    )
    halves = w_down.reshape(24, 2, 3, 128).transpose(1, 2, 0, 3)
    keep = lax.dynamic_index_in_dim(halves, core, 0, keepdims=False)
    give = lax.dynamic_index_in_dim(halves, 1 - core, 0, keepdims=False)
    got = swapped(give)
    low_rows = jnp.where(core == 0, keep, got)
    high_rows = jnp.where(core == 0, got, keep)
    down = jnp.concatenate([low_rows, high_rows], axis=1)
    return jnp.concatenate([units, down[None]], axis=0), tile


def swapped(value):
    return lax.ppermute(value, "narrow", [(i, i ^ 1) for i in range(8)])


def own_rows(reduced, core):
    out_going = reduced[:2].reshape(2, 3, 8, 6, 128).transpose(2, 0, 1, 3, 4)
    rows = lax.all_to_all(out_going, "narrow", split_axis=0, concat_axis=0, tiled=True)
    rows = rows.reshape(RING, 2, 2, 3, 6, 128).transpose(2, 4, 1, 3, 0, 5).reshape(2, 6, 3072)
    halves = reduced[2].reshape(3, 2, 24, 128).transpose(1, 0, 2, 3)
    keep = lax.dynamic_index_in_dim(halves, core, 0, keepdims=False)
    give = lax.dynamic_index_in_dim(halves, 1 - core, 0, keepdims=False)
    got = swapped(give)
    low_cols = jnp.where(core == 0, keep, got)
    high_cols = jnp.where(core == 0, got, keep)
    down = jnp.concatenate([low_cols, high_cols]).transpose(1, 0, 2).reshape(24, 768)
    return rows[0, :, :2304], rows[0, :, 2304:], rows[1], down


def shards(token_ids, lengths, groups, table, w_qkv, w_out, w_up, w_down, gains, biases):
    pair_count = token_ids.shape[0]
    vocab_rows = table.shape[0]
    model_width = table.shape[1]
    flat_ids = token_ids.reshape(-1)
    token_count = flat_ids.shape[0]
    device_total = lax.axis_size(("wide", "narrow"))
    rank_at = lax.axis_index(("wide", "narrow"))
    slot_cap = max(2, 2 * token_count // device_total)
    owner_of = flat_ids // vocab_rows
    local_of = flat_ids - owner_of * vocab_rows
    owner_hits = (owner_of[:, None] == jnp.arange(device_total)[None, :]).astype(jnp.int32)
    rank_in = jnp.sum(jnp.cumsum(owner_hits, axis=0) * owner_hits, axis=1) - 1
    slot_of = owner_of * slot_cap + rank_in
    id_slots = jnp.full((device_total * slot_cap,), -1, jnp.int32).at[slot_of].set(local_of)
    id_slots = id_slots.reshape(device_total, slot_cap)
    asked = lax.all_to_all(id_slots, ("wide", "narrow"), split_axis=0, concat_axis=0, tiled=True)
    valid = asked >= 0
    found = jnp.take(table, jnp.clip(asked, 0, vocab_rows - 1), axis=0)
    found = jnp.where(valid[..., None], found, jnp.zeros((), table.dtype))
    returned = lax.all_to_all(found, ("wide", "narrow"), split_axis=0, concat_axis=0, tiled=True)
    sent_lengths = lengths.reshape(-1)

    core = lax.axis_index("narrow") % 2
    own, tile = own_units(w_qkv[0], w_out[0], w_up[0], w_down[0], gains[0], biases[0], groups, core)
    x_low = returned.reshape(-1, model_width)[slot_of]
    kept = forward_pass(sent_lengths, own, tile, x_low)
    gathered, vectors, h1, h2, inv, norm_low, act, gate, qkv, prob, ctx, d_pool, loss_tile = kept
    loss_terms = loss_tile[:4, :2]
    token_grads, sent_rows, reduced, d_vectors = backward_pass(
        sent_lengths, vectors, d_pool, x_low, gathered, h1, h2, inv, norm_low, act, gate, qkv, prob, ctx
    )
    d_matrices = own_rows(reduced, core)
    d_vectors = lax.dynamic_slice_in_dim(d_vectors[:12], rank_at * 6, 6, 1)
    grad_slots = (
        jnp.zeros((device_total * slot_cap, model_width), jnp.bfloat16).at[slot_of].set(sent_rows)
    )
    grad_slots = grad_slots.reshape(device_total, slot_cap, model_width)
    arrived = lax.all_to_all(
        grad_slots, ("wide", "narrow"), split_axis=0, concat_axis=0, tiled=True
    )
    target_slot = jnp.where(asked >= 0, asked, vocab_rows).reshape(-1)
    table_grads = (
        jnp.zeros((vocab_rows, model_width), jnp.float32)
        .at[target_slot]
        .add(arrived.reshape(-1, model_width).astype(jnp.float32), mode="drop")
    )
    token_grads = token_grads.reshape(pair_count, 2, SEQ, model_width)
    return (
        loss_terms,
        token_grads,
        table_grads,
        d_matrices[0][None],
        d_matrices[1][None],
        d_matrices[2][None],
        d_matrices[3][None],
        d_vectors[None, :2],
        d_vectors[None, 2:],
    )


def solution(mesh):
    in_specs = (
        P(("wide", "narrow"), None, None),
        P(("wide", "narrow"), None),
        P(("wide", "narrow")),
        P(("wide", "narrow"), None),
        P(None, ("wide", "narrow"), None),
        P(None, ("wide", "narrow"), None),
        P(None, ("wide", "narrow"), None),
        P(None, ("wide", "narrow"), None),
        P(None, None, ("wide", "narrow")),
        P(None, None, ("wide", "narrow")),
    )
    out_specs = (
        P(("wide", "narrow"), None),
        P(("wide", "narrow"), None, None, None),
        P(("wide", "narrow"), None),
        P(None, ("wide", "narrow"), None),
        P(None, ("wide", "narrow"), None),
        P(None, ("wide", "narrow"), None),
        P(None, ("wide", "narrow"), None),
        P(None, None, ("wide", "narrow")),
        P(None, None, ("wide", "narrow")),
    )
    return jax.shard_map(shards, mesh=mesh, in_specs=in_specs, out_specs=out_specs, check_vma=False)
```

```python
import functools

import jax
import jax.numpy as jnp
from jax import lax
from jax.experimental import pallas as pl
from jax.experimental.pallas import tpu as pltpu
from jax.sharding import PartitionSpec as P

HEAD_DIM = 64
SEQ = 64


logit_scale = 10.0
margin = 0.3
norm_eps = 1e-12
pool_eps = 1e-06
far_low = -1e30


MESH = pl.DeviceIdType.MESH
RING = 4
ORDERS = ((0, 1, 2), (1, 2, 0), (2, 0, 1))
UNIT = 48


def where_am_i():
    wide = lax.axis_index("wide")
    narrow = lax.axis_index("narrow")
    return [narrow // 2, wide // RING, wide % RING], narrow % 2


def device_at(spot, core):
    return (spot[1] * RING + spot[2], spot[0] * 2 + core)


def moved(spot, dim, by):
    there = list(spot)
    there[dim] = (spot[dim] + by) % RING
    return there


def block_of(ref, part, core, order, spans):
    return ref.at[(part, core, order) + tuple(pl.ds(*spans[d]) for d in range(3))]


class Gather:
    def __init__(self, out, send_sem, recv_sem, spot, core, dims):
        self.out, self.send_sem, self.recv_sem = out, send_sem, recv_sem
        self.spot, self.core, self.dims = spot, core, dims
        self.sent = []

    def block(self, r, o, spans, core):
        return self.out.at[(r, core, o) + tuple(pl.ds(*spans[d]) for d in self.dims)]

    def push(self, r, o, event, spans, there, core=None, src=None):
        dst = self.block(r, o, spans, self.core)
        copy = pltpu.make_async_remote_copy(
            src_ref=dst if src is None else src,
            dst_ref=dst,
            send_sem=self.send_sem.at[r, o, event],
            recv_sem=self.recv_sem.at[r, o, event],
            device_id=device_at(there, self.core if core is None else core),
            device_id_type=MESH,
        )
        copy.start()
        self.sent.append(copy)

    def landed(self, r, o, event, spans, core=None):
        dst = self.block(r, o, spans, self.core if core is None else core)
        pltpu.make_async_copy(dst, dst, self.recv_sem.at[r, o, event]).wait()

    def spans(self, o, phase, at, half=None):
        order = ORDERS[o]
        spans = {}
        for k, d in enumerate(order):
            if k < phase:
                spans[d] = (0, RING)
            elif k == phase:
                spans[d] = (at, 1)
            else:
                spans[d] = (self.spot[d], 1)
        if half is not None:
            spans[order[0]] = (2 * half, 2)
        return spans

    def ring(self, o, phase):
        d = ORDERS[o][phase]
        v = self.spot[d]
        up, down = moved(self.spot, d, 1), moved(self.spot, d, -1)
        return v, (v - 1) % RING, (v + 1) % RING, (v + 2) % RING, up, down

    def begin(self, r, o, src):
        v, low, high, far, up, down = self.ring(o, 0)
        here = self.spans(o, 0, v)
        self.push(r, o, 0, here, up, src=src)
        self.push(r, o, 1, here, down, src=src)
        self.push(r, o, 2, here, moved(self.spot, ORDERS[o][0], 2), src=src)

    def first_done(self, r, o):
        v, low, high, far, up, down = self.ring(o, 0)
        self.landed(r, o, 0, self.spans(o, 0, low))
        self.landed(r, o, 1, self.spans(o, 0, high))
        self.landed(r, o, 2, self.spans(o, 0, far))
        self.share(r, o, 11, self.spans(o, 1, self.spot[ORDERS[o][1]]))

    def share(self, r, o, event, spans):
        self.push(r, o, event, spans, self.spot, 1 - self.core)

    def spread(self, r, o, phase, direct=False):
        v, low, high, far, up, down = self.ring(o, phase)
        event = 3 + 4 * (phase - 1)
        here = self.spans(o, phase, v)
        self.push(r, o, event, here, up)
        self.push(r, o, event + 1, here, down)
        if direct:
            self.push(r, o, event + 2, here, moved(self.spot, ORDERS[o][phase], 2))

    def relay(self, r, o, phase, direct=False):
        v, low, high, far, up, down = self.ring(o, phase)
        event, shared = 3 + 4 * (phase - 1), 11 + 3 * (phase - 1)
        self.landed(r, o, event, self.spans(o, phase, low))
        if not direct:
            self.push(r, o, event + 2, self.spans(o, phase, low, 0), up)
        self.landed(r, o, event + 1, self.spans(o, phase, high))
        if not direct:
            self.push(r, o, event + 3, self.spans(o, phase, high, 1), down)
        self.share(r, o, shared + 1, self.spans(o, phase, low))
        self.share(r, o, shared + 2, self.spans(o, phase, high))

    def finish(self, r, o, phase, direct=False):
        v, low, high, far, up, down = self.ring(o, phase)
        event, shared = 3 + 4 * (phase - 1), 11 + 3 * (phase - 1)
        if direct:
            self.landed(r, o, event + 2, self.spans(o, phase, far))
        else:
            self.landed(r, o, event + 2, self.spans(o, phase, far, 0))
            self.landed(r, o, event + 3, self.spans(o, phase, far, 1))
        self.share(r, o, shared + 3, self.spans(o, phase, far))

    def shared_done(self, r, o):
        other = 1 - self.core
        self.landed(r, o, 11, self.spans(o, 1, self.spot[ORDERS[o][1]]), other)
        for phase in (1, 2):
            v, low, high, far, up, down = self.ring(o, phase)
            shared = 11 + 3 * (phase - 1)
            for k, at in enumerate((low, high, far)):
                self.landed(r, o, shared + 1 + k, self.spans(o, phase, at), other)

    def drain(self):
        for copy in self.sent:
            copy.wait_send()


def mm(a, b):
    return jnp.dot(a, b, preferred_element_type=jnp.float32)


def mm_nt(a, b):
    return lax.dot_general(a, b, (((1,), (1,)), ((), ())), preferred_element_type=jnp.float32)


def mm_tn(a, b):
    return lax.dot_general(a, b, (((0,), (0,)), ((), ())), preferred_element_type=jnp.float32)


def head_mask():
    row = lax.broadcasted_iota(jnp.int32, (256, 256), 0) // HEAD_DIM
    col = lax.broadcasted_iota(jnp.int32, (256, 256), 1) // HEAD_DIM
    return row == col


def spread_heads(part, mask):
    four = jnp.concatenate([part] * 4, axis=0)
    return jnp.where(mask, four, jnp.zeros((), four.dtype))


def gather_heads(wide_part, mask):
    kept = jnp.where(mask, wide_part, 0.0)
    return (kept[:64] + kept[64:128]) + (kept[128:192] + kept[192:])


def panel(w, r, n2):
    c, o, x = n2 // 6, n2 // 2 % 3, n2 % 2 * 2
    pair = [w[r, c, o, x + k].reshape(768, 128) for k in range(2)]
    return jnp.concatenate(pair, axis=1)


def down_panel(w, cb, y):
    c, o = cb // 3, cb % 3
    return jnp.concatenate([w[2, c, o, x, y, z] for z in range(RING) for x in range(RING)], axis=0)


def split_low(value):
    high = value.astype(jnp.bfloat16)
    return high, (value - high.astype(jnp.float32)).astype(jnp.bfloat16)


def greet_all():
    barrier = pltpu.get_barrier_semaphore()
    me = lax.axis_index("wide") * 8 + lax.axis_index("narrow")

    def hello(k, _):
        there = (me + k) % 128
        pl.semaphore_signal(barrier, inc=1, device_id=(there // 8, there % 8), device_id_type=MESH)
        return 0

    lax.fori_loop(1, 128, hello, 0)
    return lambda: pl.semaphore_wait(barrier, 127)


def pack_rows(rows):
    n = rows.shape[0] // 8
    left, right = rows[:, :384].reshape(n, 8, 384), rows[:, 384:].reshape(n, 8, 384)
    return jnp.concatenate([left, right], axis=1).astype(jnp.bfloat16)


def unpack_rows(packed):
    wide_rows = packed.astype(jnp.float32)
    rows = jnp.concatenate([wide_rows[:, :8], wide_rows[:, 8:]], axis=2)
    return rows.reshape(-1, 768).astype(jnp.bfloat16)


def digits(value):
    high = jnp.floor(value * 0.015625)
    return high.astype(jnp.bfloat16), (value - 64.0 * high).astype(jnp.bfloat16)


def token_slots(hot_ref, local_ref):
    hot = hot_ref[...]
    row = lax.broadcasted_iota(jnp.int32, (512, 512), 0)
    col = lax.broadcasted_iota(jnp.int32, (512, 512), 1)
    before = mm((col < row).astype(jnp.bfloat16), hot)
    lane = lax.broadcasted_iota(jnp.int32, (512, 128), 1).astype(jnp.float32)
    wide_hot = hot.astype(jnp.float32)
    rank = jnp.sum(before * wide_hot, axis=1, keepdims=True)
    slot = jnp.sum(wide_hot * lane, axis=1, keepdims=True) * 8.0 + rank
    high, low = digits(local_ref[...])
    zero = jnp.zeros((), jnp.bfloat16)
    here = lane == rank
    both = mm_tn(hot, jnp.concatenate([jnp.where(here, high, zero), jnp.where(here, low, zero)], axis=1))
    return slot, both[:, :128] * 64.0 + both[:, 128:]


def slot_hot(slot_ref):
    lane = lax.broadcasted_iota(jnp.int32, (512, 128), 1).astype(jnp.float32)
    parts = [(slot_ref[...] == lane + 128.0 * i).astype(jnp.bfloat16) for i in range(8)]
    return jnp.concatenate(parts, axis=1)


def forward_kernel(
    lens_ref, sent_ref, halves_ref, hot_ref, local_ref, table_in,
    w_out, vec_out, h1_out, h2_out, inv_out, nl_out, act_out, gp_out, qkv_out, prob_out, ctx_out, x_out,
    dpool_out, loss_out, slot_out, asked_out,
    w, vecs, tiles, h1, h2, inv, nl, act, gp, qkv, prob, ctx, x_ref, resid, pooled, rnorm, pool_own, pool_swap, pool_all,
    left3, right3, stats, own, near, half_got, table, ids_out, ids_in, ids, asked, rows_out, rows_in, row_mat,
    send_sem, recv_sem, local_sem, pool_send, pool_recv, tile_send, tile_recv, swap_sem, load_sem, save_sem,
    near_send, near_recv, ids_sem, rows_sem, table_sem,
):
    spot, core = where_am_i()
    me = lax.axis_index("wide") * 8 + lax.axis_index("narrow")
    bf, f32 = jnp.bfloat16, jnp.float32
    all_here = greet_all()
    table_rows = table_in.shape[0]
    get_table = pltpu.make_async_copy(table_in, table.at[pl.ds(0, table_rows)], table_sem.at[0])
    get_table.start()
    table[pl.ds(table_rows, 4096 - table_rows), :] = jnp.zeros((4096 - table_rows, 768), bf)
    slot, wanted = token_slots(hot_ref, local_ref)
    slot_out[...] = jnp.broadcast_to(slot, (512, 128))
    ids[...] = wanted

    def row_out(i, _):
        ids_out[i] = ids[pl.ds(i, 1), :]
        return 0

    lax.fori_loop(0, 128, row_out, 0)
    all_here()

    mine = spot[0] * 2 + core
    sent = []
    for k in range(1, 8):
        there = (mine + k) % 8
        copy = pltpu.make_async_remote_copy(
            src_ref=sent_ref.at[there], dst_ref=near.at[mine], send_sem=near_send.at[k], recv_sem=near_recv.at[k],
            device_id=(lax.axis_index("wide"), there), device_id_type=MESH,
        )
        copy.start()
        sent.append(copy)
    copy = pltpu.make_async_remote_copy(
        src_ref=halves_ref.at[1 - core], dst_ref=half_got, send_sem=near_send.at[0], recv_sem=near_recv.at[0],
        device_id=device_at(spot, 1 - core), device_id_type=MESH,
    )
    copy.start()
    sent.append(copy)

    def ask(k, _):
        there = (me + k) % 128
        pltpu.make_async_remote_copy(
            src_ref=ids_out.at[there], dst_ref=ids_in.at[(128 - k) % 128],
            send_sem=ids_sem.at[0], recv_sem=ids_sem.at[1],
            device_id=(there // 8, there % 8), device_id_type=MESH,
        ).start()
        return 0

    lax.fori_loop(1, 128, ask, 0)
    ids_in[0] = ids_out[me]
    near[mine] = sent_ref[mine]
    for k in range(1, 8):
        ref = near.at[(mine + 8 - k) % 8]
        pltpu.make_async_copy(ref, ref, near_recv.at[k]).wait()
    pltpu.make_async_copy(half_got, half_got, near_recv.at[0]).wait()
    row = lax.broadcasted_iota(jnp.int32, (288, 384), 0)
    col = lax.broadcasted_iota(jnp.int32, (288, 384), 1)
    unit, at = row // UNIT, row % UNIT
    pick = col == at // 6 * UNIT + unit * 6 + at % 6
    units = mm(pick.astype(bf), near[...].reshape(384, 128)).astype(bf)
    for r in range(2):
        for o in range(3):
            first_row = UNIT * (3 * r + o)
            own[r, o] = units[first_row : first_row + UNIT].reshape(1, 1, 1, UNIT, 128)
    kept, got = halves_ref[core].astype(f32), half_got[...].astype(f32)
    for o in range(3):
        a, b = kept[24 * o : 24 * o + 24], got[24 * o : 24 * o + 24]
        upper, lower = jnp.where(core == 0, a, b), jnp.where(core == 0, b, a)
        own[2, o] = jnp.concatenate([upper, lower], axis=0).astype(bf).reshape(1, 1, 1, UNIT, 128)
    small = jnp.zeros((16, 128), f32)
    for j in range(8):
        small = small + near[j, 32:48, :].astype(f32)
    tiles[pl.ds(spot[1], 1), pl.ds(spot[2], 1)] = small.astype(bf).reshape(1, 1, 16, 128)

    g = Gather(w_out, send_sem, recv_sem, spot, core, (0, 1, 2))
    every = [(r, o) for r in range(3) for o in range(3)]
    keep = []
    for r, o in every:
        here = g.spans(o, 0, spot[ORDERS[o][0]])
        copy = pltpu.make_async_copy(own.at[r, o], g.block(r, o, here, core), local_sem.at[r, o])
        copy.start()
        keep.append(copy)
        g.begin(r, o, own.at[r, o])

    def tile_push(event, at, there):
        ref = tiles.at[at]
        copy = pltpu.make_async_remote_copy(
            src_ref=ref, dst_ref=ref, send_sem=tile_send.at[event], recv_sem=tile_recv.at[event],
            device_id=device_at(there, core), device_id_type=MESH,
        )
        copy.start()
        sent.append(copy)

    def tile_at(phase, v):
        return (pl.ds(v, 1), pl.ds(spot[2], 1)) if phase == 0 else (pl.ds(0, RING), pl.ds(v, 1))

    def tile_spread(phase):
        for k, by in enumerate((1, 2, 3)):
            tile_push(3 * phase + k, tile_at(phase, spot[phase + 1]), moved(spot, phase + 1, by))

    def tile_landed(phase):
        for k, by in enumerate((1, 2, 3)):
            ref = tiles.at[tile_at(phase, (spot[phase + 1] + RING - by) % RING)]
            pltpu.make_async_copy(ref, ref, tile_recv.at[3 * phase + k]).wait()

    tile_spread(0)
    for (r, o), copy in zip(every, keep):
        copy.wait()
        g.first_done(r, o)
        g.spread(r, o, 1, r == 0)
    tile_landed(0)
    tile_spread(1)

    others = ids_in.at[pl.ds(0, 127)]
    pltpu.make_async_copy(others, others, ids_sem.at[1]).wait()

    def row_in(i, _):
        ids[pl.ds(i, 1), :] = ids_in[i]
        return 0

    lax.fori_loop(0, 128, row_in, 0)
    high, low = digits(ids[...])
    row = lax.broadcasted_iota(jnp.int32, (1024, 128), 0)
    col = lax.broadcasted_iota(jnp.int32, (1024, 128), 1)
    member_of = (row // 8 == col).astype(bf)
    both = mm(member_of, high) * 64.0 + mm(member_of, low)
    asked_col = jnp.sum(jnp.where(col == row % 8, both, 0.0), axis=1, keepdims=True) - 1.0
    asked[...] = jnp.broadcast_to(asked_col, (1024, 128))
    row = lax.broadcasted_iota(jnp.int32, (128, 1024), 0)
    col = lax.broadcasted_iota(jnp.int32, (128, 1024), 1)
    member_of = (col // 8 == row).astype(bf)
    both = mm_tn(high, member_of) * 64.0 + mm_tn(low, member_of)
    asked_row = jnp.sum(jnp.where(row == col % 8, both, 0.0), axis=0, keepdims=True) - 1.0
    asked_out[...] = jnp.broadcast_to(asked_row, (8, 1024))
    get_table.wait()

    def find(half):
        col = asked[512 * half : 512 * half + 512, :]
        lane = lax.broadcasted_iota(jnp.int32, (512, 128), 1).astype(f32)

        def chunk(i, _):
            first_row = i * 512
            base = lane + (first_row * 1).astype(f32)
            hot = jnp.concatenate([(col == base + 128.0 * j).astype(bf) for j in range(4)], axis=1)
            part = mm(hot, table[pl.ds(pl.multiple_of(first_row, 512), 512), :])
            resid[...] = jnp.where(i == 0, part, resid[...] + part)
            return 0

        lax.fori_loop(0, 8, chunk, 0)
        for q in range(4):
            rows_out[64 * half + 16 * q : 64 * half + 16 * q + 16] = pack_rows(resid[128 * q : 128 * q + 128, :])

        def answer(k, _):
            there = (me + k) % 128
            pltpu.make_async_remote_copy(
                src_ref=rows_out.at[k], dst_ref=rows_in.at[me], send_sem=rows_sem.at[0], recv_sem=rows_sem.at[1],
                device_id=(there // 8, there % 8), device_id_type=MESH,
            ).start()
            return 0

        lax.fori_loop(max(1, 64 * half), 64 * half + 64, answer, 0)

    find(0)
    rows_in[me] = rows_out[0]
    for o in range(3):
        g.relay(0, o, 1, True)
    for o in range(3):
        g.finish(0, o, 1, True)
        g.spread(0, o, 2)
    for r in (1, 2):
        for o in range(3):
            g.relay(r, o, 1)
    find(1)
    for r in (1, 2):
        for o in range(3):
            g.finish(r, o, 1)
            g.spread(r, o, 2)
    tile_landed(1)

    row_at = lax.broadcasted_iota(jnp.int32, (128, 768), 0)
    col_at = lax.broadcasted_iota(jnp.int32, (128, 768), 1)
    all_vec = jnp.zeros((16, 768), f32)
    all_grp = jnp.zeros((16, 512), f32)
    for slab in range(16):
        part = tiles[slab // RING, slab % RING]
        pick = (col_at == row_at + UNIT * slab) & (row_at < UNIT)
        all_vec = all_vec + mm(part, pick.astype(bf))
        pick = (col_at == row_at - 64 + 32 * slab) & (row_at >= 64) & (row_at < 96)
        all_grp = all_grp + mm(part, pick[:, :512].astype(bf))
    vecs[...] = jnp.concatenate([all_vec[4:16], all_vec[0:4]], axis=0)
    group_row = all_grp[4:5]
    saves = []

    def save(scratch, out, at):
        copy = pltpu.make_async_copy(scratch, out, save_sem.at[at])
        copy.start()
        saves.append(copy)

    def load(r, o, c):
        return pltpu.make_async_copy(w_out.at[r, c, o], w.at[r, c, o], load_sem.at[r, c, o])

    def arrive(r):
        for o in range(3):
            g.relay(r, o, 2)
        for o in range(3):
            g.finish(r, o, 2)
            load(r, o, core).start()

    def arrived(r):
        for o in range(3):
            g.shared_done(r, o)
            load(r, o, 1 - core).start()
        for o in range(3):
            load(r, o, 0).wait()
            load(r, o, 1).wait()

    save(vecs, vec_out, 0)
    arrive(0)
    others = rows_in.at[pl.ds(0, 127)]
    pltpu.make_async_copy(others, others, rows_sem.at[1]).wait()
    for q in range(8):
        row_mat[128 * q : 128 * q + 128, :] = unpack_rows(rows_in[16 * q : 16 * q + 16])
    slots_hot = slot_hot(slot_out)
    for p in range(3):
        cut = slice(256 * p, 256 * p + 256)
        x_ref[:, cut] = mm(slots_hot, row_mat[:, cut]).astype(bf)
    save(x_ref, x_out, 10)
    arrived(0)
    mask = head_mask()

    def qkv_step(n2, _):
        kind, p = n2 // 3, n2 % 3
        rows = vecs[2:4, :]
        bias = jnp.where(kind == 0, rows[0:1], jnp.where(kind == 2, rows[1:2], 0.0))
        bias = jnp.where(p == 0, bias[:, :256], jnp.where(p == 1, bias[:, 256:512], bias[:, 512:]))
        qkv[n2] = (mm(x_ref[...], panel(w, 0, n2)) + bias).astype(bf)
        return 0

    lax.fori_loop(0, 9, qkv_step, 0)
    save(qkv, qkv_out, 1)
    arrive(1)

    def attend(s, _):
        rows = pl.ds(pl.multiple_of(s * SEQ, SEQ), SEQ)
        slot = lax.broadcasted_iota(jnp.int32, (SEQ, 256), 0)
        live = slot < lens_ref[s]
        for p in range(3):
            query, key_part, value = qkv[p, rows, :], qkv[3 + p, rows, :], qkv[6 + p, rows, :]
            scores = mm_nt(key_part, spread_heads(query, mask)) * 0.125
            scores = jnp.where(live, scores, far_low)
            powers = jnp.exp(scores - jnp.max(scores, axis=0, keepdims=True))
            probs = powers / jnp.sum(powers, axis=0, keepdims=True)
            prob[s, p] = probs
            ctx[p, rows, :] = gather_heads(mm_tn(probs.astype(bf), value), mask).astype(bf)
        return 0

    lax.fori_loop(0, 8, attend, 0)
    save(prob, prob_out, 2)
    save(ctx, ctx_out, 3)
    context = jnp.concatenate([ctx[0], ctx[1], ctx[2]], axis=1)
    for p in range(3):
        resid[:, 256 * p : 256 * p + 256] = mm(context, panel(w, 0, 9 + p))

    def norm_one_step(s, _):
        rows = pl.ds(pl.multiple_of(s * SEQ, SEQ), SEQ)
        value = x_ref[rows, :].astype(f32) + (resid[rows, :] + vecs[4:5, :])
        centred = value - jnp.mean(value, axis=1, keepdims=True)
        inverse = lax.rsqrt(jnp.mean(centred * centred, axis=1, keepdims=True) + norm_eps)
        scaled = centred * inverse
        h1[rows, :] = scaled
        inv[0, rows, :] = jnp.broadcast_to(inverse, (SEQ, 128))
        normed = scaled * vecs[0:1, :] + vecs[5:6, :]
        nl[rows, :] = normed.astype(bf)
        resid[rows, :] = normed + vecs[6:7, :]
        return 0

    lax.fori_loop(0, 8, norm_one_step, 0)
    save(h1, h1_out, 4)
    save(nl, nl_out, 5)
    arrived(1)
    arrive(2)

    def up_step(n2, _):
        weight = panel(w, 1, n2)
        q, p = n2 // 3, n2 % 3
        rows = vecs[8:12, :]
        bias = jnp.where(q == 0, rows[0:1], jnp.where(q == 1, rows[1:2], jnp.where(q == 2, rows[2:3], rows[3:4])))
        bias = jnp.where(p == 0, bias[:, :256], jnp.where(p == 1, bias[:, 256:512], bias[:, 512:]))
        for half in range(4):
            part = pl.ds(128 * half, 128)
            pre = mm(nl[part, :], weight) + bias
            upper = 0.5 + 0.5 * lax.erf(pre * 0.7071067811865476)
            act[n2, part, :] = (pre * upper).astype(bf)
            gp[n2, part, :] = upper + pre * (jnp.exp(-0.5 * pre * pre) * 0.3989422804014327)
        return 0

    lax.fori_loop(0, 12, up_step, 0)
    save(act, act_out, 6)
    save(gp, gp_out, 7)
    arrived(2)

    def down_step(y, _):
        hidden = jnp.concatenate([act[3 * y], act[3 * y + 1], act[3 * y + 2]], axis=1)
        for p in range(3):
            weight = jnp.concatenate([down_panel(w, 2 * p, y), down_panel(w, 2 * p + 1, y)], axis=1)
            cols = slice(256 * p, 256 * p + 256)
            resid[:, cols] = resid[:, cols] + mm(hidden, weight)
        return 0

    lax.fori_loop(0, RING, down_step, 0)

    def norm_two_step(s, _):
        rows = pl.ds(pl.multiple_of(s * SEQ, SEQ), SEQ)
        value = resid[rows, :]
        centred = value - jnp.mean(value, axis=1, keepdims=True)
        inverse = lax.rsqrt(jnp.mean(centred * centred, axis=1, keepdims=True) + norm_eps)
        scaled = centred * inverse
        h2[rows, :] = scaled
        inv[1, rows, :] = jnp.broadcast_to(inverse, (SEQ, 128))
        state = scaled * vecs[1:2, :] + vecs[7:8, :]
        live = lax.broadcasted_iota(jnp.int32, (SEQ, 768), 0) < lens_ref[s]
        mean_vec = jnp.sum(jnp.where(live, state, 0.0), axis=0, keepdims=True) / lens_ref[s].astype(f32)
        r = lax.rsqrt(jnp.sum(mean_vec * mean_vec, axis=1, keepdims=True) + pool_eps)
        pooled[s] = mean_vec * r
        rnorm[s] = jnp.broadcast_to(r, (1, 768))
        return 0

    lax.fori_loop(0, 8, norm_two_step, 0)
    save(h2, h2_out, 8)
    save(inv, inv_out, 9)

    sources = jnp.concatenate([pooled[2 * i] for i in range(4)], axis=0)
    targets = jnp.concatenate([pooled[2 * i + 1] for i in range(4)], axis=0)
    first = core == 0
    pad = jnp.zeros((4, 768), f32)
    pool_own[0] = jnp.concatenate([jnp.where(first, targets, sources), pad], axis=0)
    swap = pltpu.make_async_remote_copy(
        src_ref=pool_own.at[0], dst_ref=pool_swap, send_sem=swap_sem.at[0], recv_sem=swap_sem.at[1],
        device_id=device_at(spot, 1 - core), device_id_type=MESH,
    )
    swap.start()
    swap.wait()
    got = pool_swap[0:4, :]
    kind = jnp.concatenate(
        [jnp.where(first, sources, got), jnp.where(first, got, targets)], axis=0
    )
    q = Gather(pool_all, pool_send, pool_recv, spot, core, (1, 2, 0))
    for o in range(3):
        unit = jnp.concatenate([kind[:, 256 * o : 256 * o + 128], kind[:, 256 * o + 128 : 256 * o + 256]], axis=0)
        here = (pl.ds(spot[1], 1), pl.ds(spot[2], 1), pl.ds(spot[0], 1))
        pool_all[(0, core, o) + here] = unit.reshape(1, 1, 1, 16, 128)
    for o in range(3):
        q.begin(0, o, None)
    for o in range(3):
        q.first_done(0, o)
        q.spread(0, o, 1, True)
    for o in range(3):
        q.relay(0, o, 1, True)
    for o in range(3):
        q.finish(0, o, 1, True)
        q.spread(0, o, 2)
    for o in range(3):
        q.relay(0, o, 2)
    for o in range(3):
        q.finish(0, o, 2)
    for o in range(3):
        q.shared_done(0, o)

    for k, out in ((0, left3), (1, right3)):
        for o in range(3):
            for h in range(2):
                block = pool_all[0, k, o, :, :, :, 8 * h : 8 * h + 8, :].reshape(512, 128)
                high, low = split_low(block)
                at = 256 * o + 128 * h
                parts = (high, high, low) if k == 0 else (high, low, high)
                for i in range(3):
                    out[:, 768 * i + at : 768 * i + at + 128] = parts[i]
    pair_row = lax.broadcasted_iota(jnp.int32, (512, 256), 0)
    pair_col = lax.broadcasted_iota(jnp.int32, (512, 256), 1)
    names = lax.broadcasted_iota(jnp.int32, (16, 512), 0).astype(f32)
    member = (names == group_row).astype(bf)

    def column_lse(rows3, cols3, into):
        for p in range(2):
            cut = slice(256 * p, 256 * p + 256)
            scores = logit_scale * mm_nt(rows3[...], cols3[cut, :])
            scores = scores - jnp.where(pair_row == pair_col + 256 * p, logit_scale * margin, 0.0)
            alike = mm_tn(member, member[:, cut]) > 0.5
            scores = jnp.where(alike, scores, far_low)
            peak = jnp.max(scores, axis=0, keepdims=True)
            total = jnp.sum(jnp.exp(scores - peak), axis=0, keepdims=True)
            stats[into : into + 1, cut] = peak + jnp.log(total)

    column_lse(left3, right3, 0)
    column_lse(right3, left3, 1)
    chip = (spot[1] * RING + spot[2]) * RING + spot[0]
    mine = pl.ds(pl.multiple_of(chip * 8, 8), 8)
    weight = 1.0 / 1024.0
    at_row = lax.broadcasted_iota(jnp.int32, (8, 512), 0) + chip * 8
    at_col = lax.broadcasted_iota(jnp.int32, (8, 512), 1)
    own_pair = at_row == at_col
    pick = (lax.broadcasted_iota(jnp.int32, (8, 512), 1) == at_row).astype(bf)
    own_member = mm_nt(pick, member)
    alike = mm(own_member.astype(bf), member) > 0.5
    grads = []
    terms = []
    for k, (rows3, cols3) in enumerate(((left3, right3), (right3, left3))):
        block = pool_all[0, k, :, pl.ds(spot[1], 1), pl.ds(spot[2], 1), pl.ds(spot[0], 1)]
        cut = [block[o, 0, 0, 0, 8 * h : 8 * h + 8, :] for o in range(3) for h in range(2)]
        own8 = jnp.concatenate(cut, axis=1)
        high, low = split_low(own8)
        parts = (high, high, low) if k == 0 else (high, low, high)
        scores = logit_scale * mm_nt(jnp.concatenate(parts, axis=1), cols3[...])
        scores = scores - jnp.where(own_pair, logit_scale * margin, 0.0)
        diagonal = jnp.sum(jnp.where(own_pair, scores, 0.0), axis=1, keepdims=True)
        scores = jnp.where(alike, scores, far_low)
        peak = jnp.max(scores, axis=1, keepdims=True)
        lse = peak + jnp.log(jnp.sum(jnp.exp(scores - peak), axis=1, keepdims=True))
        other = stats[k : k + 1, :]
        mix = weight * (jnp.exp(scores - lse) + jnp.exp(scores - other))
        mix = mix - jnp.where(own_pair, 2.0 * weight, 0.0)
        mix_high, mix_low = split_low(mix)
        high_at, low_at = (0, 768) if k == 0 else (0, 1536)
        high_cols, low_cols = cols3[:, high_at : high_at + 768], cols3[:, low_at : low_at + 768]
        grad = mm(mix_high, high_cols) + mm(mix_high, low_cols) + mm(mix_low, high_cols)
        grads.append(logit_scale * jnp.where(first, grad[0:4], grad[4:8]))
        terms.append(jnp.where(first, (lse - diagonal)[0:4], (lse - diagonal)[4:8]))
    lane = lax.broadcasted_iota(jnp.int32, (4, 128), 1)
    both = jnp.where(lane == 0, terms[0], jnp.where(lane == 1, terms[1], 0.0))
    loss_out[...] = jnp.concatenate([both, jnp.zeros((4, 128), f32)], axis=0)
    for s in range(8):
        d_row = grads[s % 2][s // 2 : s // 2 + 1, :]
        row = pooled[s]
        inner = jnp.sum(row * d_row, axis=1, keepdims=True)
        dpool_out[s] = rnorm[s] * (d_row - row * inner) / lens_ref[s].astype(f32)
    g.drain()
    q.drain()
    for copy in sent:
        copy.wait_send()
    for sem, ref in ((ids_sem, ids_in), (rows_sem, rows_in)):
        others = ref.at[pl.ds(0, 127)]
        pltpu.make_async_copy(others, others, sem.at[0]).wait()
    for copy in saves:
        copy.wait()


def forward_pass(lens, sent, halves, hot, local, table):
    bf, f32 = jnp.bfloat16, jnp.float32
    shapes = [
        ((3, 2, 3, RING, RING, RING, UNIT, 128), bf),
        ((16, 768), f32),
        ((512, 768), f32),
        ((512, 768), f32),
        ((2, 512, 128), f32),
        ((512, 768), bf),
        ((12, 512, 256), bf),
        ((12, 512, 256), f32),
        ((9, 512, 256), bf),
        ((8, 3, SEQ, 256), f32),
        ((3, 512, 256), bf),
        ((512, 768), bf),
        ((8, 1, 768), f32),
        ((8, 128), f32),
        ((512, 128), f32),
        ((8, 1024), f32),
    ]
    anywhere = pl.BlockSpec(memory_space=pl.ANY)
    vmem = pl.BlockSpec(memory_space=pltpu.VMEM)
    dma = pltpu.SemaphoreType.DMA
    return pl.pallas_call(
        forward_kernel,
        out_shape=[jax.ShapeDtypeStruct(*s) for s in shapes],
        in_specs=[pl.BlockSpec(memory_space=pltpu.SMEM), vmem, vmem, vmem, vmem, anywhere],
        out_specs=[anywhere] * 12 + [vmem] * 4,
        scratch_shapes=[
            pltpu.VMEM(*shapes[0]),
            pltpu.VMEM(*shapes[1]),
            pltpu.VMEM((RING, RING, 16, 128), bf),
            *[pltpu.VMEM(*s) for s in shapes[2:12]],
            pltpu.VMEM((512, 768), f32),
            pltpu.VMEM((8, 1, 768), f32),
            pltpu.VMEM((8, 1, 768), f32),
            pltpu.VMEM((1, 8, 768), f32),
            pltpu.VMEM((8, 768), f32),
            pltpu.VMEM((1, 2, 3, RING, RING, RING, 16, 128), f32),
            pltpu.VMEM((512, 2304), bf),
            pltpu.VMEM((512, 2304), bf),
            pltpu.VMEM((8, 512), f32),
            pltpu.VMEM((3, 3, 1, 1, 1, UNIT, 128), bf),
            pltpu.VMEM((8, UNIT, 128), bf),
            pltpu.VMEM((80, 128), bf),
            pltpu.VMEM((4096, 768), bf),
            pltpu.VMEM((128, 1, 128), f32),
            pltpu.VMEM((128, 1, 128), f32),
            pltpu.VMEM((128, 128), f32),
            pltpu.VMEM((1024, 128), f32),
            pltpu.VMEM((128, 16, 384), bf),
            pltpu.VMEM((128, 16, 384), bf),
            pltpu.VMEM((1024, 768), bf),
            dma((3, 3, 18)),
            dma((3, 3, 18)),
            dma((3, 3)),
            dma((1, 3, 18)),
            dma((1, 3, 18)),
            dma((6,)),
            dma((6,)),
            dma((2,)),
            dma((3, 2, 3)),
            dma((11,)),
            dma((8,)),
            dma((8,)),
            dma((2,)),
            dma((2,)),
            dma((1,)),
        ],
        compiler_params=pltpu.CompilerParams(
            collective_id=1, has_side_effects=True, vmem_limit_bytes=62 * 1024 * 1024
        ),
        name="forward_pass",
    )(lens, sent, halves, hot, local, table)


class Reduce:
    def __init__(self, parts, bufs, out, send_sem, recv_sem, spot, core):
        self.parts, self.bufs, self.out = parts, bufs, out
        self.send_sem, self.recv_sem = send_sem, recv_sem
        self.spot, self.core = spot, core
        self.sent = []

    def copy(self, src, dst, r, o, event, there, core):
        copy = pltpu.make_async_remote_copy(
            src_ref=src,
            dst_ref=dst,
            send_sem=self.send_sem.at[r, o, event],
            recv_sem=self.recv_sem.at[r, o, event],
            device_id=device_at(there, core),
            device_id_type=MESH,
        )
        copy.start()
        self.sent.append(copy)

    def landed(self, dst, r, o, event):
        pltpu.make_async_copy(dst, dst, self.recv_sem.at[r, o, event]).wait()

    def spans(self, o, phase, at, half=None):
        order = ORDERS[o]
        spans = {}
        for k, d in enumerate(order):
            if k < phase:
                spans[d] = (self.spot[d], 1)
            elif k == phase:
                spans[d] = (at, 1)
            else:
                spans[d] = (0, RING)
        if half is not None:
            spans[order[phase + 1]] = (2 * half, 2)
        return spans

    def mine(self, r, o, spans):
        return block_of(self.parts, r, self.core, o, spans)

    def slot(self, r, o, phase, which):
        return self.bufs[(o * 3 + phase) * 2 + which // 2].at[r, which % 2]

    def add_into(self, into, others):
        sizes = into.shape[:3]

        def one(i, _):
            at = (i // sizes[1], i % sizes[1])
            if len(others) == 1:
                into[at] = into[at] + others[0][at]
            else:
                value = into[at].astype(jnp.float32)
                for other in others:
                    value = value + other[at].astype(jnp.float32)
                into[at] = value.astype(jnp.bfloat16)
            return 0

        lax.fori_loop(0, sizes[0] * sizes[1], one, 0)

    def first(self, r, o, phase):
        d = ORDERS[o][phase]
        across = (self.spot[d] + 2) % RING
        event = 1 + 4 * phase
        if phase < 2:
            for half, by in ((0, 1), (1, -1)):
                src = self.mine(r, o, self.spans(o, phase, across, half))
                self.copy(src, self.slot(r, o, phase, half), r, o, event + half, moved(self.spot, d, by), self.core)
        else:
            src = self.mine(r, o, self.spans(o, phase, across))
            self.copy(src, self.slot(r, o, phase, 0), r, o, event, moved(self.spot, d, 1), self.core)

    def second(self, r, o, phase):
        d = ORDERS[o][phase]
        event = 1 + 4 * phase
        for half, by in ((0, 1), (1, -1)):
            at = (self.spot[d] + by) % RING
            if phase < 2 or half == 0:
                view = self.slot(r, o, phase, half)
                self.landed(view, r, o, event + half)
                self.add_into(self.mine(r, o, self.spans(o, phase, at, half if phase < 2 else None)), [view])
            src = self.mine(r, o, self.spans(o, phase, at))
            self.copy(src, self.slot(r, o, phase, 2 + half), r, o, event + 2 + half, moved(self.spot, d, by), self.core)

    def third(self, r, o, phase):
        d = ORDERS[o][phase]
        event = 1 + 4 * phase
        a, b = self.slot(r, o, phase, 2), self.slot(r, o, phase, 3)
        self.landed(a, r, o, event + 2)
        self.landed(b, r, o, event + 3)
        here = self.mine(r, o, self.spans(o, phase, self.spot[d]))
        if phase < 2:
            self.add_into(here, [a, b])
        else:
            total = here[0, 0, 0].astype(jnp.float32) + a[0, 0, 0].astype(jnp.float32)
            self.out[r, o] = total + b[0, 0, 0].astype(jnp.float32)


def reduce_buffers(rounds):
    bufs = []
    for o in range(3):
        for phase in range(3):
            order = ORDERS[o]
            sizes = [RING] * 3
            for k in range(phase + 1):
                sizes[order[k]] = 1
            half = list(sizes)
            if phase < 2:
                half[order[phase + 1]] = 2
            for s in (half, sizes):
                bufs.append(pltpu.VMEM((rounds, 2, *s, UNIT, 128), jnp.bfloat16))
    return bufs


def norm_back(grad, scaled, inverse, gain):
    e = grad * gain
    mean_e = jnp.mean(e, axis=1, keepdims=True)
    mean_eh = jnp.mean(e * scaled, axis=1, keepdims=True)
    return inverse * (e - mean_e - scaled * mean_eh)


def backward_kernel(
    lens_ref, vec_ref, dpool_ref, x_ref, slot_ref,
    w_in, h1_in, h2_in, inv_in, nl_in, act_in, gp_in, qkv_in, prob_in, ctx_in,
    token_out, rows_in, qkv_out, out_out, up_out, down_out, vec_out,
    w, h1, h2, inv, nl, act, gp, qkv, prob, ctx, parts, d2d, d_res, d_low, turned, dvec, vec_slots, red_out, near_out, near_in, half_in, rows_out, *rest,
):
    bufs = rest[:18]
    send_sem, recv_sem, swap_send, swap_recv, free_sem, vec_send, vec_recv, load_sem, gp_sem, w_sem, near_send, near_recv, rows_sem = rest[18:]
    me = lax.axis_index("wide") * 8 + lax.axis_index("narrow")
    spot, core = where_am_i()
    bf, f32 = jnp.bfloat16, jnp.float32

    def load(src, dst, at):
        copy = pltpu.make_async_copy(src, dst, load_sem.at[at])
        copy.start()
        return copy

    def load_w(r, at):
        copy = pltpu.make_async_copy(w_in.at[r], w.at[at], w_sem.at[r])
        copy.start()
        return copy

    def load_gp(y, at):
        return pltpu.make_async_copy(gp_in.at[pl.ds(3 * y, 3)], gp.at[at], gp_sem.at[at])

    get_h2, get_inv = load(h2_in, h2, 0), load(inv_in, inv, 1)
    get_act = load(act_in, act, 2)
    get_w2 = load_w(2, 0)
    load_gp(0, 0).start()
    load_gp(1, 1).start()
    get_nl = load(nl_in, nl, 3)
    get_w1 = load_w(1, 1)
    get_h1, get_ctx = load(h1_in, h1, 4), load(ctx_in, ctx, 5)
    get_qkv, get_prob = load(qkv_in, qkv, 6), load(prob_in, prob, 7)
    all_here = greet_all()
    red = Reduce(parts, bufs, red_out, send_sem, recv_sem, spot, core)
    swaps = {}

    def give(r):
        if r == 0:
            pl.semaphore_wait(free_sem, 1)
        for o in range(3):
            copy = pltpu.make_async_remote_copy(
                src_ref=parts.at[r, 1 - core, o], dst_ref=d2d.at[r % 2, o],
                send_sem=swap_send.at[r, o], recv_sem=swap_recv.at[r, o],
                device_id=device_at(spot, 1 - core), device_id_type=MESH,
            )
            copy.start()
            red.sent.append(copy)

    def take(r):
        for o in range(3):
            view = d2d.at[r % 2, o]
            pltpu.make_async_copy(view, view, swap_recv.at[r, o]).wait()
            red.add_into(parts.at[r, core, o], [view])
            red.first(r, o, 0)
        if r == 2:
            pl.semaphore_signal(free_sem, inc=1, device_id=device_at(spot, 1 - core), device_id_type=MESH)

    def second(r, phase):
        for o in range(3):
            red.second(r, o, phase)

    def third(r, phase):
        for o in range(3):
            red.third(r, o, phase)
            if phase < 2:
                red.first(r, o, phase + 1)

    dvec[0] = jnp.zeros((16, 768), f32)

    def add_vec(row, value):
        dvec[0, row : row + 1, :] = dvec[0, row : row + 1, :] + value

    def total(value):
        return jnp.sum(value, axis=0, keepdims=True)

    get_h2.wait()
    get_inv.wait()

    def norm_two_step(s, _):
        rows = pl.ds(pl.multiple_of(s * SEQ, SEQ), SEQ)
        live = lax.broadcasted_iota(jnp.int32, (SEQ, 768), 0) < lens_ref[s]
        grad = jnp.where(live, jnp.broadcast_to(dpool_ref[s], (SEQ, 768)), 0.0)
        scaled = h2[rows, :]
        inverse = inv[1, rows, 0:1]
        back = norm_back(grad, scaled, inverse, vec_ref[1:2, :])
        low = back.astype(bf)
        d_res[rows, :] = back
        d_low[rows, :] = low
        add_vec(1, total(grad * scaled))
        add_vec(7, total(grad))
        add_vec(6, total(low.astype(f32)))
        return 0

    lax.fori_loop(0, 8, norm_two_step, 0)
    get_act.wait()

    def down_step(y, _):
        hidden = jnp.concatenate([act[3 * y], act[3 * y + 1], act[3 * y + 2]], axis=1)
        turned[...] = hidden.T
        for p in range(3):
            block = mm(turned[...], d_low[:, 256 * p : 256 * p + 256]).astype(bf)
            for k in range(2):
                cb = 2 * p + k
                for z in range(RING):
                    for x in range(RING):
                        at = UNIT * (RING * z + x)
                        parts[2, cb // 3, cb % 3, x, y, z] = block[at : at + UNIT, 128 * k : 128 * k + 128]
        return 0

    lax.fori_loop(0, RING, down_step, 0)
    all_here()
    give(2)
    get_w2.wait()

    def pre_step(y, _):
        at = y % 2
        load_gp(y, at).wait()
        columns = [
            jnp.concatenate([w[0, cb // 3, cb % 3, x, y, z] for z in range(RING) for x in range(RING)], axis=0)
            for cb in range(6)
        ]
        weight = jnp.concatenate(columns, axis=1)
        for j in range(3):
            grad = mm_nt(d_low[...], weight[256 * j : 256 * j + 256, :]) * gp[at, j]
            low = grad.astype(bf)
            act[3 * y + j] = low
            cut = slice(256 * j, 256 * j + 256)
            dvec[0, pl.ds(8 + y, 1), cut] = total(low.astype(f32))

        @pl.when(y < 2)
        def _():
            load_gp(y + 2, at).start()

        return 0

    lax.fori_loop(0, RING, pre_step, 0)
    get_w0 = load_w(0, 0)
    take(2)
    get_nl.wait()
    turned_nl = nl[...].T
    turned[:, :] = turned_nl

    def up_step(n2, _):
        block = mm(turned[...], act[n2]).astype(bf)
        c, o, x = n2 // 6, n2 // 2 % 3, n2 % 2 * 2
        for k in range(2):
            parts[1, c, o, x + k] = block[:, 128 * k : 128 * k + 128].reshape(RING, RING, UNIT, 128)
        return 0

    lax.fori_loop(0, 12, up_step, 0)
    give(1)
    second(2, 0)
    get_w1.wait()

    def six_blocks(at, n):
        blocks = []
        for k in range(6):
            m = n + k
            blocks.append(w[at, m // 12, m // 4 % 3, m % 4].reshape(768, 128))
        return jnp.concatenate(blocks, axis=1)

    def up_back_step(t, _):
        low = jnp.concatenate([act[3 * t], act[3 * t + 1], act[3 * t + 2]], axis=1)
        weight = six_blocks(1, 6 * t)
        for p in range(3):
            cut = slice(256 * p, 256 * p + 256)
            d_res[:, cut] = d_res[:, cut] + mm_nt(low, weight[cut, :])
        return 0

    lax.fori_loop(0, RING, up_back_step, 0)
    take(1)
    third(2, 0)
    get_h1.wait()

    def norm_one_step(s, _):
        rows = pl.ds(pl.multiple_of(s * SEQ, SEQ), SEQ)
        grad, scaled = d_res[rows, :], h1[rows, :]
        back = norm_back(grad, scaled, inv[0, rows, 0:1], vec_ref[0:1, :])
        low = back.astype(bf)
        d_res[rows, :] = back
        d_low[rows, :] = low
        add_vec(0, total(grad * scaled))
        add_vec(5, total(grad))
        add_vec(4, total(low.astype(f32)))
        return 0

    lax.fori_loop(0, 8, norm_one_step, 0)
    second(1, 0)
    get_ctx.wait()
    turned[...] = jnp.concatenate([ctx[0], ctx[1], ctx[2]], axis=1).T
    get_w0.wait()
    weight = six_blocks(0, 18)
    for p in range(3):
        cut = slice(256 * p, 256 * p + 256)
        block = mm(turned[...], d_low[:, cut]).astype(bf)
        for k in range(2):
            n = 18 + 2 * p + k
            parts[0, n // 12, n // 4 % 3, n % 4] = block[:, 128 * k : 128 * k + 128].reshape(RING, RING, UNIT, 128)
        ctx[p] = mm_nt(d_low[...], weight[cut, :]).astype(bf)
    second(2, 1)
    third(1, 0)
    get_qkv.wait()
    get_prob.wait()
    mask = head_mask()

    def attend_back(s, _):
        rows = pl.ds(pl.multiple_of(s * SEQ, SEQ), SEQ)
        for p in range(3):
            query, key_part, value = qkv[p, rows, :], qkv[3 + p, rows, :], qkv[6 + p, rows, :]
            wide_grad = spread_heads(ctx[p, rows, :], mask)
            probs = prob[s, p]
            d_value = mm(probs.astype(bf), wide_grad)
            d_probs = mm_nt(value, wide_grad)
            centre = jnp.sum(probs * d_probs, axis=0, keepdims=True)
            d_scores = (probs * (d_probs - centre)).astype(bf)
            d_query = gather_heads(mm_tn(d_scores, key_part), mask) * 0.125
            d_key = mm(d_scores, spread_heads(query, mask)) * 0.125
            low_query, low_value = d_query.astype(bf), d_value.astype(bf)
            qkv[p, rows, :] = low_query
            qkv[3 + p, rows, :] = d_key.astype(bf)
            qkv[6 + p, rows, :] = low_value
            cut = slice(256 * p, 256 * p + 256)
            dvec[0, 2:3, cut] = dvec[0, 2:3, cut] + total(low_query.astype(f32))
            dvec[0, 3:4, cut] = dvec[0, 3:4, cut] + total(low_value.astype(f32))
        return 0

    lax.fori_loop(0, 8, attend_back, 0)
    vec_sent = []

    def vec_push(event, src, there, c):
        copy = pltpu.make_async_remote_copy(
            src_ref=src, dst_ref=vec_slots.at[event], send_sem=vec_send.at[event], recv_sem=vec_recv.at[event],
            device_id=device_at(there, c), device_id_type=MESH,
        )
        copy.start()
        vec_sent.append(copy)

    def vec_landed(event):
        ref = vec_slots.at[event]
        pltpu.make_async_copy(ref, ref, vec_recv.at[event]).wait()

    def vec_start(d):
        vec_push(1 + 3 * d, dvec.at[d + 1], moved(spot, d, 1), core)
        vec_push(2 + 3 * d, dvec.at[d + 1], moved(spot, d, -1), core)

    def vec_relay(d):
        vec_landed(1 + 3 * d)
        vec_push(3 + 3 * d, vec_slots.at[1 + 3 * d], moved(spot, d, 1), core)

    def vec_add(d):
        vec_landed(2 + 3 * d)
        vec_landed(3 + 3 * d)
        sides = vec_slots[1 + 3 * d] + vec_slots[2 + 3 * d]
        dvec[d + 2] = (dvec[d + 1] + sides) + vec_slots[3 + 3 * d]

    vec_push(0, dvec.at[0], spot, 1 - core)
    turned[...] = x_ref[...].T

    def qkv_step(n2, _):
        block = mm(turned[...], qkv[n2]).astype(bf)
        c, o, x = n2 // 6, n2 // 2 % 3, n2 % 2 * 2
        for k in range(2):
            parts[0, c, o, x + k] = block[:, 128 * k : 128 * k + 128].reshape(RING, RING, UNIT, 128)
        return 0

    lax.fori_loop(0, 9, qkv_step, 0)
    give(0)
    third(2, 1)
    second(1, 1)
    vec_landed(0)
    dvec[1] = dvec[0] + vec_slots[0]
    vec_start(0)

    def input_step(t, _):
        low = jnp.concatenate([qkv[3 * t], qkv[3 * t + 1], qkv[3 * t + 2]], axis=1)
        weight = six_blocks(0, 6 * t)
        for p in range(3):
            cut = slice(256 * p, 256 * p + 256)
            d_res[:, cut] = d_res[:, cut] + mm_nt(low, weight[cut, :])
        return 0

    lax.fori_loop(0, 3, input_step, 0)
    token_copy = pltpu.make_async_copy(d_res, token_out, load_sem.at[8])
    token_copy.start()
    d_low[...] = d_res[...].astype(bf)
    slots_hot = slot_hot(slot_ref)
    for q in range(4):
        rows = mm_tn(slots_hot[:, 256 * q : 256 * q + 256], d_low[...])
        rows_out[32 * q : 32 * q + 32] = pack_rows(rows)

    def hand_back(k, _):
        there = (me + k) % 128
        pltpu.make_async_remote_copy(
            src_ref=rows_out.at[there], dst_ref=rows_in.at[(128 - k) % 128],
            send_sem=rows_sem.at[0], recv_sem=rows_sem.at[1],
            device_id=(there // 8, there % 8), device_id_type=MESH,
        ).start()
        return 0

    lax.fori_loop(1, 128, hand_back, 0)
    keep_rows = pltpu.make_async_copy(rows_out.at[me], rows_in.at[0], load_sem.at[9])
    keep_rows.start()
    take(0)
    vec_relay(0)
    third(1, 1)
    second(2, 2)
    vec_add(0)
    vec_start(1)
    second(0, 0)
    vec_relay(1)
    second(1, 2)
    third(2, 2)
    third(0, 0)
    vec_add(1)
    vec_start(2)
    second(0, 1)
    vec_relay(2)
    third(1, 2)
    third(0, 1)
    vec_add(2)
    vec_out[...] = dvec[4]
    second(0, 2)
    third(0, 2)

    mine = spot[0] * 2 + core
    for j in range(8):
        for r in range(2):
            for o in range(3):
                at = 6 * (3 * r + o)
                near_out[j, at : at + 6, :] = red_out[r, o, 6 * j : 6 * j + 6, :]
    for k in range(1, 8):
        there = (mine + k) % 8
        copy = pltpu.make_async_remote_copy(
            src_ref=near_out.at[there], dst_ref=near_in.at[mine], send_sem=near_send.at[k], recv_sem=near_recv.at[k],
            device_id=(lax.axis_index("wide"), there), device_id_type=MESH,
        )
        copy.start()
        vec_sent.append(copy)
    theirs = pl.ds(pl.multiple_of(24 * (1 - core), 8), 24)
    copy = pltpu.make_async_remote_copy(
        src_ref=red_out.at[2, :, theirs], dst_ref=half_in, send_sem=near_send.at[0], recv_sem=near_recv.at[0],
        device_id=device_at(spot, 1 - core), device_id_type=MESH,
    )
    copy.start()
    vec_sent.append(copy)
    near_in[mine] = near_out[mine]
    for k in range(1, 8):
        ref = near_in.at[(mine + 8 - k) % 8]
        pltpu.make_async_copy(ref, ref, near_recv.at[k]).wait()
    pltpu.make_async_copy(half_in, half_in, near_recv.at[0]).wait()
    for c in range(2):
        for o in range(3):
            for x in range(RING):
                n, j = c * 12 + o * 4 + x, 2 * x + c
                block = near_in[j, 6 * o : 6 * o + 6, :]
                if n < 18:
                    qkv_out[:, 128 * n : 128 * n + 128] = block
                else:
                    out_out[:, 128 * (n - 18) : 128 * (n - 18) + 128] = block
                up_out[:, 128 * n : 128 * n + 128] = near_in[j, 18 + 6 * o : 24 + 6 * o, :]
    ours = pl.ds(pl.multiple_of(24 * core, 8), 24)
    for o in range(3):
        a, b = red_out[2, o, ours, :], half_in[o]
        down_out[:, 128 * o : 128 * o + 128] = jnp.where(core == 0, a, b)
        down_out[:, 384 + 128 * o : 512 + 128 * o] = jnp.where(core == 0, b, a)
    others = rows_in.at[pl.ds(0, 127)]
    pltpu.make_async_copy(others, others, rows_sem.at[1]).wait()
    pltpu.make_async_copy(others, others, rows_sem.at[0]).wait()
    token_copy.wait()
    keep_rows.wait()
    for copy in red.sent + vec_sent:
        copy.wait_send()


def backward_pass(lens, vectors, d_pool, x, slots, w, h1, h2, inv, nl, act, gp, qkv, prob, ctx):
    bf, f32 = jnp.bfloat16, jnp.float32
    anywhere = pl.BlockSpec(memory_space=pl.ANY)
    vmem = pl.BlockSpec(memory_space=pltpu.VMEM)
    dma = pltpu.SemaphoreType.DMA
    scratch = [
        pltpu.VMEM((2, *w.shape[1:]), bf),
        pltpu.VMEM(h1.shape, f32),
        pltpu.VMEM(h2.shape, f32),
        pltpu.VMEM(inv.shape, f32),
        pltpu.VMEM(nl.shape, bf),
        pltpu.VMEM(act.shape, bf),
        pltpu.VMEM((2, 3, 512, 256), f32),
        pltpu.VMEM(qkv.shape, bf),
        pltpu.VMEM(prob.shape, f32),
        pltpu.VMEM(ctx.shape, bf),
        pltpu.VMEM(w.shape, bf),
        pltpu.VMEM((2, *w.shape[2:]), bf),
        pltpu.VMEM((512, 768), f32),
        pltpu.VMEM((512, 768), bf),
        pltpu.VMEM((768, 512), bf),
        pltpu.VMEM((5, 16, 768), f32),
        pltpu.VMEM((10, 16, 768), f32),
        pltpu.VMEM((3, 3, UNIT, 128), f32),
        pltpu.VMEM((8, 40, 128), f32),
        pltpu.VMEM((8, 40, 128), f32),
        pltpu.VMEM((3, 24, 128), f32),
        pltpu.VMEM((128, 16, 384), bf),
        *reduce_buffers(3),
        dma((3, 3, 13)),
        dma((3, 3, 13)),
        dma((3, 3)),
        dma((3, 3)),
        pltpu.SemaphoreType.REGULAR,
        dma((10,)),
        dma((10,)),
        dma((10,)),
        dma((2,)),
        dma((3,)),
        dma((8,)),
        dma((8,)),
        dma((2,)),
    ]
    shapes = [
        ((512, 768), f32),
        ((128, 16, 384), bf),
        ((6, 2304), f32),
        ((6, 768), f32),
        ((6, 3072), f32),
        ((24, 768), f32),
        ((16, 768), f32),
    ]
    return pl.pallas_call(
        backward_kernel,
        out_shape=[jax.ShapeDtypeStruct(*s) for s in shapes],
        in_specs=[pl.BlockSpec(memory_space=pltpu.SMEM)] + [vmem] * 4 + [anywhere] * 10,
        out_specs=[anywhere] * 2 + [vmem] * 5,
        scratch_shapes=scratch,
        compiler_params=pltpu.CompilerParams(
            collective_id=2, has_side_effects=True, vmem_limit_bytes=64 * 1024 * 1024 - 65536
        ),
        name="backward_pass",
    )(lens, vectors, d_pool, x, slots, w, h1, h2, inv, nl, act, gp, qkv, prob, ctx)


TABLE_STEP = 560


def table_kernel(rows_ref, asked_ref, out_ref, rows):
    at = pl.program_id(0)

    @pl.when(at == 0)
    def _():
        for q in range(8):
            rows[128 * q : 128 * q + 128, :] = unpack_rows(rows_ref[16 * q : 16 * q + 16])

    name = (lax.broadcasted_iota(jnp.int32, (TABLE_STEP, 1024), 0) + at * TABLE_STEP).astype(jnp.float32)
    out_ref[...] = mm((name == asked_ref[0:1, :]).astype(jnp.bfloat16), rows[...])


def table_sums(rows, asked, table_rows):
    return pl.pallas_call(
        table_kernel,
        out_shape=jax.ShapeDtypeStruct((table_rows, 768), jnp.float32),
        grid=(table_rows // TABLE_STEP,),
        in_specs=[
            pl.BlockSpec((128, 16, 384), lambda i: (0, 0, 0)),
            pl.BlockSpec((8, 1024), lambda i: (0, 0)),
        ],
        out_specs=pl.BlockSpec((TABLE_STEP, 768), lambda i: (i, 0)),
        scratch_shapes=[pltpu.VMEM((1024, 768), jnp.bfloat16)],
        compiler_params=pltpu.CompilerParams(vmem_limit_bytes=40 * 1024 * 1024),
        name="table_sums",
    )(rows, asked)


def shards(token_ids, lengths, groups, table, w_qkv, w_out, w_up, w_down, gains, biases):
    bf, f32 = jnp.bfloat16, jnp.float32
    flat_ids = token_ids.reshape(-1)
    table_rows = table.shape[0]
    rank_at = lax.axis_index(("wide", "narrow"))
    owner = flat_ids // table_rows
    hot = (owner[:, None] == jnp.arange(128)[None, :]).astype(bf)
    local = jnp.broadcast_to((flat_ids - owner * table_rows + 1).astype(f32)[:, None], (512, 128))
    first = jnp.concatenate([w_qkv[0], w_out[0]], axis=1)
    units = jnp.stack([first, w_up[0]]).reshape(2, 6, 2, 3, RING, 128)
    units = units.transpose(4, 2, 0, 3, 1, 5).reshape(8, 36, 128)
    vectors = jnp.concatenate([gains[0], biases[0]])
    named = jnp.concatenate([groups.astype(bf)[None], jnp.zeros((11, 4), bf)])
    spread = jnp.concatenate(
        [jnp.tile(vectors, (1, 8)), jnp.zeros((12, 16), bf), jnp.tile(named, (1, 8)), jnp.zeros((12, 32), bf)], axis=1
    )
    lane = jnp.arange(128)
    place = jnp.where(lane < 48, lane // 6, jnp.where(lane < 64, 8, (lane - 64) // 4))
    spread = jnp.where((place == rank_at % 8)[None, :], spread, jnp.zeros((), bf))
    sent = jnp.concatenate([units, jnp.broadcast_to(spread[None], (8, 12, 128))], axis=1)
    halves = w_down[0].reshape(24, 2, 3, 128).transpose(1, 2, 0, 3).reshape(2, 72, 128)
    halves = jnp.pad(halves, ((0, 0), (0, 8), (0, 0)))
    lens = lengths.reshape(-1)
    kept = forward_pass(lens, sent, halves, hot, local, table)
    w, vecs, h1, h2, inv, nl, act, gate, qkv, prob, ctx, x, d_pool, loss_tile, slots, asked = kept
    token_grads, row_grads, d_qkv, d_out, d_up, d_down, d_vectors = backward_pass(
        lens, vecs, d_pool, x, slots, w, h1, h2, inv, nl, act, gate, qkv, prob, ctx
    )
    d_vectors = lax.dynamic_slice_in_dim(d_vectors[:12], rank_at * 6, 6, 1)
    return (
        loss_tile[:4, :2],
        token_grads.reshape(token_ids.shape + (768,)),
        table_sums(row_grads, asked, table_rows),
        d_qkv[None],
        d_out[None],
        d_up[None],
        d_down[None],
        d_vectors[None, :2],
        d_vectors[None, 2:],
    )


def solution(mesh):
    in_specs = (
        P(("wide", "narrow"), None, None),
        P(("wide", "narrow"), None),
        P(("wide", "narrow")),
        P(("wide", "narrow"), None),
        P(None, ("wide", "narrow"), None),
        P(None, ("wide", "narrow"), None),
        P(None, ("wide", "narrow"), None),
        P(None, ("wide", "narrow"), None),
        P(None, None, ("wide", "narrow")),
        P(None, None, ("wide", "narrow")),
    )
    out_specs = (
        P(("wide", "narrow"), None),
        P(("wide", "narrow"), None, None, None),
        P(("wide", "narrow"), None),
        P(None, ("wide", "narrow"), None),
        P(None, ("wide", "narrow"), None),
        P(None, ("wide", "narrow"), None),
        P(None, ("wide", "narrow"), None),
        P(None, None, ("wide", "narrow")),
        P(None, None, ("wide", "narrow")),
    )
    return jax.shard_map(shards, mesh=mesh, in_specs=in_specs, out_specs=out_specs, check_vma=False)
```

```python
import functools

import jax
import jax.numpy as jnp
from jax import lax
from jax.experimental import pallas as pl
from jax.experimental.pallas import tpu as pltpu
from jax.sharding import PartitionSpec as P

HEAD_DIM = 64
SEQ = 64


logit_scale = 10.0
margin = 0.3
norm_eps = 1e-12
pool_eps = 1e-06
far_low = -1e30


MESH = pl.DeviceIdType.MESH
RING = 4
ORDERS = ((0, 1, 2), (1, 2, 0), (2, 0, 1))
UNIT = 48


def where_am_i():
    wide = lax.axis_index("wide")
    narrow = lax.axis_index("narrow")
    return [narrow // 2, wide // RING, wide % RING], narrow % 2


def device_at(spot, core):
    return (spot[1] * RING + spot[2], spot[0] * 2 + core)


def moved(spot, dim, by):
    there = list(spot)
    there[dim] = (spot[dim] + by) % RING
    return there


def block_of(ref, part, core, order, spans):
    return ref.at[(part, core, order) + tuple(pl.ds(*spans[d]) for d in range(3))]


class Gather:
    def __init__(self, out, fifteen, send_sem, recv_sem, spot, core, dims):
        self.out, self.send_sem, self.recv_sem = out, send_sem, recv_sem
        self.spot, self.core, self.dims = spot, core, dims
        self.fifteen = fifteen
        self.sent = []

    def block(self, r, o, spans, core):
        return self.out.at[(r, core, o) + tuple(pl.ds(*spans[d]) for d in self.dims)]

    def here(self, o):
        return {d: (self.spot[d], 1) for d in range(3)}

    def plane(self, o, at, half=None):
        first, second, ring = ORDERS[o]
        spans = {first: (0, RING) if half is None else (2 * half, 2), second: (0, RING), ring: (at, 1)}
        return spans

    def push(self, r, o, event, spans, there, core=None, src=None):
        dst = self.block(r, o, spans, self.core)
        copy = pltpu.make_async_remote_copy(
            src_ref=dst if src is None else src,
            dst_ref=dst,
            send_sem=self.send_sem.at[r, o, event],
            recv_sem=self.recv_sem.at[r, o, event],
            device_id=device_at(there, self.core if core is None else core),
            device_id_type=MESH,
        )
        copy.start()
        return copy

    def landed(self, r, o, event, spans, core=None):
        dst = self.block(r, o, spans, self.core if core is None else core)
        pltpu.make_async_copy(dst, dst, self.recv_sem.at[r, o, event]).wait()

    def begin(self, r, o, src):
        first, second, ring = ORDERS[o]
        here = self.here(o)

        def one(k, _):
            there = moved(moved(self.spot, first, k % RING), second, k // RING)
            self.push(r, o, 0, here, there, src=src)
            return 0

        lax.fori_loop(1, 16, one, 0)

    def plane_done(self, r, o, sem):
        pltpu.make_async_copy(self.fifteen, self.fifteen, sem.at[r, o, 0]).wait()

    def planes(self, r, o):
        self.plane_done(r, o, self.recv_sem)
        self.share(r, o, 5, self.plane(o, self.spot[ORDERS[o][2]]))

    def ring(self, o):
        d = ORDERS[o][2]
        v = self.spot[d]
        up, down = moved(self.spot, d, 1), moved(self.spot, d, -1)
        return v, (v - 1) % RING, (v + 1) % RING, (v + 2) % RING, up, down

    def share(self, r, o, event, spans):
        self.sent.append(self.push(r, o, event, spans, self.spot, 1 - self.core))

    def spread(self, r, o, direct=False):
        v, low, high, far, up, down = self.ring(o)
        here = self.plane(o, v)
        self.sent.append(self.push(r, o, 1, here, up))
        self.sent.append(self.push(r, o, 2, here, down))
        if direct:
            self.sent.append(self.push(r, o, 3, here, moved(self.spot, ORDERS[o][2], 2)))

    def relay(self, r, o):
        v, low, high, far, up, down = self.ring(o)
        self.landed(r, o, 1, self.plane(o, low))
        self.sent.append(self.push(r, o, 3, self.plane(o, low, 0), up))
        self.landed(r, o, 2, self.plane(o, high))
        self.sent.append(self.push(r, o, 4, self.plane(o, high, 1), down))
        self.share(r, o, 6, self.plane(o, low))
        self.share(r, o, 7, self.plane(o, high))

    def finish(self, r, o):
        v, low, high, far, up, down = self.ring(o)
        self.landed(r, o, 3, self.plane(o, far, 0))
        self.landed(r, o, 4, self.plane(o, far, 1))
        self.share(r, o, 8, self.plane(o, far))

    def collect(self, r, o):
        v, low, high, far, up, down = self.ring(o)
        for k, at in enumerate((low, high, far)):
            self.landed(r, o, 1 + k, self.plane(o, at))
            self.share(r, o, 6 + k, self.plane(o, at))

    def shared_done(self, r, o):
        v, low, high, far, up, down = self.ring(o)
        for k, at in enumerate((v, low, high, far)):
            self.landed(r, o, 5 + k, self.plane(o, at), 1 - self.core)

    def drain(self, rounds):
        for r in range(rounds):
            for o in range(3):
                self.plane_done(r, o, self.send_sem)
        for copy in self.sent:
            copy.wait_send()


def mm(a, b):
    return jnp.dot(a, b, preferred_element_type=jnp.float32)


def mm_nt(a, b):
    return lax.dot_general(a, b, (((1,), (1,)), ((), ())), preferred_element_type=jnp.float32)


def mm_tn(a, b):
    return lax.dot_general(a, b, (((0,), (0,)), ((), ())), preferred_element_type=jnp.float32)


def head_mask():
    row = lax.broadcasted_iota(jnp.int32, (256, 256), 0) // HEAD_DIM
    col = lax.broadcasted_iota(jnp.int32, (256, 256), 1) // HEAD_DIM
    return row == col


def spread_heads(part, mask):
    four = jnp.concatenate([part] * 4, axis=0)
    return jnp.where(mask, four, jnp.zeros((), four.dtype))


def gather_heads(wide_part, mask):
    kept = jnp.where(mask, wide_part, 0.0)
    return (kept[:64] + kept[64:128]) + (kept[128:192] + kept[192:])


def panel(w, r, n2):
    c, o, x = n2 // 6, n2 // 2 % 3, n2 % 2 * 2
    pair = [w[r, c, o, x + k].reshape(768, 128) for k in range(2)]
    return jnp.concatenate(pair, axis=1)


def down_panel(w, cb, y):
    c, o = cb // 3, cb % 3
    return jnp.concatenate([w[2, c, o, x, y, z] for z in range(RING) for x in range(RING)], axis=0)


def split_low(value):
    high = value.astype(jnp.bfloat16)
    return high, (value - high.astype(jnp.float32)).astype(jnp.bfloat16)


def greet_all():
    barrier = pltpu.get_barrier_semaphore()
    me = lax.axis_index("wide") * 8 + lax.axis_index("narrow")

    def hello(k, _):
        there = (me + k) % 128
        pl.semaphore_signal(barrier, inc=1, device_id=(there // 8, there % 8), device_id_type=MESH)
        return 0

    lax.fori_loop(1, 128, hello, 0)
    return lambda: pl.semaphore_wait(barrier, 127)


def pack_rows(rows):
    n = rows.shape[0] // 8
    left, right = rows[:, :384].reshape(n, 8, 384), rows[:, 384:].reshape(n, 8, 384)
    return jnp.concatenate([left, right], axis=1).astype(jnp.bfloat16)


def unpack_rows(packed):
    wide_rows = packed.astype(jnp.float32)
    rows = jnp.concatenate([wide_rows[:, :8], wide_rows[:, 8:]], axis=2)
    return rows.reshape(-1, 768).astype(jnp.bfloat16)


def digits(value):
    high = jnp.floor(value * 0.015625)
    return high.astype(jnp.bfloat16), (value - 64.0 * high).astype(jnp.bfloat16)


def token_slots(ids_ref, table_rows):
    f32, bf = jnp.float32, jnp.bfloat16
    sents = jnp.concatenate([ids_ref[s // 2, s % 2 : s % 2 + 1, :] for s in range(8)], axis=0)
    row = lax.broadcasted_iota(jnp.int32, (512, 8), 0)
    col = lax.broadcasted_iota(jnp.int32, (512, 8), 1)
    member_of = (row // SEQ == col).astype(bf)
    wide_ids = jnp.zeros((512, SEQ), f32)
    for shift in (0, 7, 14):
        digit = ((sents >> shift) & 127).astype(f32).astype(bf)
        wide_ids = wide_ids + mm(member_of, digit) * float(1 << shift)
    row = lax.broadcasted_iota(jnp.int32, (512, SEQ), 0)
    col = lax.broadcasted_iota(jnp.int32, (512, SEQ), 1)
    name = jnp.sum(jnp.where(row % SEQ == col, wide_ids, 0.0), axis=1, keepdims=True)
    owner = jnp.floor((name + 0.5) * (1.0 / table_rows))
    local = name - owner * float(table_rows) + 1.0
    lane = lax.broadcasted_iota(jnp.int32, (512, 128), 1).astype(f32)
    hot = (lane == owner).astype(bf)
    row = lax.broadcasted_iota(jnp.int32, (512, 512), 0)
    col = lax.broadcasted_iota(jnp.int32, (512, 512), 1)
    before = mm((col < row).astype(bf), hot)
    rank = jnp.sum(jnp.where(lane == owner, before, 0.0), axis=1, keepdims=True)
    high, low = digits(jnp.broadcast_to(local, (512, 128)))
    zero = jnp.zeros((), bf)
    here = lane == rank
    both = mm_tn(hot, jnp.concatenate([jnp.where(here, high, zero), jnp.where(here, low, zero)], axis=1))
    return owner * 8.0 + rank, both[:, :128] * 64.0 + both[:, 128:]


def slot_hot(slot_ref):
    lane = lax.broadcasted_iota(jnp.int32, (512, 128), 1).astype(jnp.float32)
    parts = [(slot_ref[...] == lane + 128.0 * i).astype(jnp.bfloat16) for i in range(8)]
    return jnp.concatenate(parts, axis=1)


def forward_kernel(
    lens_ref, groups_ref, ids_ref, wq_ref, wo_ref, wu_ref, wd_ref, gains_ref, bias_ref, table_in,
    w_out, vec_out, h1_out, h2_out, inv_out, nl_out, act_out, gp_out, qkv_out, prob_out, ctx_out, x_out,
    dpool_out, loss_out, slot_out, asked_out,
    w, vecs, tiles, h1, h2, inv, nl, act, gp, qkv, prob, ctx, x_ref, resid, pooled, rnorm, pool_own, pool_swap, pool_all,
    left3, right3, stats, own, sent_ref, near, halves_ref, half_got, table, ids_out, ids_in, ids, asked, rows_out, rows_in,
    row_mat, units_size, pool_size,
    send_sem, recv_sem, local_sem, pool_send, pool_recv, tile_send, tile_recv, swap_sem, load_sem, save_sem,
    near_send, near_recv, ids_sem, rows_sem, table_sem,
):
    spot, core = where_am_i()
    me = lax.axis_index("wide") * 8 + lax.axis_index("narrow")
    mine = spot[0] * 2 + core
    bf, f32 = jnp.bfloat16, jnp.float32
    all_here = greet_all()
    table_rows = table_in.shape[0]
    get_table = pltpu.make_async_copy(table_in, table.at[pl.ds(0, table_rows)], table_sem.at[0])
    get_table.start()
    table[pl.ds(table_rows, 4096 - table_rows), :] = jnp.zeros((4096 - table_rows, 768), bf)
    slot, wanted = token_slots(ids_ref, table_rows)
    slot_out[...] = jnp.broadcast_to(slot, (512, 128))
    ids[...] = wanted

    def row_out(i, _):
        ids_out[i] = ids[pl.ds(i, 1), :]
        return 0

    lax.fori_loop(0, 128, row_out, 0)

    for c in range(2):
        for o in range(3):
            for x in range(RING):
                n, j = c * 12 + o * 4 + x, 2 * x + c
                source = wq_ref if n < 18 else wo_ref
                cut = slice(128 * (n % 18), 128 * (n % 18) + 128)
                sent_ref[j, 6 * o : 6 * o + 6, :] = source[0, :, cut].astype(f32)
                sent_ref[j, 18 + 6 * o : 24 + 6 * o, :] = wu_ref[0, :, 128 * n : 128 * n + 128].astype(f32)
    lane = lax.broadcasted_iota(jnp.int32, (8, 128), 1)
    place = (lane == 6 * mine + lax.broadcasted_iota(jnp.int32, (8, 128), 0)).astype(bf)[0:6]
    named = jnp.zeros((1, 128), f32)
    for p in range(4):
        named = named + jnp.where(lane[0:1] == 64 + 4 * mine + p, groups_ref[p].astype(f32), 0.0)
    gain_rows, bias_rows = mm(gains_ref[0], place), mm_tn(bias_ref[0], place)
    for j in range(8):
        sent_ref[j, 36:38, :] = gain_rows
        sent_ref[j, 38:48, :] = bias_rows
        sent_ref[j, 36:37, :] = sent_ref[j, 36:37, :] + named
    for o in range(3):
        a, b = wd_ref[0, :, 128 * o : 128 * o + 128], wd_ref[0, :, 384 + 128 * o : 512 + 128 * o]
        a, b = a.astype(f32), b.astype(f32)
        halves_ref[0, o] = jnp.where(core == 0, a, b)
        halves_ref[1, o] = jnp.where(core == 0, b, a)
    all_here()

    sent = []
    for k in range(1, 8):
        there = (mine + k) % 8
        copy = pltpu.make_async_remote_copy(
            src_ref=sent_ref.at[there], dst_ref=near.at[mine], send_sem=near_send.at[k], recv_sem=near_recv.at[k],
            device_id=(lax.axis_index("wide"), there), device_id_type=MESH,
        )
        copy.start()
        sent.append(copy)
    copy = pltpu.make_async_remote_copy(
        src_ref=halves_ref.at[1], dst_ref=half_got, send_sem=near_send.at[0], recv_sem=near_recv.at[0],
        device_id=device_at(spot, 1 - core), device_id_type=MESH,
    )
    copy.start()
    sent.append(copy)

    def ask(k, _):
        there = (me + k) % 128
        pltpu.make_async_remote_copy(
            src_ref=ids_out.at[there], dst_ref=ids_in.at[(128 - k) % 128],
            send_sem=ids_sem.at[0], recv_sem=ids_sem.at[1],
            device_id=(there // 8, there % 8), device_id_type=MESH,
        ).start()
        return 0

    lax.fori_loop(1, 128, ask, 0)
    ids_in[0] = ids_out[me]
    near[mine] = sent_ref[mine]
    for k in range(1, 8):
        ref = near.at[(mine + 8 - k) % 8]
        pltpu.make_async_copy(ref, ref, near_recv.at[k]).wait()
    pltpu.make_async_copy(half_got, half_got, near_recv.at[0]).wait()
    row = lax.broadcasted_iota(jnp.int32, (288, 384), 0)
    col = lax.broadcasted_iota(jnp.int32, (288, 384), 1)
    unit, at = row // UNIT, row % UNIT
    pick = col == at // 6 * UNIT + unit * 6 + at % 6
    units = mm(pick.astype(bf), near[...].reshape(384, 128).astype(bf)).astype(bf)
    for r in range(2):
        for o in range(3):
            first_row = UNIT * (3 * r + o)
            own[r, o] = units[first_row : first_row + UNIT].reshape(1, 1, 1, UNIT, 128)
    for o in range(3):
        a, b = halves_ref[0, o], half_got[o]
        upper, lower = jnp.where(core == 0, a, b), jnp.where(core == 0, b, a)
        own[2, o] = jnp.concatenate([upper, lower], axis=0).astype(bf).reshape(1, 1, 1, UNIT, 128)
    small = jnp.zeros((16, 128), f32)
    for j in range(8):
        small = small + near[j, 32:48, :]
    tiles[pl.ds(spot[1], 1), pl.ds(spot[2], 1)] = small.astype(bf).reshape(1, 1, 16, 128)

    g = Gather(w_out, units_size, send_sem, recv_sem, spot, core, (0, 1, 2))
    every = [(r, o) for r in range(3) for o in range(3)]
    keep = []
    for r, o in every:
        copy = pltpu.make_async_copy(own.at[r, o], g.block(r, o, g.here(o), core), local_sem.at[r, o])
        copy.start()
        keep.append(copy)
        g.begin(r, o, own.at[r, o])

    def tile_push(event, at, there):
        ref = tiles.at[at]
        copy = pltpu.make_async_remote_copy(
            src_ref=ref, dst_ref=ref, send_sem=tile_send.at[event], recv_sem=tile_recv.at[event],
            device_id=device_at(there, core), device_id_type=MESH,
        )
        copy.start()
        sent.append(copy)

    def tile_at(phase, v):
        return (pl.ds(v, 1), pl.ds(spot[2], 1)) if phase == 0 else (pl.ds(0, RING), pl.ds(v, 1))

    def tile_spread(phase):
        for k, by in enumerate((1, 2, 3)):
            tile_push(3 * phase + k, tile_at(phase, spot[phase + 1]), moved(spot, phase + 1, by))

    def tile_landed(phase):
        for k, by in enumerate((1, 2, 3)):
            ref = tiles.at[tile_at(phase, (spot[phase + 1] + RING - by) % RING)]
            pltpu.make_async_copy(ref, ref, tile_recv.at[3 * phase + k]).wait()

    tile_spread(0)
    for copy in keep:
        copy.wait()

    others = ids_in.at[pl.ds(0, 127)]
    pltpu.make_async_copy(others, others, ids_sem.at[1]).wait()

    def row_in(i, _):
        ids[pl.ds(i, 1), :] = ids_in[i]
        return 0

    lax.fori_loop(0, 128, row_in, 0)
    high, low = digits(ids[...])
    row = lax.broadcasted_iota(jnp.int32, (1024, 128), 0)
    col = lax.broadcasted_iota(jnp.int32, (1024, 128), 1)
    member_of = (row // 8 == col).astype(bf)
    both = mm(member_of, high) * 64.0 + mm(member_of, low)
    asked_col = jnp.sum(jnp.where(col == row % 8, both, 0.0), axis=1, keepdims=True) - 1.0
    asked[...] = jnp.broadcast_to(asked_col, (1024, 128))
    row = lax.broadcasted_iota(jnp.int32, (128, 1024), 0)
    col = lax.broadcasted_iota(jnp.int32, (128, 1024), 1)
    member_of = (col // 8 == row).astype(bf)
    both = mm_tn(high, member_of) * 64.0 + mm_tn(low, member_of)
    asked_row = jnp.sum(jnp.where(row == col % 8, both, 0.0), axis=0, keepdims=True) - 1.0
    asked_out[...] = jnp.broadcast_to(asked_row, (8, 1024))
    get_table.wait()

    def find(half):
        col = asked[512 * half : 512 * half + 512, :]
        lane = lax.broadcasted_iota(jnp.int32, (512, 128), 1).astype(f32)

        def chunk(i, _):
            first_row = i * 512
            base = lane + (first_row * 1).astype(f32)
            hot = jnp.concatenate([(col == base + 128.0 * j).astype(bf) for j in range(4)], axis=1)
            part = mm(hot, table[pl.ds(pl.multiple_of(first_row, 512), 512), :])
            resid[...] = jnp.where(i == 0, part, resid[...] + part)
            return 0

        lax.fori_loop(0, 8, chunk, 0)
        for q in range(4):
            rows_out[64 * half + 16 * q : 64 * half + 16 * q + 16] = pack_rows(resid[128 * q : 128 * q + 128, :])

        def answer(k, _):
            there = (me + k) % 128
            pltpu.make_async_remote_copy(
                src_ref=rows_out.at[k], dst_ref=rows_in.at[me], send_sem=rows_sem.at[0], recv_sem=rows_sem.at[1],
                device_id=(there // 8, there % 8), device_id_type=MESH,
            ).start()
            return 0

        lax.fori_loop(max(1, 64 * half), 64 * half + 64, answer, 0)

    find(0)
    rows_in[me] = rows_out[0]
    tile_landed(0)
    tile_spread(1)
    for o in range(3):
        g.planes(0, o)
        g.spread(0, o)
    find(1)
    for o in range(3):
        g.relay(0, o)
    for r in (1, 2):
        for o in range(3):
            g.planes(r, o)
    tile_landed(1)

    row_at = lax.broadcasted_iota(jnp.int32, (128, 768), 0)
    col_at = lax.broadcasted_iota(jnp.int32, (128, 768), 1)
    all_vec = jnp.zeros((16, 768), f32)
    all_grp = jnp.zeros((16, 512), f32)
    for slab in range(16):
        part = tiles[slab // RING, slab % RING]
        pick = (col_at == row_at + UNIT * slab) & (row_at < UNIT)
        all_vec = all_vec + mm(part, pick.astype(bf))
        pick = (col_at == row_at - 64 + 32 * slab) & (row_at >= 64) & (row_at < 96)
        all_grp = all_grp + mm(part, pick[:, :512].astype(bf))
    vecs[...] = jnp.concatenate([all_vec[4:16], all_vec[0:4]], axis=0)
    group_row = all_grp[4:5]
    saves = []

    def save(scratch, out, at):
        copy = pltpu.make_async_copy(scratch, out, save_sem.at[at])
        copy.start()
        saves.append(copy)

    def load(r, o, c):
        return pltpu.make_async_copy(w_out.at[r, c, o], w.at[r, c, o], load_sem.at[r, c, o])

    def collect(r):
        for o in range(3):
            g.collect(r, o)
            load(r, o, core).start()

    def arrived(r):
        for o in range(3):
            g.shared_done(r, o)
            load(r, o, 1 - core).start()
        for o in range(3):
            load(r, o, 0).wait()
            load(r, o, 1).wait()

    save(vecs, vec_out, 0)
    for o in range(3):
        g.finish(0, o)
        load(0, o, core).start()
    others = rows_in.at[pl.ds(0, 127)]
    pltpu.make_async_copy(others, others, rows_sem.at[1]).wait()
    for o in range(3):
        g.spread(1, o, True)
    for q in range(8):
        row_mat[128 * q : 128 * q + 128, :] = unpack_rows(rows_in[16 * q : 16 * q + 16])
    slots_hot = slot_hot(slot_out)
    for p in range(3):
        cut = slice(256 * p, 256 * p + 256)
        x_ref[:, cut] = mm(slots_hot, row_mat[:, cut]).astype(bf)
    save(x_ref, x_out, 10)
    arrived(0)
    mask = head_mask()

    def qkv_step(n2, _):
        kind, p = n2 // 3, n2 % 3
        rows = vecs[2:4, :]
        bias = jnp.where(kind == 0, rows[0:1], jnp.where(kind == 2, rows[1:2], 0.0))
        bias = jnp.where(p == 0, bias[:, :256], jnp.where(p == 1, bias[:, 256:512], bias[:, 512:]))
        qkv[n2] = (mm(x_ref[...], panel(w, 0, n2)) + bias).astype(bf)
        return 0

    lax.fori_loop(0, 9, qkv_step, 0)
    for o in range(3):
        g.spread(2, o, True)
    save(qkv, qkv_out, 1)

    def attend(s, _):
        rows = pl.ds(pl.multiple_of(s * SEQ, SEQ), SEQ)
        slot = lax.broadcasted_iota(jnp.int32, (SEQ, 256), 0)
        live = slot < lens_ref[s % 2, s // 2]
        for p in range(3):
            query, key_part, value = qkv[p, rows, :], qkv[3 + p, rows, :], qkv[6 + p, rows, :]
            scores = mm_nt(key_part, spread_heads(query, mask)) * 0.125
            scores = jnp.where(live, scores, far_low)
            powers = jnp.exp(scores - jnp.max(scores, axis=0, keepdims=True))
            probs = powers / jnp.sum(powers, axis=0, keepdims=True)
            prob[s, p] = probs
            ctx[p, rows, :] = gather_heads(mm_tn(probs.astype(bf), value), mask).astype(bf)
        return 0

    lax.fori_loop(0, 4, attend, 0)
    collect(1)
    lax.fori_loop(4, 8, attend, 0)
    save(prob, prob_out, 2)
    save(ctx, ctx_out, 3)
    context = jnp.concatenate([ctx[0], ctx[1], ctx[2]], axis=1)
    for p in range(3):
        resid[:, 256 * p : 256 * p + 256] = mm(context, panel(w, 0, 9 + p))

    def norm_one_step(s, _):
        rows = pl.ds(pl.multiple_of(s * SEQ, SEQ), SEQ)
        value = x_ref[rows, :].astype(f32) + (resid[rows, :] + vecs[4:5, :])
        centred = value - jnp.mean(value, axis=1, keepdims=True)
        inverse = lax.rsqrt(jnp.mean(centred * centred, axis=1, keepdims=True) + norm_eps)
        scaled = centred * inverse
        h1[rows, :] = scaled
        inv[0, rows, :] = jnp.broadcast_to(inverse, (SEQ, 128))
        normed = scaled * vecs[0:1, :] + vecs[5:6, :]
        nl[rows, :] = normed.astype(bf)
        resid[rows, :] = normed + vecs[6:7, :]
        return 0

    lax.fori_loop(0, 8, norm_one_step, 0)
    save(h1, h1_out, 4)
    save(nl, nl_out, 5)
    arrived(1)
    collect(2)

    def up_step(n2, _):
        weight = panel(w, 1, n2)
        q, p = n2 // 3, n2 % 3
        rows = vecs[8:12, :]
        bias = jnp.where(q == 0, rows[0:1], jnp.where(q == 1, rows[1:2], jnp.where(q == 2, rows[2:3], rows[3:4])))
        bias = jnp.where(p == 0, bias[:, :256], jnp.where(p == 1, bias[:, 256:512], bias[:, 512:]))
        for half in range(4):
            part = pl.ds(128 * half, 128)
            pre = mm(nl[part, :], weight) + bias
            upper = 0.5 + 0.5 * lax.erf(pre * 0.7071067811865476)
            act[n2, part, :] = (pre * upper).astype(bf)
            gp[n2, part, :] = upper + pre * (jnp.exp(-0.5 * pre * pre) * 0.3989422804014327)
        return 0

    lax.fori_loop(0, 12, up_step, 0)
    save(act, act_out, 6)
    save(gp, gp_out, 7)
    arrived(2)

    def down_step(y, _):
        hidden = jnp.concatenate([act[3 * y], act[3 * y + 1], act[3 * y + 2]], axis=1)
        for p in range(3):
            weight = jnp.concatenate([down_panel(w, 2 * p, y), down_panel(w, 2 * p + 1, y)], axis=1)
            cols = slice(256 * p, 256 * p + 256)
            resid[:, cols] = resid[:, cols] + mm(hidden, weight)
        return 0

    lax.fori_loop(0, RING, down_step, 0)

    def norm_two_step(s, _):
        rows = pl.ds(pl.multiple_of(s * SEQ, SEQ), SEQ)
        value = resid[rows, :]
        centred = value - jnp.mean(value, axis=1, keepdims=True)
        inverse = lax.rsqrt(jnp.mean(centred * centred, axis=1, keepdims=True) + norm_eps)
        scaled = centred * inverse
        h2[rows, :] = scaled
        inv[1, rows, :] = jnp.broadcast_to(inverse, (SEQ, 128))
        state = scaled * vecs[1:2, :] + vecs[7:8, :]
        live = lax.broadcasted_iota(jnp.int32, (SEQ, 768), 0) < lens_ref[s % 2, s // 2]
        mean_vec = jnp.sum(jnp.where(live, state, 0.0), axis=0, keepdims=True) / lens_ref[s % 2, s // 2].astype(f32)
        r = lax.rsqrt(jnp.sum(mean_vec * mean_vec, axis=1, keepdims=True) + pool_eps)
        pooled[s] = mean_vec * r
        rnorm[s] = jnp.broadcast_to(r, (1, 768))
        return 0

    lax.fori_loop(0, 8, norm_two_step, 0)
    save(h2, h2_out, 8)
    save(inv, inv_out, 9)

    sources = jnp.concatenate([pooled[2 * i] for i in range(4)], axis=0)
    targets = jnp.concatenate([pooled[2 * i + 1] for i in range(4)], axis=0)
    first = core == 0
    pad = jnp.zeros((4, 768), f32)
    pool_own[0] = jnp.concatenate([jnp.where(first, targets, sources), pad], axis=0)
    swap = pltpu.make_async_remote_copy(
        src_ref=pool_own.at[0], dst_ref=pool_swap, send_sem=swap_sem.at[0], recv_sem=swap_sem.at[1],
        device_id=device_at(spot, 1 - core), device_id_type=MESH,
    )
    swap.start()
    swap.wait()
    got = pool_swap[0:4, :]
    kind = jnp.concatenate(
        [jnp.where(first, sources, got), jnp.where(first, got, targets)], axis=0
    )
    q = Gather(pool_all, pool_size, pool_send, pool_recv, spot, core, (1, 2, 0))
    for o in range(3):
        unit = jnp.concatenate([kind[:, 256 * o : 256 * o + 128], kind[:, 256 * o + 128 : 256 * o + 256]], axis=0)
        here = (pl.ds(spot[1], 1), pl.ds(spot[2], 1), pl.ds(spot[0], 1))
        pool_all[(0, core, o) + here] = unit.reshape(1, 1, 1, 16, 128)
    for o in range(3):
        q.begin(0, o, None)
    for o in range(3):
        q.planes(0, o)
        q.spread(0, o, True)
    for o in range(3):
        q.collect(0, o)
    for o in range(3):
        q.shared_done(0, o)

    for k, out in ((0, left3), (1, right3)):
        for o in range(3):
            for h in range(2):
                block = pool_all[0, k, o, :, :, :, 8 * h : 8 * h + 8, :].reshape(512, 128)
                high, low = split_low(block)
                at = 256 * o + 128 * h
                parts = (high, high, low) if k == 0 else (high, low, high)
                for i in range(3):
                    out[:, 768 * i + at : 768 * i + at + 128] = parts[i]
    pair_row = lax.broadcasted_iota(jnp.int32, (512, 256), 0)
    pair_col = lax.broadcasted_iota(jnp.int32, (512, 256), 1)
    names = lax.broadcasted_iota(jnp.int32, (16, 512), 0).astype(f32)
    member = (names == group_row).astype(bf)

    def column_lse(rows3, cols3, into):
        for p in range(2):
            cut = slice(256 * p, 256 * p + 256)
            scores = logit_scale * mm_nt(rows3[...], cols3[cut, :])
            scores = scores - jnp.where(pair_row == pair_col + 256 * p, logit_scale * margin, 0.0)
            alike = mm_tn(member, member[:, cut]) > 0.5
            scores = jnp.where(alike, scores, far_low)
            peak = jnp.max(scores, axis=0, keepdims=True)
            total = jnp.sum(jnp.exp(scores - peak), axis=0, keepdims=True)
            stats[into : into + 1, cut] = peak + jnp.log(total)

    column_lse(left3, right3, 0)
    column_lse(right3, left3, 1)
    chip = (spot[1] * RING + spot[2]) * RING + spot[0]
    mine = pl.ds(pl.multiple_of(chip * 8, 8), 8)
    weight = 1.0 / 1024.0
    at_row = lax.broadcasted_iota(jnp.int32, (8, 512), 0) + chip * 8
    at_col = lax.broadcasted_iota(jnp.int32, (8, 512), 1)
    own_pair = at_row == at_col
    pick = (lax.broadcasted_iota(jnp.int32, (8, 512), 1) == at_row).astype(bf)
    own_member = mm_nt(pick, member)
    alike = mm(own_member.astype(bf), member) > 0.5
    grads = []
    terms = []
    for k, (rows3, cols3) in enumerate(((left3, right3), (right3, left3))):
        block = pool_all[0, k, :, pl.ds(spot[1], 1), pl.ds(spot[2], 1), pl.ds(spot[0], 1)]
        cut = [block[o, 0, 0, 0, 8 * h : 8 * h + 8, :] for o in range(3) for h in range(2)]
        own8 = jnp.concatenate(cut, axis=1)
        high, low = split_low(own8)
        parts = (high, high, low) if k == 0 else (high, low, high)
        scores = logit_scale * mm_nt(jnp.concatenate(parts, axis=1), cols3[...])
        scores = scores - jnp.where(own_pair, logit_scale * margin, 0.0)
        diagonal = jnp.sum(jnp.where(own_pair, scores, 0.0), axis=1, keepdims=True)
        scores = jnp.where(alike, scores, far_low)
        peak = jnp.max(scores, axis=1, keepdims=True)
        lse = peak + jnp.log(jnp.sum(jnp.exp(scores - peak), axis=1, keepdims=True))
        other = stats[k : k + 1, :]
        mix = weight * (jnp.exp(scores - lse) + jnp.exp(scores - other))
        mix = mix - jnp.where(own_pair, 2.0 * weight, 0.0)
        mix_high, mix_low = split_low(mix)
        high_at, low_at = (0, 768) if k == 0 else (0, 1536)
        high_cols, low_cols = cols3[:, high_at : high_at + 768], cols3[:, low_at : low_at + 768]
        grad = mm(mix_high, high_cols) + mm(mix_high, low_cols) + mm(mix_low, high_cols)
        grads.append(logit_scale * jnp.where(first, grad[0:4], grad[4:8]))
        terms.append(jnp.where(first, (lse - diagonal)[0:4], (lse - diagonal)[4:8]))
    row = lax.broadcasted_iota(jnp.int32, (4, 128), 0)
    lane = lax.broadcasted_iota(jnp.int32, (4, 128), 1)
    rows = [jnp.sum(jnp.where(row == lane, terms[k], 0.0), axis=0, keepdims=True) for k in range(2)]
    loss_out[...] = jnp.concatenate(rows + [jnp.zeros((6, 128), f32)], axis=0)
    for s in range(8):
        d_row = grads[s % 2][s // 2 : s // 2 + 1, :]
        row = pooled[s]
        inner = jnp.sum(row * d_row, axis=1, keepdims=True)
        dpool_out[s] = rnorm[s] * (d_row - row * inner) / lens_ref[s % 2, s // 2].astype(f32)
    g.drain(3)
    q.drain(1)
    for copy in sent:
        copy.wait_send()
    for sem, ref in ((ids_sem, ids_in), (rows_sem, rows_in)):
        others = ref.at[pl.ds(0, 127)]
        pltpu.make_async_copy(others, others, sem.at[0]).wait()
    for copy in saves:
        copy.wait()


def forward_pass(lengths, groups, ids, w_qkv, w_out, w_up, w_down, gains, biases, table):
    bf, f32 = jnp.bfloat16, jnp.float32
    shapes = [
        ((3, 2, 3, RING, RING, RING, UNIT, 128), bf),
        ((16, 768), f32),
        ((512, 768), f32),
        ((512, 768), f32),
        ((2, 512, 128), f32),
        ((512, 768), bf),
        ((12, 512, 256), bf),
        ((12, 512, 256), f32),
        ((9, 512, 256), bf),
        ((8, 3, SEQ, 256), f32),
        ((3, 512, 256), bf),
        ((512, 768), bf),
        ((8, 1, 768), f32),
        ((8, 128), f32),
        ((512, 128), f32),
        ((8, 1024), f32),
    ]
    anywhere = pl.BlockSpec(memory_space=pl.ANY)
    vmem = pl.BlockSpec(memory_space=pltpu.VMEM)
    dma = pltpu.SemaphoreType.DMA
    return pl.pallas_call(
        forward_kernel,
        out_shape=[jax.ShapeDtypeStruct(*s) for s in shapes],
        in_specs=[pl.BlockSpec(memory_space=pltpu.SMEM)] * 2 + [vmem] * 7 + [anywhere],
        out_specs=[anywhere] * 12 + [vmem] * 4,
        scratch_shapes=[
            pltpu.VMEM(*shapes[0]),
            pltpu.VMEM(*shapes[1]),
            pltpu.VMEM((RING, RING, 16, 128), bf),
            *[pltpu.VMEM(*s) for s in shapes[2:12]],
            pltpu.VMEM((512, 768), f32),
            pltpu.VMEM((8, 1, 768), f32),
            pltpu.VMEM((8, 1, 768), f32),
            pltpu.VMEM((1, 8, 768), f32),
            pltpu.VMEM((8, 768), f32),
            pltpu.VMEM((1, 2, 3, RING, RING, RING, 16, 128), f32),
            pltpu.VMEM((512, 2304), bf),
            pltpu.VMEM((512, 2304), bf),
            pltpu.VMEM((8, 512), f32),
            pltpu.VMEM((3, 3, 1, 1, 1, UNIT, 128), bf),
            pltpu.VMEM((8, UNIT, 128), f32),
            pltpu.VMEM((8, UNIT, 128), f32),
            pltpu.VMEM((2, 3, 24, 128), f32),
            pltpu.VMEM((3, 24, 128), f32),
            pltpu.VMEM((4096, 768), bf),
            pltpu.VMEM((128, 1, 128), f32),
            pltpu.VMEM((128, 1, 128), f32),
            pltpu.VMEM((128, 128), f32),
            pltpu.VMEM((1024, 128), f32),
            pltpu.VMEM((128, 16, 384), bf),
            pltpu.VMEM((128, 16, 384), bf),
            pltpu.VMEM((1024, 768), bf),
            pltpu.VMEM((15, UNIT, 128), bf),
            pltpu.VMEM((15, 16, 128), f32),
            dma((3, 3, 9)),
            dma((3, 3, 9)),
            dma((3, 3)),
            dma((1, 3, 9)),
            dma((1, 3, 9)),
            dma((6,)),
            dma((6,)),
            dma((2,)),
            dma((3, 2, 3)),
            dma((11,)),
            dma((8,)),
            dma((8,)),
            dma((2,)),
            dma((2,)),
            dma((1,)),
        ],
        compiler_params=pltpu.CompilerParams(
            collective_id=1, has_side_effects=True, vmem_limit_bytes=62 * 1024 * 1024
        ),
        name="forward_pass",
    )(lengths, groups, ids, w_qkv, w_out, w_up, w_down, gains, biases, table)


class Reduce:
    def __init__(self, parts, bufs, plane, out, send_sem, recv_sem, spot, core):
        self.parts, self.bufs, self.plane_in, self.out = parts, bufs, plane, out
        self.send_sem, self.recv_sem = send_sem, recv_sem
        self.spot, self.core = spot, core
        self.sent = []

    def copy(self, src, dst, r, o, event, there):
        copy = pltpu.make_async_remote_copy(
            src_ref=src,
            dst_ref=dst,
            send_sem=self.send_sem.at[r, o, event],
            recv_sem=self.recv_sem.at[r, o, event],
            device_id=device_at(there, self.core),
            device_id_type=MESH,
        )
        copy.start()
        return copy

    def landed(self, dst, r, o, event):
        pltpu.make_async_copy(dst, dst, self.recv_sem.at[r, o, event]).wait()

    def spans(self, o, at, half=None):
        ring, first, second = ORDERS[o]
        return {ring: (at, 1), first: (0, RING) if half is None else (2 * half, 2), second: (0, RING)}

    def mine(self, r, o, spans):
        return block_of(self.parts, r, self.core, o, spans)

    def slot(self, r, o, which):
        return self.bufs[o * 2].at[r, which] if which < 3 else self.bufs[o * 2 + 1].at[0, which - 3]

    def add_into(self, into, others):
        sizes = into.shape[:3]

        def one(i, _):
            at = (i // sizes[1], i % sizes[1])
            if len(others) == 1:
                into[at] = into[at] + others[0][at]
            else:
                value = into[at].astype(jnp.float32)
                for other in others:
                    value = value + other[at].astype(jnp.float32)
                into[at] = value.astype(jnp.bfloat16)
            return 0

        lax.fori_loop(0, sizes[0] * sizes[1], one, 0)

    def first(self, r, o):
        d = ORDERS[o][0]
        if r > 0:
            for by in (1, 3, 2):
                there = moved(self.spot, d, by)
                src = self.mine(r, o, self.spans(o, there[d]))
                self.sent.append(self.copy(src, self.slot(r, o, by - 1), r, o, by - 1, there))
            return
        across = (self.spot[d] + 2) % RING
        for half, by in ((0, 1), (1, -1)):
            src = self.mine(r, o, self.spans(o, across, half))
            self.sent.append(self.copy(src, self.slot(r, o, 3 + half), r, o, 2 + 3 * half, moved(self.spot, d, by)))

    def second(self, r, o):
        d = ORDERS[o][0]
        for half, by in ((0, 1), (1, -1)):
            at = (self.spot[d] + by) % RING
            view = self.slot(r, o, 3 + half)
            self.landed(view, r, o, 2 + 3 * half)
            self.add_into(self.mine(r, o, self.spans(o, at, half)), [view])
            src = self.mine(r, o, self.spans(o, at))
            self.sent.append(self.copy(src, self.slot(r, o, half), r, o, half, moved(self.spot, d, by)))

    def third(self, r, o):
        ring, first, second = ORDERS[o]
        views = [self.slot(r, o, k) for k in range(3 if r > 0 else 2)]
        for k, view in enumerate(views):
            self.landed(view, r, o, k)
        self.add_into(self.mine(r, o, self.spans(o, self.spot[ring])), views)

        def one(k, _):
            there = moved(moved(self.spot, first, k % RING), second, k // RING)
            src = self.mine(r, o, {d: (there[d], 1) for d in range(3)})
            self.copy(src, self.plane_in.at[r, o, pl.ds(k, 1), pl.ds(0, 1), pl.ds(0, 1)], r, o, 4, there)
            return 0

        lax.fori_loop(1, 16, one, 0)

    def fourth(self, r, o):
        others = self.plane_in.at[r, o, pl.ds(1, 15)]
        self.landed(others, r, o, 4)
        here = self.mine(r, o, {d: (self.spot[d], 1) for d in range(3)})
        total = here[0, 0, 0].astype(jnp.float32)
        for k in range(1, 16):
            total = total + self.plane_in[r, o, k, 0, 0].astype(jnp.float32)
        self.out[r, o] = total

    def drain(self):
        for r in range(3):
            for o in range(3):
                others = self.plane_in.at[r, o, pl.ds(1, 15)]
                pltpu.make_async_copy(others, others, self.send_sem.at[r, o, 4]).wait()
        for copy in self.sent:
            copy.wait_send()


def reduce_buffers(rounds):
    bufs = []
    for o in range(3):
        ring, first, second = ORDERS[o]
        sizes = [RING] * 3
        sizes[ring] = 1
        half = list(sizes)
        half[first] = 2
        bufs.append(pltpu.VMEM((rounds, 3, *sizes, UNIT, 128), jnp.bfloat16))
        bufs.append(pltpu.VMEM((1, 2, *half, UNIT, 128), jnp.bfloat16))
    return bufs


def norm_back(grad, scaled, inverse, gain):
    e = grad * gain
    mean_e = jnp.mean(e, axis=1, keepdims=True)
    mean_eh = jnp.mean(e * scaled, axis=1, keepdims=True)
    return inverse * (e - mean_e - scaled * mean_eh)


def backward_kernel(
    lens_ref, vec_ref, dpool_ref, x_ref, slot_ref,
    w_in, h1_in, h2_in, inv_in, nl_in, act_in, gp_in, qkv_in, prob_in, ctx_in,
    token_out, rows_in, qkv_out, out_out, up_out, down_out, vec_out,
    w, h1, h2, inv, nl, act, gp, qkv, prob, ctx, parts, d2d, d_res, d_low, turned, dvec, vec_slots, red_out, near_out, near_in, half_in, rows_out, *rest,
):
    bufs, plane_in, rest = rest[:6], rest[6], rest[7:]
    send_sem, recv_sem, swap_send, swap_recv, free_sem, vec_send, vec_recv, load_sem, gp_sem, w_sem, near_send, near_recv, rows_sem = rest
    me = lax.axis_index("wide") * 8 + lax.axis_index("narrow")
    spot, core = where_am_i()
    bf, f32 = jnp.bfloat16, jnp.float32

    def load(src, dst, at):
        copy = pltpu.make_async_copy(src, dst, load_sem.at[at])
        copy.start()
        return copy

    def load_w(r, at):
        copy = pltpu.make_async_copy(w_in.at[r], w.at[at], w_sem.at[r])
        copy.start()
        return copy

    def load_gp(y, at):
        return pltpu.make_async_copy(gp_in.at[pl.ds(3 * y, 3)], gp.at[at], gp_sem.at[at])

    get_h2, get_inv = load(h2_in, h2, 0), load(inv_in, inv, 1)
    get_act = load(act_in, act, 2)
    get_w2 = load_w(2, 0)
    load_gp(0, 0).start()
    load_gp(1, 1).start()
    get_nl = load(nl_in, nl, 3)
    get_w1 = load_w(1, 1)
    get_h1, get_ctx = load(h1_in, h1, 4), load(ctx_in, ctx, 5)
    get_qkv, get_prob = load(qkv_in, qkv, 6), load(prob_in, prob, 7)
    all_here = greet_all()
    red = Reduce(parts, bufs, plane_in, red_out, send_sem, recv_sem, spot, core)
    swaps = {}

    def give(r):
        if r == 0:
            pl.semaphore_wait(free_sem, 1)
        for o in range(3):
            copy = pltpu.make_async_remote_copy(
                src_ref=parts.at[r, 1 - core, o], dst_ref=d2d.at[r % 2, o],
                send_sem=swap_send.at[r, o], recv_sem=swap_recv.at[r, o],
                device_id=device_at(spot, 1 - core), device_id_type=MESH,
            )
            copy.start()
            red.sent.append(copy)

    def take(r):
        for o in range(3):
            view = d2d.at[r % 2, o]
            pltpu.make_async_copy(view, view, swap_recv.at[r, o]).wait()
            red.add_into(parts.at[r, core, o], [view])
            red.first(r, o)
        if r == 2:
            pl.semaphore_signal(free_sem, inc=1, device_id=device_at(spot, 1 - core), device_id_type=MESH)

    def second(r):
        for o in range(3):
            red.second(r, o)

    def third(r):
        for o in range(3):
            red.third(r, o)

    def fourth(r):
        for o in range(3):
            red.fourth(r, o)

    dvec[0] = jnp.zeros((16, 768), f32)

    def add_vec(row, value):
        dvec[0, row : row + 1, :] = dvec[0, row : row + 1, :] + value

    def total(value):
        return jnp.sum(value, axis=0, keepdims=True)

    get_h2.wait()
    get_inv.wait()

    def norm_two_step(s, _):
        rows = pl.ds(pl.multiple_of(s * SEQ, SEQ), SEQ)
        live = lax.broadcasted_iota(jnp.int32, (SEQ, 768), 0) < lens_ref[s % 2, s // 2]
        grad = jnp.where(live, jnp.broadcast_to(dpool_ref[s], (SEQ, 768)), 0.0)
        scaled = h2[rows, :]
        inverse = inv[1, rows, 0:1]
        back = norm_back(grad, scaled, inverse, vec_ref[1:2, :])
        low = back.astype(bf)
        d_res[rows, :] = back
        d_low[rows, :] = low
        add_vec(1, total(grad * scaled))
        add_vec(7, total(grad))
        add_vec(6, total(low.astype(f32)))
        return 0

    lax.fori_loop(0, 8, norm_two_step, 0)
    get_act.wait()

    def down_step(y, _):
        hidden = jnp.concatenate([act[3 * y], act[3 * y + 1], act[3 * y + 2]], axis=1)
        turned[...] = hidden.T
        for p in range(3):
            block = mm(turned[...], d_low[:, 256 * p : 256 * p + 256]).astype(bf)
            for k in range(2):
                cb = 2 * p + k
                for z in range(RING):
                    for x in range(RING):
                        at = UNIT * (RING * z + x)
                        parts[2, cb // 3, cb % 3, x, y, z] = block[at : at + UNIT, 128 * k : 128 * k + 128]
        return 0

    lax.fori_loop(0, RING, down_step, 0)
    all_here()
    give(2)
    get_w2.wait()

    def pre_step(y, _):
        at = y % 2
        load_gp(y, at).wait()
        columns = [
            jnp.concatenate([w[0, cb // 3, cb % 3, x, y, z] for z in range(RING) for x in range(RING)], axis=0)
            for cb in range(6)
        ]
        weight = jnp.concatenate(columns, axis=1)
        for j in range(3):
            grad = mm_nt(d_low[...], weight[256 * j : 256 * j + 256, :]) * gp[at, j]
            low = grad.astype(bf)
            act[3 * y + j] = low
            cut = slice(256 * j, 256 * j + 256)
            dvec[0, pl.ds(8 + y, 1), cut] = total(low.astype(f32))

        @pl.when(y < 2)
        def _():
            load_gp(y + 2, at).start()

        return 0

    lax.fori_loop(0, RING, pre_step, 0)
    get_w0 = load_w(0, 0)
    take(2)
    get_nl.wait()
    turned_nl = nl[...].T
    turned[:, :] = turned_nl

    def up_step(n2, _):
        block = mm(turned[...], act[n2]).astype(bf)
        c, o, x = n2 // 6, n2 // 2 % 3, n2 % 2 * 2
        for k in range(2):
            parts[1, c, o, x + k] = block[:, 128 * k : 128 * k + 128].reshape(RING, RING, UNIT, 128)
        return 0

    lax.fori_loop(0, 12, up_step, 0)
    give(1)
    get_w1.wait()

    def six_blocks(at, n):
        blocks = []
        for k in range(6):
            m = n + k
            blocks.append(w[at, m // 12, m // 4 % 3, m % 4].reshape(768, 128))
        return jnp.concatenate(blocks, axis=1)

    def up_back_step(t, _):
        low = jnp.concatenate([act[3 * t], act[3 * t + 1], act[3 * t + 2]], axis=1)
        weight = six_blocks(1, 6 * t)
        for p in range(3):
            cut = slice(256 * p, 256 * p + 256)
            d_res[:, cut] = d_res[:, cut] + mm_nt(low, weight[cut, :])
        return 0

    lax.fori_loop(0, RING, up_back_step, 0)
    take(1)
    get_h1.wait()

    def norm_one_step(s, _):
        rows = pl.ds(pl.multiple_of(s * SEQ, SEQ), SEQ)
        grad, scaled = d_res[rows, :], h1[rows, :]
        back = norm_back(grad, scaled, inv[0, rows, 0:1], vec_ref[0:1, :])
        low = back.astype(bf)
        d_res[rows, :] = back
        d_low[rows, :] = low
        add_vec(0, total(grad * scaled))
        add_vec(5, total(grad))
        add_vec(4, total(low.astype(f32)))
        return 0

    lax.fori_loop(0, 8, norm_one_step, 0)
    get_ctx.wait()
    turned[...] = jnp.concatenate([ctx[0], ctx[1], ctx[2]], axis=1).T
    get_w0.wait()
    weight = six_blocks(0, 18)
    for p in range(3):
        cut = slice(256 * p, 256 * p + 256)
        block = mm(turned[...], d_low[:, cut]).astype(bf)
        for k in range(2):
            n = 18 + 2 * p + k
            parts[0, n // 12, n // 4 % 3, n % 4] = block[:, 128 * k : 128 * k + 128].reshape(RING, RING, UNIT, 128)
        ctx[p] = mm_nt(d_low[...], weight[cut, :]).astype(bf)
    third(2)
    get_qkv.wait()
    get_prob.wait()
    mask = head_mask()

    def attend_back(s, _):
        rows = pl.ds(pl.multiple_of(s * SEQ, SEQ), SEQ)
        for p in range(3):
            query, key_part, value = qkv[p, rows, :], qkv[3 + p, rows, :], qkv[6 + p, rows, :]
            wide_grad = spread_heads(ctx[p, rows, :], mask)
            probs = prob[s, p]
            d_value = mm(probs.astype(bf), wide_grad)
            d_probs = mm_nt(value, wide_grad)
            centre = jnp.sum(probs * d_probs, axis=0, keepdims=True)
            d_scores = (probs * (d_probs - centre)).astype(bf)
            d_query = gather_heads(mm_tn(d_scores, key_part), mask) * 0.125
            d_key = mm(d_scores, spread_heads(query, mask)) * 0.125
            low_query, low_value = d_query.astype(bf), d_value.astype(bf)
            qkv[p, rows, :] = low_query
            qkv[3 + p, rows, :] = d_key.astype(bf)
            qkv[6 + p, rows, :] = low_value
            cut = slice(256 * p, 256 * p + 256)
            dvec[0, 2:3, cut] = dvec[0, 2:3, cut] + total(low_query.astype(f32))
            dvec[0, 3:4, cut] = dvec[0, 3:4, cut] + total(low_value.astype(f32))
        return 0

    lax.fori_loop(0, 8, attend_back, 0)
    vec_sent = []

    def vec_push(event, src, there, c):
        copy = pltpu.make_async_remote_copy(
            src_ref=src, dst_ref=vec_slots.at[event], send_sem=vec_send.at[event], recv_sem=vec_recv.at[event],
            device_id=device_at(there, c), device_id_type=MESH,
        )
        copy.start()
        vec_sent.append(copy)

    def vec_landed(event):
        ref = vec_slots.at[event]
        pltpu.make_async_copy(ref, ref, vec_recv.at[event]).wait()

    def vec_start(d):
        for by in (1, 2, 3):
            vec_push(3 * d + by, dvec.at[d + 1], moved(spot, d, by), core)

    def vec_add(d):
        for by in (1, 2, 3):
            vec_landed(3 * d + by)
        sides = vec_slots[1 + 3 * d] + vec_slots[3 + 3 * d]
        dvec[d + 2] = (dvec[d + 1] + sides) + vec_slots[2 + 3 * d]

    vec_push(0, dvec.at[0], spot, 1 - core)
    third(1)

    def input_step(t, _):
        low = jnp.concatenate([qkv[3 * t], qkv[3 * t + 1], qkv[3 * t + 2]], axis=1)
        weight = six_blocks(0, 6 * t)
        for p in range(3):
            cut = slice(256 * p, 256 * p + 256)
            d_res[:, cut] = d_res[:, cut] + mm_nt(low, weight[cut, :])
        return 0

    lax.fori_loop(0, 3, input_step, 0)
    token_copy = pltpu.make_async_copy(d_res, token_out, load_sem.at[8])
    token_copy.start()
    d_low[...] = d_res[...].astype(bf)
    slots_hot = slot_hot(slot_ref)
    for q in range(4):
        rows = mm_tn(slots_hot[:, 256 * q : 256 * q + 256], d_low[...])
        rows_out[32 * q : 32 * q + 32] = pack_rows(rows)

    def hand_back(k, _):
        there = (me + k) % 128
        pltpu.make_async_remote_copy(
            src_ref=rows_out.at[there], dst_ref=rows_in.at[(128 - k) % 128],
            send_sem=rows_sem.at[0], recv_sem=rows_sem.at[1],
            device_id=(there // 8, there % 8), device_id_type=MESH,
        ).start()
        return 0

    lax.fori_loop(1, 128, hand_back, 0)
    keep_rows = pltpu.make_async_copy(rows_out.at[me], rows_in.at[0], load_sem.at[9])
    keep_rows.start()
    turned[...] = x_ref[...].T

    def qkv_step(n2, _):
        block = mm(turned[...], qkv[n2]).astype(bf)
        c, o, x = n2 // 6, n2 // 2 % 3, n2 % 2 * 2
        for k in range(2):
            parts[0, c, o, x + k] = block[:, 128 * k : 128 * k + 128].reshape(RING, RING, UNIT, 128)
        return 0

    lax.fori_loop(0, 9, qkv_step, 0)
    give(0)
    vec_landed(0)
    dvec[1] = dvec[0] + vec_slots[0]
    vec_start(0)
    fourth(2)
    take(0)
    vec_add(0)
    vec_start(1)
    fourth(1)
    second(0)
    vec_add(1)
    vec_start(2)
    third(0)
    vec_add(2)
    vec_out[...] = dvec[4]
    fourth(0)

    mine = spot[0] * 2 + core
    for j in range(8):
        for r in range(2):
            for o in range(3):
                at = 6 * (3 * r + o)
                near_out[j, at : at + 6, :] = red_out[r, o, 6 * j : 6 * j + 6, :]
    for k in range(1, 8):
        there = (mine + k) % 8
        copy = pltpu.make_async_remote_copy(
            src_ref=near_out.at[there], dst_ref=near_in.at[mine], send_sem=near_send.at[k], recv_sem=near_recv.at[k],
            device_id=(lax.axis_index("wide"), there), device_id_type=MESH,
        )
        copy.start()
        vec_sent.append(copy)
    theirs = pl.ds(pl.multiple_of(24 * (1 - core), 8), 24)
    copy = pltpu.make_async_remote_copy(
        src_ref=red_out.at[2, :, theirs], dst_ref=half_in, send_sem=near_send.at[0], recv_sem=near_recv.at[0],
        device_id=device_at(spot, 1 - core), device_id_type=MESH,
    )
    copy.start()
    vec_sent.append(copy)
    near_in[mine] = near_out[mine]
    for k in range(1, 8):
        ref = near_in.at[(mine + 8 - k) % 8]
        pltpu.make_async_copy(ref, ref, near_recv.at[k]).wait()
    pltpu.make_async_copy(half_in, half_in, near_recv.at[0]).wait()
    for c in range(2):
        for o in range(3):
            for x in range(RING):
                n, j = c * 12 + o * 4 + x, 2 * x + c
                block = near_in[j, 6 * o : 6 * o + 6, :]
                if n < 18:
                    qkv_out[:, 128 * n : 128 * n + 128] = block
                else:
                    out_out[:, 128 * (n - 18) : 128 * (n - 18) + 128] = block
                up_out[:, 128 * n : 128 * n + 128] = near_in[j, 18 + 6 * o : 24 + 6 * o, :]
    ours = pl.ds(pl.multiple_of(24 * core, 8), 24)
    for o in range(3):
        a, b = red_out[2, o, ours, :], half_in[o]
        down_out[:, 128 * o : 128 * o + 128] = jnp.where(core == 0, a, b)
        down_out[:, 384 + 128 * o : 512 + 128 * o] = jnp.where(core == 0, b, a)
    others = rows_in.at[pl.ds(0, 127)]
    pltpu.make_async_copy(others, others, rows_sem.at[1]).wait()
    pltpu.make_async_copy(others, others, rows_sem.at[0]).wait()
    token_copy.wait()
    keep_rows.wait()
    red.drain()
    for copy in vec_sent:
        copy.wait_send()


def backward_pass(lens, vectors, d_pool, x, slots, w, h1, h2, inv, nl, act, gp, qkv, prob, ctx):
    bf, f32 = jnp.bfloat16, jnp.float32
    anywhere = pl.BlockSpec(memory_space=pl.ANY)
    vmem = pl.BlockSpec(memory_space=pltpu.VMEM)
    dma = pltpu.SemaphoreType.DMA
    scratch = [
        pltpu.VMEM((2, *w.shape[1:]), bf),
        pltpu.VMEM(h1.shape, f32),
        pltpu.VMEM(h2.shape, f32),
        pltpu.VMEM(inv.shape, f32),
        pltpu.VMEM(nl.shape, bf),
        pltpu.VMEM(act.shape, bf),
        pltpu.VMEM((2, 3, 512, 256), f32),
        pltpu.VMEM(qkv.shape, bf),
        pltpu.VMEM(prob.shape, f32),
        pltpu.VMEM(ctx.shape, bf),
        pltpu.VMEM(w.shape, bf),
        pltpu.VMEM((2, *w.shape[2:]), bf),
        pltpu.VMEM((512, 768), f32),
        pltpu.VMEM((512, 768), bf),
        pltpu.VMEM((768, 512), bf),
        pltpu.VMEM((5, 16, 768), f32),
        pltpu.VMEM((10, 16, 768), f32),
        pltpu.VMEM((3, 3, UNIT, 128), f32),
        pltpu.VMEM((8, 40, 128), f32),
        pltpu.VMEM((8, 40, 128), f32),
        pltpu.VMEM((3, 24, 128), f32),
        pltpu.VMEM((128, 16, 384), bf),
        *reduce_buffers(3),
        pltpu.VMEM((3, 3, 16, 1, 1, UNIT, 128), bf),
        dma((3, 3, 6)),
        dma((3, 3, 6)),
        dma((3, 3)),
        dma((3, 3)),
        pltpu.SemaphoreType.REGULAR,
        dma((10,)),
        dma((10,)),
        dma((10,)),
        dma((2,)),
        dma((3,)),
        dma((8,)),
        dma((8,)),
        dma((2,)),
    ]
    shapes = [
        ((512, 768), f32),
        ((128, 16, 384), bf),
        ((6, 2304), f32),
        ((6, 768), f32),
        ((6, 3072), f32),
        ((24, 768), f32),
        ((16, 768), f32),
    ]
    return pl.pallas_call(
        backward_kernel,
        out_shape=[jax.ShapeDtypeStruct(*s) for s in shapes],
        in_specs=[pl.BlockSpec(memory_space=pltpu.SMEM)] + [vmem] * 4 + [anywhere] * 10,
        out_specs=[anywhere] * 2 + [vmem] * 5,
        scratch_shapes=scratch,
        compiler_params=pltpu.CompilerParams(
            collective_id=2, has_side_effects=True, vmem_limit_bytes=64 * 1024 * 1024 - 65536
        ),
        name="backward_pass",
    )(lens, vectors, d_pool, x, slots, w, h1, h2, inv, nl, act, gp, qkv, prob, ctx)


TABLE_STEP = 560


def table_kernel(
    rows_ref, asked_ref, qkv_ref, out_ref, up_ref, down_ref, vec_ref, loss_ref, token_ref,
    table_out, token_out, qkv_out, proj_out, up_out, down_out, gain_out, bias_out, loss_out, rows,
):
    at = pl.program_id(0)
    token_out[...] = token_ref[...]

    @pl.when(at == 0)
    def _():
        for q in range(8):
            rows[128 * q : 128 * q + 128, :] = unpack_rows(rows_ref[16 * q : 16 * q + 16])
        for i in range(6):
            qkv_out[i] = qkv_ref[i : i + 1, :]
            proj_out[i] = out_ref[i : i + 1, :]
            up_out[i] = up_ref[i : i + 1, :]
        down_out[0] = down_ref[...]
        me = lax.axis_index("wide") * 8 + lax.axis_index("narrow")
        turned = pltpu.roll(vec_ref[...], 768 - 6 * me, 1)[:, :128]
        gain_out[0] = turned[0:2, 0:6]
        across = turned.T
        for i in range(6):
            bias_out[i] = across[i : i + 1, 2:12]
        loss_out[...] = loss_ref[0:2, 0:4]

    name = (lax.broadcasted_iota(jnp.int32, (TABLE_STEP, 1024), 0) + at * TABLE_STEP).astype(jnp.float32)
    table_out[...] = mm((name == asked_ref[0:1, :]).astype(jnp.bfloat16), rows[...])


def table_sums(rows, asked, d_qkv, d_out, d_up, d_down, vectors, loss, tokens, table_rows):
    f32 = jnp.float32
    ins = (rows, asked, d_qkv, d_out, d_up, d_down, vectors, loss)
    outs = [(6, 1, 2304), (6, 1, 768), (6, 1, 3072), (1, 24, 768), (1, 2, 6), (6, 1, 10), (2, 4)]
    steps = table_rows // TABLE_STEP
    token_step = -(-512 // steps // 8) * 8

    def whole(shape):
        return pl.BlockSpec(shape, lambda i: (0,) * len(shape))

    token_block = pl.BlockSpec((token_step, 768), lambda i: (i, 0))
    return pl.pallas_call(
        table_kernel,
        out_shape=[jax.ShapeDtypeStruct(s, f32) for s in [(table_rows, 768), (512, 768)] + outs],
        grid=(steps,),
        in_specs=[whole(v.shape) for v in ins] + [token_block],
        out_specs=[pl.BlockSpec((TABLE_STEP, 768), lambda i: (i, 0)), token_block] + [whole(s) for s in outs],
        scratch_shapes=[pltpu.VMEM((1024, 768), jnp.bfloat16)],
        compiler_params=pltpu.CompilerParams(vmem_limit_bytes=63 * 1024 * 1024),
        name="table_sums",
    )(*ins, tokens)


def shards(token_ids, lengths, groups, table, w_qkv, w_out, w_up, w_down, gains, biases):
    lens = lengths.T
    kept = forward_pass(lens, groups, token_ids, w_qkv, w_out, w_up, w_down, gains, jnp.swapaxes(biases, 1, 2), table)
    w, vecs, h1, h2, inv, nl, act, gate, qkv, prob, ctx, x, d_pool, loss_tile, slots, asked = kept
    token_grads, row_grads, d_qkv, d_out, d_up, d_down, d_vectors = backward_pass(
        lens, vecs, d_pool, x, slots, w, h1, h2, inv, nl, act, gate, qkv, prob, ctx
    )
    table_rows = table.shape[0]
    sums = table_sums(row_grads, asked, d_qkv, d_out, d_up, d_down, d_vectors, loss_tile, token_grads, table_rows)
    table_grads, token_grads, d_qkv, d_out, d_up, d_down, d_gains, d_biases, loss_terms = sums
    return (
        loss_terms.T,
        token_grads.reshape(token_ids.shape + (768,)),
        table_grads,
        jnp.swapaxes(d_qkv, 0, 1),
        jnp.swapaxes(d_out, 0, 1),
        jnp.swapaxes(d_up, 0, 1),
        d_down,
        d_gains,
        jnp.transpose(d_biases, (1, 2, 0)),
    )


def solution(mesh):
    in_specs = (
        P(("wide", "narrow"), None, None),
        P(("wide", "narrow"), None),
        P(("wide", "narrow")),
        P(("wide", "narrow"), None),
        P(None, ("wide", "narrow"), None),
        P(None, ("wide", "narrow"), None),
        P(None, ("wide", "narrow"), None),
        P(None, ("wide", "narrow"), None),
        P(None, None, ("wide", "narrow")),
        P(None, None, ("wide", "narrow")),
    )
    out_specs = (
        P(("wide", "narrow"), None),
        P(("wide", "narrow"), None, None, None),
        P(("wide", "narrow"), None),
        P(None, ("wide", "narrow"), None),
        P(None, ("wide", "narrow"), None),
        P(None, ("wide", "narrow"), None),
        P(None, ("wide", "narrow"), None),
        P(None, None, ("wide", "narrow")),
        P(None, None, ("wide", "narrow")),
    )
    return jax.shard_map(shards, mesh=mesh, in_specs=in_specs, out_specs=out_specs, check_vma=False)
```

```python
import functools

import jax
import jax.numpy as jnp
from jax import lax
from jax.experimental import pallas as pl
from jax.experimental.pallas import tpu as pltpu
from jax.sharding import PartitionSpec as P

HEAD_DIM = 64
SEQ = 64


logit_scale = 10.0
margin = 0.3
norm_eps = 1e-12
pool_eps = 1e-06
far_low = -1e30


MESH = pl.DeviceIdType.MESH
RING = 4
ORDERS = ((0, 1, 2), (1, 2, 0), (2, 0, 1))
UNIT = 48


def where_am_i():
    wide = lax.axis_index("wide")
    narrow = lax.axis_index("narrow")
    return [narrow // 2, wide // RING, wide % RING], narrow % 2


def device_at(spot, core):
    return (spot[1] * RING + spot[2], spot[0] * 2 + core)


def moved(spot, dim, by):
    there = list(spot)
    there[dim] = (spot[dim] + by) % RING
    return there


def block_of(ref, part, core, order, spans):
    return ref.at[(part, core, order) + tuple(pl.ds(*spans[d]) for d in range(3))]


class Gather:
    def __init__(self, out, fifteen, send_sem, recv_sem, spot, core, dims):
        self.out, self.send_sem, self.recv_sem = out, send_sem, recv_sem
        self.spot, self.core, self.dims = spot, core, dims
        self.fifteen = fifteen
        self.sent = []

    def block(self, r, o, spans, core):
        return self.out.at[(r, core, o) + tuple(pl.ds(*spans[d]) for d in self.dims)]

    def here(self, o):
        return {d: (self.spot[d], 1) for d in range(3)}

    def plane(self, o, at, half=None):
        first, second, ring = ORDERS[o]
        spans = {first: (0, RING) if half is None else (2 * half, 2), second: (0, RING), ring: (at, 1)}
        return spans

    def push(self, r, o, event, spans, there, core=None, src=None):
        dst = self.block(r, o, spans, self.core)
        copy = pltpu.make_async_remote_copy(
            src_ref=dst if src is None else src,
            dst_ref=dst,
            send_sem=self.send_sem.at[r, o, event],
            recv_sem=self.recv_sem.at[r, o, event],
            device_id=device_at(there, self.core if core is None else core),
            device_id_type=MESH,
        )
        copy.start()
        return copy

    def landed(self, r, o, event, spans, core=None):
        dst = self.block(r, o, spans, self.core if core is None else core)
        pltpu.make_async_copy(dst, dst, self.recv_sem.at[r, o, event]).wait()

    def begin(self, r, o, src):
        first, second, ring = ORDERS[o]
        here = self.here(o)

        def one(k, _):
            there = moved(moved(self.spot, first, k % RING), second, k // RING)
            self.push(r, o, 0, here, there, src=src)
            return 0

        lax.fori_loop(1, 16, one, 0)

    def plane_done(self, r, o, sem):
        pltpu.make_async_copy(self.fifteen, self.fifteen, sem.at[r, o, 0]).wait()

    def planes(self, r, o):
        self.plane_done(r, o, self.recv_sem)
        self.share(r, o, 5, self.plane(o, self.spot[ORDERS[o][2]]))

    def ring(self, o):
        d = ORDERS[o][2]
        v = self.spot[d]
        up, down = moved(self.spot, d, 1), moved(self.spot, d, -1)
        return v, (v - 1) % RING, (v + 1) % RING, (v + 2) % RING, up, down

    def share(self, r, o, event, spans):
        self.sent.append(self.push(r, o, event, spans, self.spot, 1 - self.core))

    def spread(self, r, o, direct=False):
        v, low, high, far, up, down = self.ring(o)
        here = self.plane(o, v)
        self.sent.append(self.push(r, o, 1, here, up))
        self.sent.append(self.push(r, o, 2, here, down))
        if direct:
            self.sent.append(self.push(r, o, 3, here, moved(self.spot, ORDERS[o][2], 2)))

    def relay(self, r, o):
        v, low, high, far, up, down = self.ring(o)
        self.landed(r, o, 1, self.plane(o, low))
        self.sent.append(self.push(r, o, 3, self.plane(o, low, 0), up))
        self.landed(r, o, 2, self.plane(o, high))
        self.sent.append(self.push(r, o, 4, self.plane(o, high, 1), down))
        self.share(r, o, 6, self.plane(o, low))
        self.share(r, o, 7, self.plane(o, high))

    def finish(self, r, o):
        v, low, high, far, up, down = self.ring(o)
        self.landed(r, o, 3, self.plane(o, far, 0))
        self.landed(r, o, 4, self.plane(o, far, 1))
        self.share(r, o, 8, self.plane(o, far))

    def collect(self, r, o):
        v, low, high, far, up, down = self.ring(o)
        for k, at in enumerate((low, high, far)):
            self.landed(r, o, 1 + k, self.plane(o, at))
            self.share(r, o, 6 + k, self.plane(o, at))

    def shared_done(self, r, o):
        v, low, high, far, up, down = self.ring(o)
        for k, at in enumerate((v, low, high, far)):
            self.landed(r, o, 5 + k, self.plane(o, at), 1 - self.core)

    def drain(self, rounds):
        for r in range(rounds):
            for o in range(3):
                self.plane_done(r, o, self.send_sem)
        for copy in self.sent:
            copy.wait_send()


def mm(a, b):
    return jnp.dot(a, b, preferred_element_type=jnp.float32)


def mm_nt(a, b):
    return lax.dot_general(a, b, (((1,), (1,)), ((), ())), preferred_element_type=jnp.float32)


def mm_tn(a, b):
    return lax.dot_general(a, b, (((0,), (0,)), ((), ())), preferred_element_type=jnp.float32)


def head_mask():
    row = lax.broadcasted_iota(jnp.int32, (256, 256), 0) // HEAD_DIM
    col = lax.broadcasted_iota(jnp.int32, (256, 256), 1) // HEAD_DIM
    return row == col


def spread_heads(part, mask):
    four = jnp.concatenate([part] * 4, axis=0)
    return jnp.where(mask, four, jnp.zeros((), four.dtype))


def gather_heads(wide_part, mask):
    kept = jnp.where(mask, wide_part, 0.0)
    return (kept[:64] + kept[64:128]) + (kept[128:192] + kept[192:])


def panel(w, r, n2):
    c, o, x = n2 // 6, n2 // 2 % 3, n2 % 2 * 2
    pair = [w[r, c, o, x + k].reshape(768, 128) for k in range(2)]
    return jnp.concatenate(pair, axis=1)


def down_panel(w, cb, y):
    c, o = cb // 3, cb % 3
    return jnp.concatenate([w[2, c, o, x, y, z] for z in range(RING) for x in range(RING)], axis=0)


def split_low(value):
    high = value.astype(jnp.bfloat16)
    return high, (value - high.astype(jnp.float32)).astype(jnp.bfloat16)


def greet_all():
    barrier = pltpu.get_barrier_semaphore()
    me = lax.axis_index("wide") * 8 + lax.axis_index("narrow")

    def hello(k, _):
        there = (me + k) % 128
        pl.semaphore_signal(barrier, inc=1, device_id=(there // 8, there % 8), device_id_type=MESH)
        return 0

    lax.fori_loop(1, 128, hello, 0)
    return lambda: pl.semaphore_wait(barrier, 127)


def pack_rows(rows):
    n = rows.shape[0] // 8
    left, right = rows[:, :384].reshape(n, 8, 384), rows[:, 384:].reshape(n, 8, 384)
    return jnp.concatenate([left, right], axis=1).astype(jnp.bfloat16)


def unpack_rows(packed):
    wide_rows = packed.astype(jnp.float32)
    rows = jnp.concatenate([wide_rows[:, :8], wide_rows[:, 8:]], axis=2)
    return rows.reshape(-1, 768).astype(jnp.bfloat16)


def digits(value):
    high = jnp.floor(value * 0.015625)
    return high.astype(jnp.bfloat16), (value - 64.0 * high).astype(jnp.bfloat16)


def token_slots(ids_ref, table_rows):
    f32, bf = jnp.float32, jnp.bfloat16
    sents = jnp.concatenate([ids_ref[s // 2, s % 2 : s % 2 + 1, :] for s in range(8)], axis=0)
    row = lax.broadcasted_iota(jnp.int32, (512, 8), 0)
    col = lax.broadcasted_iota(jnp.int32, (512, 8), 1)
    member_of = (row // SEQ == col).astype(bf)
    wide_ids = jnp.zeros((512, SEQ), f32)
    for shift in (0, 7, 14):
        digit = ((sents >> shift) & 127).astype(f32).astype(bf)
        wide_ids = wide_ids + mm(member_of, digit) * float(1 << shift)
    row = lax.broadcasted_iota(jnp.int32, (512, SEQ), 0)
    col = lax.broadcasted_iota(jnp.int32, (512, SEQ), 1)
    name = jnp.sum(jnp.where(row % SEQ == col, wide_ids, 0.0), axis=1, keepdims=True)
    owner = jnp.floor((name + 0.5) * (1.0 / table_rows))
    local = name - owner * float(table_rows) + 1.0
    lane = lax.broadcasted_iota(jnp.int32, (512, 128), 1).astype(f32)
    hot = (lane == owner).astype(bf)
    row = lax.broadcasted_iota(jnp.int32, (512, 512), 0)
    col = lax.broadcasted_iota(jnp.int32, (512, 512), 1)
    before = mm((col < row).astype(bf), hot)
    rank = jnp.sum(jnp.where(lane == owner, before, 0.0), axis=1, keepdims=True)
    high, low = digits(jnp.broadcast_to(local, (512, 128)))
    zero = jnp.zeros((), bf)
    here = lane == rank
    both = mm_tn(hot, jnp.concatenate([jnp.where(here, high, zero), jnp.where(here, low, zero)], axis=1))
    return owner * 8.0 + rank, both[:, :128] * 64.0 + both[:, 128:]


def two_digits(value, base):
    high = jnp.floor((value + 0.5) * (1.0 / base))
    return high.astype(jnp.bfloat16), (value - base * high).astype(jnp.bfloat16)


def hot_tiles(high, low_hot, first, count):
    zero = jnp.zeros((), jnp.bfloat16)
    return [jnp.where(high == (first + i).astype(jnp.bfloat16), low_hot, zero) for i in range(count)]


def lane_names(rows):
    return lax.broadcasted_iota(jnp.int32, (rows, 128), 1).astype(jnp.float32).astype(jnp.bfloat16)


def slot_hot(slot_ref):
    high, low = two_digits(slot_ref[...], 128.0)
    zero = jnp.zeros((), jnp.bfloat16)
    low_hot = jnp.where(low == lane_names(512), jnp.ones((), jnp.bfloat16), zero)
    return jnp.concatenate(hot_tiles(high, low_hot, jnp.float32(0.0), 8), axis=1)


def forward_kernel(
    lens_ref, groups_ref, ids_ref, wq_ref, wo_ref, wu_ref, wd_ref, gains_ref, bias_ref, table_in,
    w_out, vec_out, h1_out, h2_out, inv_out, nl_out, act_out, gp_out, qkv_out, prob_out, ctx_out, x_out,
    dpool_out, loss_out, slot_out, asked_out,
    w, vecs, tiles, h1, h2, inv, nl, act, gp, qkv, prob, ctx, x_ref, resid, pooled, rnorm, pool_own, pool_swap, pool_all,
    left3, right3, stats, own, sent_ref, near, halves_ref, half_got, table, ids_out, ids_in, ids, asked, rows_out, rows_in,
    row_mat, units_size, pool_size,
    send_sem, recv_sem, local_sem, pool_send, pool_recv, tile_send, tile_recv, swap_sem, save_sem,
    near_send, near_recv, ids_sem, rows_sem, table_sem,
):
    spot, core = where_am_i()
    me = lax.axis_index("wide") * 8 + lax.axis_index("narrow")
    mine = spot[0] * 2 + core
    bf, f32 = jnp.bfloat16, jnp.float32
    all_here = greet_all()
    table_rows = table_in.shape[0]
    get_table = pltpu.make_async_copy(table_in, table.at[pl.ds(0, table_rows)], table_sem.at[0])
    get_table.start()
    table[pl.ds(table_rows, 4096 - table_rows), :] = jnp.zeros((4096 - table_rows, 768), bf)
    slot, wanted = token_slots(ids_ref, table_rows)
    slot_out[...] = jnp.broadcast_to(slot, (512, 128))
    ids[...] = wanted

    def row_out(i, _):
        ids_out[i] = ids[pl.ds(i, 1), :]
        return 0

    lax.fori_loop(0, 128, row_out, 0)

    for c in range(2):
        for o in range(3):
            for x in range(RING):
                n, j = c * 12 + o * 4 + x, 2 * x + c
                source = wq_ref if n < 18 else wo_ref
                cut = slice(128 * (n % 18), 128 * (n % 18) + 128)
                sent_ref[j, 6 * o : 6 * o + 6, :] = source[0, :, cut].astype(f32)
                sent_ref[j, 18 + 6 * o : 24 + 6 * o, :] = wu_ref[0, :, 128 * n : 128 * n + 128].astype(f32)
    lane = lax.broadcasted_iota(jnp.int32, (8, 128), 1)
    place = (lane == 6 * mine + lax.broadcasted_iota(jnp.int32, (8, 128), 0)).astype(bf)[0:6]
    named = jnp.zeros((1, 128), f32)
    for p in range(4):
        named = named + jnp.where(lane[0:1] == 64 + 4 * mine + p, groups_ref[p].astype(f32), 0.0)
    gain_rows, bias_rows = mm(gains_ref[0], place), mm_tn(bias_ref[0], place)
    for j in range(8):
        sent_ref[j, 36:38, :] = gain_rows
        sent_ref[j, 38:48, :] = bias_rows
        sent_ref[j, 36:37, :] = sent_ref[j, 36:37, :] + named
    for o in range(3):
        a, b = wd_ref[0, :, 128 * o : 128 * o + 128], wd_ref[0, :, 384 + 128 * o : 512 + 128 * o]
        a, b = a.astype(f32), b.astype(f32)
        halves_ref[0, o] = jnp.where(core == 0, a, b)
        halves_ref[1, o] = jnp.where(core == 0, b, a)
    all_here()

    sent = []
    for k in range(1, 8):
        there = (mine + k) % 8
        copy = pltpu.make_async_remote_copy(
            src_ref=sent_ref.at[there], dst_ref=near.at[mine], send_sem=near_send.at[k], recv_sem=near_recv.at[k],
            device_id=(lax.axis_index("wide"), there), device_id_type=MESH,
        )
        copy.start()
        sent.append(copy)
    copy = pltpu.make_async_remote_copy(
        src_ref=halves_ref.at[1], dst_ref=half_got, send_sem=near_send.at[0], recv_sem=near_recv.at[0],
        device_id=device_at(spot, 1 - core), device_id_type=MESH,
    )
    copy.start()
    sent.append(copy)

    def ask(k, _):
        there = (me + k) % 128
        pltpu.make_async_remote_copy(
            src_ref=ids_out.at[there], dst_ref=ids_in.at[(128 - k) % 128],
            send_sem=ids_sem.at[0], recv_sem=ids_sem.at[1],
            device_id=(there // 8, there % 8), device_id_type=MESH,
        ).start()
        return 0

    lax.fori_loop(1, 128, ask, 0)
    ids_in[0] = ids_out[me]
    near[mine] = sent_ref[mine]
    for k in range(1, 8):
        ref = near.at[(mine + 8 - k) % 8]
        pltpu.make_async_copy(ref, ref, near_recv.at[k]).wait()
    pltpu.make_async_copy(half_got, half_got, near_recv.at[0]).wait()
    row = lax.broadcasted_iota(jnp.int32, (288, 384), 0)
    col = lax.broadcasted_iota(jnp.int32, (288, 384), 1)
    unit, at = row // UNIT, row % UNIT
    pick = col == at // 6 * UNIT + unit * 6 + at % 6
    units = mm(pick.astype(bf), near[...].reshape(384, 128).astype(bf)).astype(bf)
    for r in range(2):
        for o in range(3):
            first_row = UNIT * (3 * r + o)
            own[r, o] = units[first_row : first_row + UNIT].reshape(1, 1, 1, UNIT, 128)
    for o in range(3):
        a, b = halves_ref[0, o], half_got[o]
        upper, lower = jnp.where(core == 0, a, b), jnp.where(core == 0, b, a)
        own[2, o] = jnp.concatenate([upper, lower], axis=0).astype(bf).reshape(1, 1, 1, UNIT, 128)
    small = jnp.zeros((16, 128), f32)
    for j in range(8):
        small = small + near[j, 32:48, :]
    tiles[pl.ds(spot[1], 1), pl.ds(spot[2], 1)] = small.astype(bf).reshape(1, 1, 16, 128)

    g = Gather(w, units_size, send_sem, recv_sem, spot, core, (0, 1, 2))
    every = [(r, o) for r in range(3) for o in range(3)]
    keep = []
    for r, o in every:
        copy = pltpu.make_async_copy(own.at[r, o], g.block(r, o, g.here(o), core), local_sem.at[r, o])
        copy.start()
        keep.append(copy)
        if r < 2:
            g.begin(r, o, own.at[r, o])

    def tile_push(event, at, there):
        ref = tiles.at[at]
        copy = pltpu.make_async_remote_copy(
            src_ref=ref, dst_ref=ref, send_sem=tile_send.at[event], recv_sem=tile_recv.at[event],
            device_id=device_at(there, core), device_id_type=MESH,
        )
        copy.start()
        sent.append(copy)

    def tile_at(phase, v):
        return (pl.ds(v, 1), pl.ds(spot[2], 1)) if phase == 0 else (pl.ds(0, RING), pl.ds(v, 1))

    def tile_spread(phase):
        for k, by in enumerate((1, 2, 3)):
            tile_push(3 * phase + k, tile_at(phase, spot[phase + 1]), moved(spot, phase + 1, by))

    def tile_landed(phase):
        for k, by in enumerate((1, 2, 3)):
            ref = tiles.at[tile_at(phase, (spot[phase + 1] + RING - by) % RING)]
            pltpu.make_async_copy(ref, ref, tile_recv.at[3 * phase + k]).wait()

    tile_spread(0)
    for copy in keep:
        copy.wait()

    others = ids_in.at[pl.ds(0, 127)]
    pltpu.make_async_copy(others, others, ids_sem.at[1]).wait()

    def row_in(i, _):
        ids[pl.ds(i, 1), :] = ids_in[i]
        return 0

    lax.fori_loop(0, 128, row_in, 0)
    high, low = digits(ids[...])
    row = lax.broadcasted_iota(jnp.int32, (1024, 128), 0)
    col = lax.broadcasted_iota(jnp.int32, (1024, 128), 1)
    member_of = (row // 8 == col).astype(bf)
    both = mm(member_of, high) * 64.0 + mm(member_of, low)
    asked_col = jnp.sum(jnp.where(col == row % 8, both, 0.0), axis=1, keepdims=True) - 1.0
    asked[...] = jnp.broadcast_to(asked_col, (1024, 128))
    row = lax.broadcasted_iota(jnp.int32, (128, 1024), 0)
    col = lax.broadcasted_iota(jnp.int32, (128, 1024), 1)
    member_of = (col // 8 == row).astype(bf)
    both = mm_tn(high, member_of) * 64.0 + mm_tn(low, member_of)
    asked_row = jnp.sum(jnp.where(row == col % 8, both, 0.0), axis=0, keepdims=True) - 1.0
    asked_out[...] = jnp.broadcast_to(asked_row, (8, 1024))
    get_table.wait()

    def find(half):
        high, low = two_digits(asked[512 * half : 512 * half + 512, :], 128.0)
        low_hot = jnp.where(low == lane_names(512), jnp.ones((), bf), jnp.zeros((), bf))

        def chunk(i, _):
            hot = jnp.concatenate(hot_tiles(high, low_hot, (4 * i).astype(f32), 4), axis=1)
            part = mm(hot, table[pl.ds(pl.multiple_of(i * 512, 512), 512), :])
            resid[...] = jnp.where(i == 0, part, resid[...] + part)
            return 0

        lax.fori_loop(0, 8, chunk, 0)
        for q in range(4):
            rows_out[64 * half + 16 * q : 64 * half + 16 * q + 16] = pack_rows(resid[128 * q : 128 * q + 128, :])

        def answer(k, _):
            there = (me + k) % 128
            pltpu.make_async_remote_copy(
                src_ref=rows_out.at[k], dst_ref=rows_in.at[me], send_sem=rows_sem.at[0], recv_sem=rows_sem.at[1],
                device_id=(there // 8, there % 8), device_id_type=MESH,
            ).start()
            return 0

        lax.fori_loop(max(1, 64 * half), 64 * half + 64, answer, 0)

    find(0)
    rows_in[me] = rows_out[0]
    tile_landed(0)
    tile_spread(1)
    for o in range(3):
        g.planes(0, o)
        g.spread(0, o)
    find(1)
    for o in range(3):
        g.relay(0, o)
    for o in range(3):
        g.planes(1, o)
    tile_landed(1)

    row_at = lax.broadcasted_iota(jnp.int32, (128, 768), 0)
    col_at = lax.broadcasted_iota(jnp.int32, (128, 768), 1)
    all_vec = jnp.zeros((16, 768), f32)
    all_grp = jnp.zeros((16, 512), f32)
    for slab in range(16):
        part = tiles[slab // RING, slab % RING]
        pick = (col_at == row_at + UNIT * slab) & (row_at < UNIT)
        all_vec = all_vec + mm(part, pick.astype(bf))
        pick = (col_at == row_at - 64 + 32 * slab) & (row_at >= 64) & (row_at < 96)
        all_grp = all_grp + mm(part, pick[:, :512].astype(bf))
    vecs[...] = jnp.concatenate([all_vec[4:16], all_vec[0:4]], axis=0)
    group_row = all_grp[4:5]
    saves = []

    def save(scratch, out, at):
        copy = pltpu.make_async_copy(scratch, out, save_sem.at[at])
        copy.start()
        saves.append(copy)

    def collect(r):
        for o in range(3):
            g.collect(r, o)

    def arrived(r):
        for o in range(3):
            g.shared_done(r, o)
        save(w.at[r], w_out.at[r], 11 + r)

    save(vecs, vec_out, 0)
    for o in range(3):
        g.finish(0, o)
    others = rows_in.at[pl.ds(0, 127)]
    pltpu.make_async_copy(others, others, rows_sem.at[1]).wait()
    for o in range(3):
        g.spread(1, o, True)
    for o in range(3):
        g.begin(2, o, own.at[2, o])
    for q in range(8):
        row_mat[128 * q : 128 * q + 128, :] = unpack_rows(rows_in[16 * q : 16 * q + 16])
    slots_hot = slot_hot(slot_out)
    for p in range(3):
        cut = slice(256 * p, 256 * p + 256)
        x_ref[:, cut] = mm(slots_hot, row_mat[:, cut]).astype(bf)
    save(x_ref, x_out, 10)
    arrived(0)
    mask = head_mask()

    def qkv_step(n2, _):
        kind, p = n2 // 3, n2 % 3
        rows = vecs[2:4, :]
        bias = jnp.where(kind == 0, rows[0:1], jnp.where(kind == 2, rows[1:2], 0.0))
        bias = jnp.where(p == 0, bias[:, :256], jnp.where(p == 1, bias[:, 256:512], bias[:, 512:]))
        qkv[n2] = (mm(x_ref[...], panel(w, 0, n2)) + bias).astype(bf)
        return 0

    lax.fori_loop(0, 9, qkv_step, 0)
    save(qkv, qkv_out, 1)

    def attend(s, _):
        rows = pl.ds(pl.multiple_of(s * SEQ, SEQ), SEQ)
        slot = lax.broadcasted_iota(jnp.int32, (SEQ, 256), 0)
        live = slot < lens_ref[s % 2, s // 2]
        for p in range(3):
            query, key_part, value = qkv[p, rows, :], qkv[3 + p, rows, :], qkv[6 + p, rows, :]
            scores = mm_nt(key_part, spread_heads(query, mask)) * 0.125
            scores = jnp.where(live, scores, far_low)
            powers = jnp.exp(scores - jnp.max(scores, axis=0, keepdims=True))
            probs = powers / jnp.sum(powers, axis=0, keepdims=True)
            prob[s, p] = probs
            ctx[p, rows, :] = gather_heads(mm_tn(probs.astype(bf), value), mask).astype(bf)
        return 0

    lax.fori_loop(0, 4, attend, 0)
    collect(1)
    for o in range(3):
        g.planes(2, o)
        g.spread(2, o, True)
    lax.fori_loop(4, 8, attend, 0)
    save(prob, prob_out, 2)
    save(ctx, ctx_out, 3)
    context = jnp.concatenate([ctx[0], ctx[1], ctx[2]], axis=1)
    for p in range(3):
        resid[:, 256 * p : 256 * p + 256] = mm(context, panel(w, 0, 9 + p))

    def norm_one_step(s, _):
        rows = pl.ds(pl.multiple_of(s * SEQ, SEQ), SEQ)
        value = x_ref[rows, :].astype(f32) + (resid[rows, :] + vecs[4:5, :])
        centred = value - jnp.mean(value, axis=1, keepdims=True)
        inverse = lax.rsqrt(jnp.mean(centred * centred, axis=1, keepdims=True) + norm_eps)
        scaled = centred * inverse
        h1[rows, :] = scaled
        inv[0, rows, :] = jnp.broadcast_to(inverse, (SEQ, 128))
        normed = scaled * vecs[0:1, :] + vecs[5:6, :]
        nl[rows, :] = normed.astype(bf)
        resid[rows, :] = normed + vecs[6:7, :]
        return 0

    lax.fori_loop(0, 8, norm_one_step, 0)
    save(h1, h1_out, 4)
    save(nl, nl_out, 5)
    arrived(1)

    def up_step(n2, _):
        weight = panel(w, 1, n2)
        q, p = n2 // 3, n2 % 3
        rows = vecs[8:12, :]
        bias = jnp.where(q == 0, rows[0:1], jnp.where(q == 1, rows[1:2], jnp.where(q == 2, rows[2:3], rows[3:4])))
        bias = jnp.where(p == 0, bias[:, :256], jnp.where(p == 1, bias[:, 256:512], bias[:, 512:]))
        for half in range(4):
            part = pl.ds(128 * half, 128)
            pre = mm(nl[part, :], weight) + bias
            upper = 0.5 + 0.5 * lax.erf(pre * 0.7071067811865476)
            act[n2, part, :] = (pre * upper).astype(bf)
            gp[n2, part, :] = upper + pre * (jnp.exp(-0.5 * pre * pre) * 0.3989422804014327)
        return 0

    lax.fori_loop(0, 4, up_step, 0)
    collect(2)
    lax.fori_loop(4, 12, up_step, 0)
    save(act, act_out, 6)
    save(gp, gp_out, 7)
    arrived(2)

    def down_step(y, _):
        hidden = jnp.concatenate([act[3 * y], act[3 * y + 1], act[3 * y + 2]], axis=1)
        for p in range(3):
            weight = jnp.concatenate([down_panel(w, 2 * p, y), down_panel(w, 2 * p + 1, y)], axis=1)
            cols = slice(256 * p, 256 * p + 256)
            resid[:, cols] = resid[:, cols] + mm(hidden, weight)
        return 0

    lax.fori_loop(0, RING, down_step, 0)

    def norm_two_step(s, _):
        rows = pl.ds(pl.multiple_of(s * SEQ, SEQ), SEQ)
        value = resid[rows, :]
        centred = value - jnp.mean(value, axis=1, keepdims=True)
        inverse = lax.rsqrt(jnp.mean(centred * centred, axis=1, keepdims=True) + norm_eps)
        scaled = centred * inverse
        h2[rows, :] = scaled
        inv[1, rows, :] = jnp.broadcast_to(inverse, (SEQ, 128))
        state = scaled * vecs[1:2, :] + vecs[7:8, :]
        live = lax.broadcasted_iota(jnp.int32, (SEQ, 768), 0) < lens_ref[s % 2, s // 2]
        mean_vec = jnp.sum(jnp.where(live, state, 0.0), axis=0, keepdims=True) / lens_ref[s % 2, s // 2].astype(f32)
        r = lax.rsqrt(jnp.sum(mean_vec * mean_vec, axis=1, keepdims=True) + pool_eps)
        pooled[s] = mean_vec * r
        rnorm[s] = jnp.broadcast_to(r, (1, 768))
        return 0

    lax.fori_loop(0, 8, norm_two_step, 0)
    save(h2, h2_out, 8)
    save(inv, inv_out, 9)

    sources = jnp.concatenate([pooled[2 * i] for i in range(4)], axis=0)
    targets = jnp.concatenate([pooled[2 * i + 1] for i in range(4)], axis=0)
    first = core == 0
    pad = jnp.zeros((4, 768), f32)
    pool_own[0] = jnp.concatenate([jnp.where(first, targets, sources), pad], axis=0)
    swap = pltpu.make_async_remote_copy(
        src_ref=pool_own.at[0], dst_ref=pool_swap, send_sem=swap_sem.at[0], recv_sem=swap_sem.at[1],
        device_id=device_at(spot, 1 - core), device_id_type=MESH,
    )
    swap.start()
    swap.wait()
    got = pool_swap[0:4, :]
    kind = jnp.concatenate(
        [jnp.where(first, sources, got), jnp.where(first, got, targets)], axis=0
    )
    q = Gather(pool_all, pool_size, pool_send, pool_recv, spot, core, (1, 2, 0))
    for o in range(3):
        unit = jnp.concatenate([kind[:, 256 * o : 256 * o + 128], kind[:, 256 * o + 128 : 256 * o + 256]], axis=0)
        here = (pl.ds(spot[1], 1), pl.ds(spot[2], 1), pl.ds(spot[0], 1))
        pool_all[(0, core, o) + here] = unit.reshape(1, 1, 1, 16, 128)
    for o in range(3):
        q.begin(0, o, None)
    for o in range(3):
        q.planes(0, o)
        q.spread(0, o, True)
    for o in range(3):
        q.collect(0, o)
    for o in range(3):
        q.shared_done(0, o)

    for k, out in ((0, left3), (1, right3)):
        for o in range(3):
            for h in range(2):
                block = pool_all[0, k, o, :, :, :, 8 * h : 8 * h + 8, :].reshape(512, 128)
                high, low = split_low(block)
                at = 256 * o + 128 * h
                parts = (high, high, low) if k == 0 else (high, low, high)
                for i in range(3):
                    out[:, 768 * i + at : 768 * i + at + 128] = parts[i]
    pair_row = lax.broadcasted_iota(jnp.int32, (512, 256), 0)
    pair_col = lax.broadcasted_iota(jnp.int32, (512, 256), 1)
    names = lax.broadcasted_iota(jnp.int32, (16, 512), 0).astype(f32)
    member = (names == group_row).astype(bf)

    def column_lse(rows3, cols3, into):
        for p in range(2):
            cut = slice(256 * p, 256 * p + 256)
            scores = logit_scale * mm_nt(rows3[...], cols3[cut, :])
            scores = scores - jnp.where(pair_row == pair_col + 256 * p, logit_scale * margin, 0.0)
            alike = mm_tn(member, member[:, cut]) > 0.5
            scores = jnp.where(alike, scores, far_low)
            peak = jnp.max(scores, axis=0, keepdims=True)
            total = jnp.sum(jnp.exp(scores - peak), axis=0, keepdims=True)
            stats[into : into + 1, cut] = peak + jnp.log(total)

    column_lse(left3, right3, 0)
    column_lse(right3, left3, 1)
    chip = (spot[1] * RING + spot[2]) * RING + spot[0]
    mine = pl.ds(pl.multiple_of(chip * 8, 8), 8)
    weight = 1.0 / 1024.0
    at_row = lax.broadcasted_iota(jnp.int32, (8, 512), 0) + chip * 8
    at_col = lax.broadcasted_iota(jnp.int32, (8, 512), 1)
    own_pair = at_row == at_col
    pick = (lax.broadcasted_iota(jnp.int32, (8, 512), 1) == at_row).astype(bf)
    own_member = mm_nt(pick, member)
    alike = mm(own_member.astype(bf), member) > 0.5
    grads = []
    terms = []
    for k, (rows3, cols3) in enumerate(((left3, right3), (right3, left3))):
        block = pool_all[0, k, :, pl.ds(spot[1], 1), pl.ds(spot[2], 1), pl.ds(spot[0], 1)]
        cut = [block[o, 0, 0, 0, 8 * h : 8 * h + 8, :] for o in range(3) for h in range(2)]
        own8 = jnp.concatenate(cut, axis=1)
        high, low = split_low(own8)
        parts = (high, high, low) if k == 0 else (high, low, high)
        scores = logit_scale * mm_nt(jnp.concatenate(parts, axis=1), cols3[...])
        scores = scores - jnp.where(own_pair, logit_scale * margin, 0.0)
        diagonal = jnp.sum(jnp.where(own_pair, scores, 0.0), axis=1, keepdims=True)
        scores = jnp.where(alike, scores, far_low)
        peak = jnp.max(scores, axis=1, keepdims=True)
        lse = peak + jnp.log(jnp.sum(jnp.exp(scores - peak), axis=1, keepdims=True))
        other = stats[k : k + 1, :]
        mix = weight * (jnp.exp(scores - lse) + jnp.exp(scores - other))
        mix = mix - jnp.where(own_pair, 2.0 * weight, 0.0)
        mix_high, mix_low = split_low(mix)
        high_at, low_at = (0, 768) if k == 0 else (0, 1536)
        high_cols, low_cols = cols3[:, high_at : high_at + 768], cols3[:, low_at : low_at + 768]
        grad = mm(mix_high, high_cols) + mm(mix_high, low_cols) + mm(mix_low, high_cols)
        grads.append(logit_scale * jnp.where(first, grad[0:4], grad[4:8]))
        terms.append(jnp.where(first, (lse - diagonal)[0:4], (lse - diagonal)[4:8]))
    row = lax.broadcasted_iota(jnp.int32, (4, 128), 0)
    lane = lax.broadcasted_iota(jnp.int32, (4, 128), 1)
    rows = [jnp.sum(jnp.where(row == lane, terms[k], 0.0), axis=0, keepdims=True) for k in range(2)]
    loss_out[...] = jnp.concatenate(rows + [jnp.zeros((6, 128), f32)], axis=0)
    for s in range(8):
        d_row = grads[s % 2][s // 2 : s // 2 + 1, :]
        row = pooled[s]
        inner = jnp.sum(row * d_row, axis=1, keepdims=True)
        dpool_out[s] = rnorm[s] * (d_row - row * inner) / lens_ref[s % 2, s // 2].astype(f32)
    g.drain(3)
    q.drain(1)
    for copy in sent:
        copy.wait_send()
    for sem, ref in ((ids_sem, ids_in), (rows_sem, rows_in)):
        others = ref.at[pl.ds(0, 127)]
        pltpu.make_async_copy(others, others, sem.at[0]).wait()
    for copy in saves:
        copy.wait()


def forward_pass(lengths, groups, ids, w_qkv, w_out, w_up, w_down, gains, biases, table):
    bf, f32 = jnp.bfloat16, jnp.float32
    shapes = [
        ((3, 2, 3, RING, RING, RING, UNIT, 128), bf),
        ((16, 768), f32),
        ((512, 768), f32),
        ((512, 768), f32),
        ((2, 512, 128), f32),
        ((512, 768), bf),
        ((12, 512, 256), bf),
        ((12, 512, 256), f32),
        ((9, 512, 256), bf),
        ((8, 3, SEQ, 256), f32),
        ((3, 512, 256), bf),
        ((512, 768), bf),
        ((8, 1, 768), f32),
        ((8, 128), f32),
        ((512, 128), f32),
        ((8, 1024), f32),
    ]
    anywhere = pl.BlockSpec(memory_space=pl.ANY)
    vmem = pl.BlockSpec(memory_space=pltpu.VMEM)
    dma = pltpu.SemaphoreType.DMA
    return pl.pallas_call(
        forward_kernel,
        out_shape=[jax.ShapeDtypeStruct(*s) for s in shapes],
        in_specs=[pl.BlockSpec(memory_space=pltpu.SMEM)] * 2 + [vmem] * 7 + [anywhere],
        out_specs=[anywhere] * 12 + [vmem] * 4,
        scratch_shapes=[
            pltpu.VMEM(*shapes[0]),
            pltpu.VMEM(*shapes[1]),
            pltpu.VMEM((RING, RING, 16, 128), bf),
            *[pltpu.VMEM(*s) for s in shapes[2:12]],
            pltpu.VMEM((512, 768), f32),
            pltpu.VMEM((8, 1, 768), f32),
            pltpu.VMEM((8, 1, 768), f32),
            pltpu.VMEM((1, 8, 768), f32),
            pltpu.VMEM((8, 768), f32),
            pltpu.VMEM((1, 2, 3, RING, RING, RING, 16, 128), f32),
            pltpu.VMEM((512, 2304), bf),
            pltpu.VMEM((512, 2304), bf),
            pltpu.VMEM((8, 512), f32),
            pltpu.VMEM((3, 3, 1, 1, 1, UNIT, 128), bf),
            pltpu.VMEM((8, UNIT, 128), f32),
            pltpu.VMEM((8, UNIT, 128), f32),
            pltpu.VMEM((2, 3, 24, 128), f32),
            pltpu.VMEM((3, 24, 128), f32),
            pltpu.VMEM((4096, 768), bf),
            pltpu.VMEM((128, 1, 128), f32),
            pltpu.VMEM((128, 1, 128), f32),
            pltpu.VMEM((128, 128), f32),
            pltpu.VMEM((1024, 128), f32),
            pltpu.VMEM((128, 16, 384), bf),
            pltpu.VMEM((128, 16, 384), bf),
            pltpu.VMEM((1024, 768), bf),
            pltpu.VMEM((15, UNIT, 128), bf),
            pltpu.VMEM((15, 16, 128), f32),
            dma((3, 3, 9)),
            dma((3, 3, 9)),
            dma((3, 3)),
            dma((1, 3, 9)),
            dma((1, 3, 9)),
            dma((6,)),
            dma((6,)),
            dma((2,)),
            dma((14,)),
            dma((8,)),
            dma((8,)),
            dma((2,)),
            dma((2,)),
            dma((1,)),
        ],
        compiler_params=pltpu.CompilerParams(
            collective_id=1, has_side_effects=True, vmem_limit_bytes=62 * 1024 * 1024
        ),
        name="forward_pass",
    )(lengths, groups, ids, w_qkv, w_out, w_up, w_down, gains, biases, table)


class Reduce:
    def __init__(self, parts, bufs, plane, out, send_sem, recv_sem, spot, core):
        self.parts, self.bufs, self.plane_in, self.out = parts, bufs, plane, out
        self.send_sem, self.recv_sem = send_sem, recv_sem
        self.spot, self.core = spot, core
        self.sent = []

    def copy(self, src, dst, r, o, event, there):
        copy = pltpu.make_async_remote_copy(
            src_ref=src,
            dst_ref=dst,
            send_sem=self.send_sem.at[r, o, event],
            recv_sem=self.recv_sem.at[r, o, event],
            device_id=device_at(there, self.core),
            device_id_type=MESH,
        )
        copy.start()
        return copy

    def landed(self, dst, r, o, event):
        pltpu.make_async_copy(dst, dst, self.recv_sem.at[r, o, event]).wait()

    def spans(self, o, at, half=None):
        ring, first, second = ORDERS[o]
        return {ring: (at, 1), first: (0, RING) if half is None else (2 * half, 2), second: (0, RING)}

    def mine(self, r, o, spans):
        return block_of(self.parts, r, self.core, o, spans)

    def slot(self, r, o, which):
        return self.bufs[o * 2].at[r, which] if which < 3 else self.bufs[o * 2 + 1].at[0, which - 3]

    def add_into(self, into, others):
        sizes = into.shape[:3]

        def one(i, _):
            at = (i // sizes[1], i % sizes[1])
            if len(others) == 1:
                into[at] = into[at] + others[0][at]
            else:
                value = into[at].astype(jnp.float32)
                for other in others:
                    value = value + other[at].astype(jnp.float32)
                into[at] = value.astype(jnp.bfloat16)
            return 0

        lax.fori_loop(0, sizes[0] * sizes[1], one, 0)

    def first(self, r, o):
        d = ORDERS[o][0]
        if True:
            for by in (1, 3, 2):
                there = moved(self.spot, d, by)
                src = self.mine(r, o, self.spans(o, there[d]))
                self.sent.append(self.copy(src, self.slot(r, o, by - 1), r, o, by - 1, there))
            return
        across = (self.spot[d] + 2) % RING
        for half, by in ((0, 1), (1, -1)):
            src = self.mine(r, o, self.spans(o, across, half))
            self.sent.append(self.copy(src, self.slot(r, o, 3 + half), r, o, 2 + 3 * half, moved(self.spot, d, by)))

    def second(self, r, o):
        d = ORDERS[o][0]
        for half, by in ((0, 1), (1, -1)):
            at = (self.spot[d] + by) % RING
            view = self.slot(r, o, 3 + half)
            self.landed(view, r, o, 2 + 3 * half)
            self.add_into(self.mine(r, o, self.spans(o, at, half)), [view])
            src = self.mine(r, o, self.spans(o, at))
            self.sent.append(self.copy(src, self.slot(r, o, half), r, o, half, moved(self.spot, d, by)))

    def third(self, r, o):
        ring, first, second = ORDERS[o]
        views = [self.slot(r, o, k) for k in range(3)]
        for k, view in enumerate(views):
            self.landed(view, r, o, k)
        self.add_into(self.mine(r, o, self.spans(o, self.spot[ring])), views)

        def one(k, _):
            there = moved(moved(self.spot, first, k % RING), second, k // RING)
            src = self.mine(r, o, {d: (there[d], 1) for d in range(3)})
            self.copy(src, self.plane_in.at[r, o, pl.ds(k, 1), pl.ds(0, 1), pl.ds(0, 1)], r, o, 4, there)
            return 0

        lax.fori_loop(1, 16, one, 0)

    def fourth(self, r, o):
        others = self.plane_in.at[r, o, pl.ds(1, 15)]
        self.landed(others, r, o, 4)
        here = self.mine(r, o, {d: (self.spot[d], 1) for d in range(3)})
        total = here[0, 0, 0].astype(jnp.float32)
        for k in range(1, 16):
            total = total + self.plane_in[r, o, k, 0, 0].astype(jnp.float32)
        self.out[r, o] = total

    def drain(self):
        for r in range(3):
            for o in range(3):
                others = self.plane_in.at[r, o, pl.ds(1, 15)]
                pltpu.make_async_copy(others, others, self.send_sem.at[r, o, 4]).wait()
        for copy in self.sent:
            copy.wait_send()


def reduce_buffers(rounds):
    bufs = []
    for o in range(3):
        ring, first, second = ORDERS[o]
        sizes = [RING] * 3
        sizes[ring] = 1
        half = list(sizes)
        half[first] = 2
        bufs.append(pltpu.VMEM((rounds, 3, *sizes, UNIT, 128), jnp.bfloat16))
        bufs.append(pltpu.VMEM((1, 2, *half, UNIT, 128), jnp.bfloat16))
    return bufs


TABLE_STEP = 784
TABLE_BASE = 112


def asked_digits(asked_ref):
    high, low = two_digits(jnp.broadcast_to(asked_ref[0:1, :], (TABLE_BASE, 1024)), float(TABLE_BASE))
    name = lax.broadcasted_iota(jnp.int32, (TABLE_BASE, 1024), 0).astype(jnp.float32).astype(jnp.bfloat16)
    return high, jnp.where(low == name, jnp.ones((), jnp.bfloat16), jnp.zeros((), jnp.bfloat16))


def norm_back(grad, scaled, inverse, gain):
    e = grad * gain
    mean_e = jnp.mean(e, axis=1, keepdims=True)
    mean_eh = jnp.mean(e * scaled, axis=1, keepdims=True)
    return inverse * (e - mean_e - scaled * mean_eh)


def backward_kernel(
    lens_ref, vec_ref, dpool_ref, x_ref, slot_ref,
    w_in, h1_in, h2_in, inv_in, nl_in, act_in, gp_in, qkv_in, prob_in, ctx_in,
    token_out, rows_in, qkv_out, out_out, up_out, down_out, vec_out,
    w, h1, h2, inv, nl, act, gp, qkv, prob, ctx, parts, d2d, d_res, d_low, turned, dvec, vec_slots, red_out, near_out, near_in, half_in, rows_out, *rest,
):
    bufs, plane_in, rest = rest[:6], rest[6], rest[7:]
    send_sem, recv_sem, swap_send, swap_recv, free_sem, vec_send, vec_recv, load_sem, gp_sem, w_sem, near_send, near_recv, rows_sem = rest
    me = lax.axis_index("wide") * 8 + lax.axis_index("narrow")
    spot, core = where_am_i()
    bf, f32 = jnp.bfloat16, jnp.float32

    def load(src, dst, at):
        copy = pltpu.make_async_copy(src, dst, load_sem.at[at])
        copy.start()
        return copy

    def load_w(r, at):
        copy = pltpu.make_async_copy(w_in.at[r], w.at[at], w_sem.at[r])
        copy.start()
        return copy

    def load_gp(y, at):
        return pltpu.make_async_copy(gp_in.at[pl.ds(3 * y, 3)], gp.at[at], gp_sem.at[at])

    get_h2, get_inv = load(h2_in, h2, 0), load(inv_in, inv, 1)
    get_act = load(act_in, act, 2)
    get_w2 = load_w(2, 0)
    load_gp(0, 0).start()
    load_gp(1, 1).start()
    get_nl = load(nl_in, nl, 3)
    get_w1 = load_w(1, 1)
    get_h1, get_ctx = load(h1_in, h1, 4), load(ctx_in, ctx, 5)
    get_qkv, get_prob = load(qkv_in, qkv, 6), load(prob_in, prob, 7)
    all_here = greet_all()
    red = Reduce(parts, bufs, plane_in, red_out, send_sem, recv_sem, spot, core)
    swaps = {}

    def give(r):
        if r == 0:
            pl.semaphore_wait(free_sem, 1)
        for o in range(3):
            copy = pltpu.make_async_remote_copy(
                src_ref=parts.at[r, 1 - core, o], dst_ref=d2d.at[r % 2, o],
                send_sem=swap_send.at[r, o], recv_sem=swap_recv.at[r, o],
                device_id=device_at(spot, 1 - core), device_id_type=MESH,
            )
            copy.start()
            red.sent.append(copy)

    def take(r):
        for o in range(3):
            view = d2d.at[r % 2, o]
            pltpu.make_async_copy(view, view, swap_recv.at[r, o]).wait()
            red.add_into(parts.at[r, core, o], [view])
            red.first(r, o)
        if r == 2:
            pl.semaphore_signal(free_sem, inc=1, device_id=device_at(spot, 1 - core), device_id_type=MESH)

    def second(r):
        for o in range(3):
            red.second(r, o)

    def third(r):
        for o in range(3):
            red.third(r, o)

    def fourth(r):
        for o in range(3):
            red.fourth(r, o)

    dvec[0] = jnp.zeros((16, 768), f32)

    def add_vec(row, value):
        dvec[0, row : row + 1, :] = dvec[0, row : row + 1, :] + value

    def total(value):
        return jnp.sum(value, axis=0, keepdims=True)

    get_h2.wait()
    get_inv.wait()

    def norm_two_step(s, _):
        rows = pl.ds(pl.multiple_of(s * SEQ, SEQ), SEQ)
        live = lax.broadcasted_iota(jnp.int32, (SEQ, 768), 0) < lens_ref[s % 2, s // 2]
        grad = jnp.where(live, jnp.broadcast_to(dpool_ref[s], (SEQ, 768)), 0.0)
        scaled = h2[rows, :]
        inverse = inv[1, rows, 0:1]
        back = norm_back(grad, scaled, inverse, vec_ref[1:2, :])
        low = back.astype(bf)
        d_res[rows, :] = back
        d_low[rows, :] = low
        add_vec(1, total(grad * scaled))
        add_vec(7, total(grad))
        add_vec(6, total(low.astype(f32)))
        return 0

    lax.fori_loop(0, 8, norm_two_step, 0)
    get_act.wait()

    def down_step(y, _):
        hidden = jnp.concatenate([act[3 * y], act[3 * y + 1], act[3 * y + 2]], axis=1)
        turned[...] = hidden.T
        for p in range(3):
            block = mm(turned[...], d_low[:, 256 * p : 256 * p + 256]).astype(bf)
            for k in range(2):
                cb = 2 * p + k
                for z in range(RING):
                    for x in range(RING):
                        at = UNIT * (RING * z + x)
                        parts[2, cb // 3, cb % 3, x, y, z] = block[at : at + UNIT, 128 * k : 128 * k + 128]
        return 0

    lax.fori_loop(0, RING, down_step, 0)
    all_here()
    give(2)
    get_w2.wait()

    def pre_step(y, _):
        at = y % 2
        load_gp(y, at).wait()
        columns = [
            jnp.concatenate([w[0, cb // 3, cb % 3, x, y, z] for z in range(RING) for x in range(RING)], axis=0)
            for cb in range(6)
        ]
        weight = jnp.concatenate(columns, axis=1)
        for j in range(3):
            grad = mm_nt(d_low[...], weight[256 * j : 256 * j + 256, :]) * gp[at, j]
            low = grad.astype(bf)
            act[3 * y + j] = low
            cut = slice(256 * j, 256 * j + 256)
            dvec[0, pl.ds(8 + y, 1), cut] = total(low.astype(f32))

        @pl.when(y < 2)
        def _():
            load_gp(y + 2, at).start()

        return 0

    lax.fori_loop(0, RING, pre_step, 0)
    get_w0 = load_w(0, 0)
    get_nl.wait()
    turned_nl = nl[...].T
    turned[:, :] = turned_nl

    def up_step(n2, _):
        block = mm(turned[...], act[n2]).astype(bf)
        c, o, x = n2 // 6, n2 // 2 % 3, n2 % 2 * 2
        for k in range(2):
            parts[1, c, o, x + k] = block[:, 128 * k : 128 * k + 128].reshape(RING, RING, UNIT, 128)
        return 0

    lax.fori_loop(0, 12, up_step, 0)
    give(1)
    take(2)
    get_w1.wait()

    def six_blocks(at, n):
        blocks = []
        for k in range(6):
            m = n + k
            blocks.append(w[at, m // 12, m // 4 % 3, m % 4].reshape(768, 128))
        return jnp.concatenate(blocks, axis=1)

    def up_back_step(t, _):
        low = jnp.concatenate([act[3 * t], act[3 * t + 1], act[3 * t + 2]], axis=1)
        weight = six_blocks(1, 6 * t)
        for p in range(3):
            cut = slice(256 * p, 256 * p + 256)
            d_res[:, cut] = d_res[:, cut] + mm_nt(low, weight[cut, :])
        return 0

    lax.fori_loop(0, RING, up_back_step, 0)
    get_h1.wait()

    def norm_one_step(s, _):
        rows = pl.ds(pl.multiple_of(s * SEQ, SEQ), SEQ)
        grad, scaled = d_res[rows, :], h1[rows, :]
        back = norm_back(grad, scaled, inv[0, rows, 0:1], vec_ref[0:1, :])
        low = back.astype(bf)
        d_res[rows, :] = back
        d_low[rows, :] = low
        add_vec(0, total(grad * scaled))
        add_vec(5, total(grad))
        add_vec(4, total(low.astype(f32)))
        return 0

    lax.fori_loop(0, 8, norm_one_step, 0)
    take(1)
    get_ctx.wait()
    turned[...] = jnp.concatenate([ctx[0], ctx[1], ctx[2]], axis=1).T
    get_w0.wait()
    weight = six_blocks(0, 18)
    for p in range(3):
        cut = slice(256 * p, 256 * p + 256)
        block = mm(turned[...], d_low[:, cut]).astype(bf)
        for k in range(2):
            n = 18 + 2 * p + k
            parts[0, n // 12, n // 4 % 3, n % 4] = block[:, 128 * k : 128 * k + 128].reshape(RING, RING, UNIT, 128)
        ctx[p] = mm_nt(d_low[...], weight[cut, :]).astype(bf)
    get_qkv.wait()
    get_prob.wait()
    mask = head_mask()

    def attend_back(s, _):
        rows = pl.ds(pl.multiple_of(s * SEQ, SEQ), SEQ)
        for p in range(3):
            query, key_part, value = qkv[p, rows, :], qkv[3 + p, rows, :], qkv[6 + p, rows, :]
            wide_grad = spread_heads(ctx[p, rows, :], mask)
            probs = prob[s, p]
            d_value = mm(probs.astype(bf), wide_grad)
            d_probs = mm_nt(value, wide_grad)
            centre = jnp.sum(probs * d_probs, axis=0, keepdims=True)
            d_scores = (probs * (d_probs - centre)).astype(bf)
            d_query = gather_heads(mm_tn(d_scores, key_part), mask) * 0.125
            d_key = mm(d_scores, spread_heads(query, mask)) * 0.125
            low_query, low_value = d_query.astype(bf), d_value.astype(bf)
            qkv[p, rows, :] = low_query
            qkv[3 + p, rows, :] = d_key.astype(bf)
            qkv[6 + p, rows, :] = low_value
            cut = slice(256 * p, 256 * p + 256)
            dvec[0, 2:3, cut] = dvec[0, 2:3, cut] + total(low_query.astype(f32))
            dvec[0, 3:4, cut] = dvec[0, 3:4, cut] + total(low_value.astype(f32))
        return 0

    lax.fori_loop(0, 4, attend_back, 0)
    third(2)
    lax.fori_loop(4, 8, attend_back, 0)
    vec_sent = []

    def vec_push(event, src, there, c):
        copy = pltpu.make_async_remote_copy(
            src_ref=src, dst_ref=vec_slots.at[event], send_sem=vec_send.at[event], recv_sem=vec_recv.at[event],
            device_id=device_at(there, c), device_id_type=MESH,
        )
        copy.start()
        vec_sent.append(copy)

    def vec_landed(event):
        ref = vec_slots.at[event]
        pltpu.make_async_copy(ref, ref, vec_recv.at[event]).wait()

    def vec_start(d):
        for by in (1, 2, 3):
            vec_push(3 * d + by, dvec.at[d + 1], moved(spot, d, by), core)

    def vec_add(d):
        for by in (1, 2, 3):
            vec_landed(3 * d + by)
        sides = vec_slots[1 + 3 * d] + vec_slots[3 + 3 * d]
        dvec[d + 2] = (dvec[d + 1] + sides) + vec_slots[2 + 3 * d]

    vec_push(0, dvec.at[0], spot, 1 - core)

    third(1)
    def input_step(t, _):
        low = jnp.concatenate([qkv[3 * t], qkv[3 * t + 1], qkv[3 * t + 2]], axis=1)
        weight = six_blocks(0, 6 * t)
        for p in range(3):
            cut = slice(256 * p, 256 * p + 256)
            d_res[:, cut] = d_res[:, cut] + mm_nt(low, weight[cut, :])
        return 0

    lax.fori_loop(0, 3, input_step, 0)
    token_copy = pltpu.make_async_copy(d_res, token_out, load_sem.at[8])
    token_copy.start()
    d_low[...] = d_res[...].astype(bf)
    slots_hot = slot_hot(slot_ref)
    for q in range(4):
        rows = mm_tn(slots_hot[:, 256 * q : 256 * q + 256], d_low[...])
        rows_out[32 * q : 32 * q + 32] = pack_rows(rows)

    def hand_back(k, _):
        there = (me + k) % 128
        pltpu.make_async_remote_copy(
            src_ref=rows_out.at[there], dst_ref=rows_in.at[(128 - k) % 128],
            send_sem=rows_sem.at[0], recv_sem=rows_sem.at[1],
            device_id=(there // 8, there % 8), device_id_type=MESH,
        ).start()
        return 0

    lax.fori_loop(1, 128, hand_back, 0)
    keep_rows = pltpu.make_async_copy(rows_out.at[me], rows_in.at[0], load_sem.at[9])
    keep_rows.start()
    turned[...] = x_ref[...].T

    def qkv_step(i, _):
        n2 = (i + 6 * (1 - core)) % 9
        block = mm(turned[...], qkv[n2]).astype(bf)
        c, o, x = n2 // 6, n2 // 2 % 3, n2 % 2 * 2
        for k in range(2):
            parts[0, c, o, x + k] = block[:, 128 * k : 128 * k + 128].reshape(RING, RING, UNIT, 128)
        return 0

    lax.fori_loop(0, 6, qkv_step, 0)
    give(0)
    lax.fori_loop(6, 9, qkv_step, 0)
    vec_landed(0)
    dvec[1] = dvec[0] + vec_slots[0]
    vec_start(0)
    fourth(2)
    take(0)
    vec_add(0)
    vec_start(1)
    fourth(1)
    vec_add(1)
    vec_start(2)
    third(0)
    vec_add(2)
    vec_out[...] = dvec[4]
    fourth(0)

    mine = spot[0] * 2 + core
    for j in range(8):
        for r in range(2):
            for o in range(3):
                at = 6 * (3 * r + o)
                near_out[j, at : at + 6, :] = red_out[r, o, 6 * j : 6 * j + 6, :]
    for k in range(1, 8):
        there = (mine + k) % 8
        copy = pltpu.make_async_remote_copy(
            src_ref=near_out.at[there], dst_ref=near_in.at[mine], send_sem=near_send.at[k], recv_sem=near_recv.at[k],
            device_id=(lax.axis_index("wide"), there), device_id_type=MESH,
        )
        copy.start()
        vec_sent.append(copy)
    theirs = pl.ds(pl.multiple_of(24 * (1 - core), 8), 24)
    copy = pltpu.make_async_remote_copy(
        src_ref=red_out.at[2, :, theirs], dst_ref=half_in, send_sem=near_send.at[0], recv_sem=near_recv.at[0],
        device_id=device_at(spot, 1 - core), device_id_type=MESH,
    )
    copy.start()
    vec_sent.append(copy)
    near_in[mine] = near_out[mine]
    for k in range(1, 8):
        ref = near_in.at[(mine + 8 - k) % 8]
        pltpu.make_async_copy(ref, ref, near_recv.at[k]).wait()
    pltpu.make_async_copy(half_in, half_in, near_recv.at[0]).wait()
    for c in range(2):
        for o in range(3):
            for x in range(RING):
                n, j = c * 12 + o * 4 + x, 2 * x + c
                block = near_in[j, 6 * o : 6 * o + 6, :]
                if n < 18:
                    qkv_out[:, 128 * n : 128 * n + 128] = block
                else:
                    out_out[:, 128 * (n - 18) : 128 * (n - 18) + 128] = block
                up_out[:, 128 * n : 128 * n + 128] = near_in[j, 18 + 6 * o : 24 + 6 * o, :]
    ours = pl.ds(pl.multiple_of(24 * core, 8), 24)
    for o in range(3):
        a, b = red_out[2, o, ours, :], half_in[o]
        down_out[:, 128 * o : 128 * o + 128] = jnp.where(core == 0, a, b)
        down_out[:, 384 + 128 * o : 512 + 128 * o] = jnp.where(core == 0, b, a)
    others = rows_in.at[pl.ds(0, 127)]
    pltpu.make_async_copy(others, others, rows_sem.at[1]).wait()
    pltpu.make_async_copy(others, others, rows_sem.at[0]).wait()
    token_copy.wait()
    keep_rows.wait()
    red.drain()
    for copy in vec_sent:
        copy.wait_send()


def backward_pass(lens, vectors, d_pool, x, slots, w, h1, h2, inv, nl, act, gp, qkv, prob, ctx):
    bf, f32 = jnp.bfloat16, jnp.float32
    anywhere = pl.BlockSpec(memory_space=pl.ANY)
    vmem = pl.BlockSpec(memory_space=pltpu.VMEM)
    dma = pltpu.SemaphoreType.DMA
    scratch = [
        pltpu.VMEM((2, *w.shape[1:]), bf),
        pltpu.VMEM(h1.shape, f32),
        pltpu.VMEM(h2.shape, f32),
        pltpu.VMEM(inv.shape, f32),
        pltpu.VMEM(nl.shape, bf),
        pltpu.VMEM(act.shape, bf),
        pltpu.VMEM((2, 3, 512, 256), f32),
        pltpu.VMEM(qkv.shape, bf),
        pltpu.VMEM(prob.shape, f32),
        pltpu.VMEM(ctx.shape, bf),
        pltpu.VMEM(w.shape, bf),
        pltpu.VMEM((2, *w.shape[2:]), bf),
        pltpu.VMEM((512, 768), f32),
        pltpu.VMEM((512, 768), bf),
        pltpu.VMEM((768, 512), bf),
        pltpu.VMEM((5, 16, 768), f32),
        pltpu.VMEM((10, 16, 768), f32),
        pltpu.VMEM((3, 3, UNIT, 128), f32),
        pltpu.VMEM((8, 40, 128), f32),
        pltpu.VMEM((8, 40, 128), f32),
        pltpu.VMEM((3, 24, 128), f32),
        pltpu.VMEM((128, 16, 384), bf),
        *reduce_buffers(3),
        pltpu.VMEM((3, 3, 16, 1, 1, UNIT, 128), bf),
        dma((3, 3, 6)),
        dma((3, 3, 6)),
        dma((3, 3)),
        dma((3, 3)),
        pltpu.SemaphoreType.REGULAR,
        dma((10,)),
        dma((10,)),
        dma((10,)),
        dma((2,)),
        dma((3,)),
        dma((8,)),
        dma((8,)),
        dma((2,)),
    ]
    shapes = [
        ((512, 768), f32),
        ((128, 16, 384), bf),
        ((6, 2304), f32),
        ((6, 768), f32),
        ((6, 3072), f32),
        ((24, 768), f32),
        ((16, 768), f32),
    ]
    return pl.pallas_call(
        backward_kernel,
        out_shape=[jax.ShapeDtypeStruct(*s) for s in shapes],
        in_specs=[pl.BlockSpec(memory_space=pltpu.SMEM)] + [vmem] * 4 + [anywhere] * 10,
        out_specs=[anywhere] * 2 + [vmem] * 5,
        scratch_shapes=scratch,
        compiler_params=pltpu.CompilerParams(
            collective_id=2, has_side_effects=True, vmem_limit_bytes=64 * 1024 * 1024 - 65536
        ),
        name="backward_pass",
    )(lens, vectors, d_pool, x, slots, w, h1, h2, inv, nl, act, gp, qkv, prob, ctx)


def table_kernel(
    rows_ref, asked_ref, qkv_ref, out_ref, up_ref, down_ref, vec_ref, loss_ref, token_ref,
    table_out, token_out, qkv_out, proj_out, up_out, down_out, gain_out, bias_out, loss_out, rows,
):
    at = pl.program_id(0)
    token_out[...] = token_ref[...]

    @pl.when(at == 0)
    def _():
        for q in range(8):
            rows[128 * q : 128 * q + 128, :] = unpack_rows(rows_ref[16 * q : 16 * q + 16])
        for i in range(6):
            qkv_out[i] = qkv_ref[i : i + 1, :]
            proj_out[i] = out_ref[i : i + 1, :]
            up_out[i] = up_ref[i : i + 1, :]
        down_out[0] = down_ref[...]
        me = lax.axis_index("wide") * 8 + lax.axis_index("narrow")
        turned = pltpu.roll(vec_ref[...], 768 - 6 * me, 1)[:, :128]
        gain_out[0] = turned[0:2, 0:6]
        across = turned.T
        for i in range(6):
            bias_out[i] = across[i : i + 1, 2:12]
        loss_out[...] = loss_ref[0:2, 0:4]

    high, low_hot = asked_digits(asked_ref)
    first = (at * (TABLE_STEP // TABLE_BASE)).astype(jnp.float32)
    hot = jnp.concatenate(hot_tiles(high, low_hot, first, TABLE_STEP // TABLE_BASE), axis=0)
    table_out[...] = mm(hot, rows[...])


def table_sums(rows, asked, d_qkv, d_out, d_up, d_down, vectors, loss, tokens, table_rows):
    f32 = jnp.float32
    ins = (rows, asked, d_qkv, d_out, d_up, d_down, vectors, loss)
    outs = [(6, 1, 2304), (6, 1, 768), (6, 1, 3072), (1, 24, 768), (1, 2, 6), (6, 1, 10), (2, 4)]
    steps = table_rows // TABLE_STEP
    token_step = -(-512 // steps // 8) * 8

    def whole(shape):
        return pl.BlockSpec(shape, lambda i: (0,) * len(shape))

    token_block = pl.BlockSpec((token_step, 768), lambda i: (i, 0))
    return pl.pallas_call(
        table_kernel,
        out_shape=[jax.ShapeDtypeStruct(s, f32) for s in [(table_rows, 768), (512, 768)] + outs],
        grid=(steps,),
        in_specs=[whole(v.shape) for v in ins] + [token_block],
        out_specs=[pl.BlockSpec((TABLE_STEP, 768), lambda i: (i, 0)), token_block] + [whole(s) for s in outs],
        scratch_shapes=[pltpu.VMEM((1024, 768), jnp.bfloat16)],
        compiler_params=pltpu.CompilerParams(vmem_limit_bytes=63 * 1024 * 1024),
        name="table_sums",
    )(*ins, tokens)


def shards(token_ids, lengths, groups, table, w_qkv, w_out, w_up, w_down, gains, biases):
    lens = lengths.T
    kept = forward_pass(lens, groups, token_ids, w_qkv, w_out, w_up, w_down, gains, jnp.swapaxes(biases, 1, 2), table)
    w, vecs, h1, h2, inv, nl, act, gate, qkv, prob, ctx, x, d_pool, loss_tile, slots, asked = kept
    token_grads, row_grads, d_qkv, d_out, d_up, d_down, d_vectors = backward_pass(
        lens, vecs, d_pool, x, slots, w, h1, h2, inv, nl, act, gate, qkv, prob, ctx
    )
    table_rows = table.shape[0]
    sums = table_sums(row_grads, asked, d_qkv, d_out, d_up, d_down, d_vectors, loss_tile, token_grads, table_rows)
    table_grads, token_grads, d_qkv, d_out, d_up, d_down, d_gains, d_biases, loss_terms = sums
    return (
        loss_terms.T,
        token_grads.reshape(token_ids.shape + (768,)),
        table_grads,
        jnp.swapaxes(d_qkv, 0, 1),
        jnp.swapaxes(d_out, 0, 1),
        jnp.swapaxes(d_up, 0, 1),
        d_down,
        d_gains,
        jnp.transpose(d_biases, (1, 2, 0)),
    )


def solution(mesh):
    in_specs = (
        P(("wide", "narrow"), None, None),
        P(("wide", "narrow"), None),
        P(("wide", "narrow")),
        P(("wide", "narrow"), None),
        P(None, ("wide", "narrow"), None),
        P(None, ("wide", "narrow"), None),
        P(None, ("wide", "narrow"), None),
        P(None, ("wide", "narrow"), None),
        P(None, None, ("wide", "narrow")),
        P(None, None, ("wide", "narrow")),
    )
    out_specs = (
        P(("wide", "narrow"), None),
        P(("wide", "narrow"), None, None, None),
        P(("wide", "narrow"), None),
        P(None, ("wide", "narrow"), None),
        P(None, ("wide", "narrow"), None),
        P(None, ("wide", "narrow"), None),
        P(None, ("wide", "narrow"), None),
        P(None, None, ("wide", "narrow")),
        P(None, None, ("wide", "narrow")),
    )
    return jax.shard_map(shards, mesh=mesh, in_specs=in_specs, out_specs=out_specs, check_vma=False)
```

```python
import functools

import jax
import jax.numpy as jnp
from jax import lax
from jax.experimental import pallas as pl
from jax.experimental.pallas import tpu as pltpu
from jax.sharding import PartitionSpec as P

HEAD_DIM = 64
SEQ = 64


logit_scale = 10.0
margin = 0.3
norm_eps = 1e-12
pool_eps = 1e-06
far_low = -1e30


MESH = pl.DeviceIdType.MESH
RING = 4
ORDERS = ((0, 1, 2), (1, 2, 0), (2, 0, 1))
UNIT = 48


def where_am_i():
    wide = lax.axis_index("wide")
    narrow = lax.axis_index("narrow")
    return [narrow // 2, wide // RING, wide % RING], narrow % 2


def device_at(spot, core):
    return (spot[1] * RING + spot[2], spot[0] * 2 + core)


def moved(spot, dim, by):
    there = list(spot)
    there[dim] = (spot[dim] + by) % RING
    return there


def block_of(ref, part, core, order, spans):
    return ref.at[(part, core, order) + tuple(pl.ds(*spans[d]) for d in range(3))]


class Gather:
    def __init__(self, out, fifteen, send_sem, recv_sem, spot, core, dims):
        self.out, self.send_sem, self.recv_sem = out, send_sem, recv_sem
        self.spot, self.core, self.dims = spot, core, dims
        self.fifteen = fifteen
        self.sent = []

    def block(self, r, o, spans, core):
        return self.out.at[(r, core, o) + tuple(pl.ds(*spans[d]) for d in self.dims)]

    def here(self, o):
        return {d: (self.spot[d], 1) for d in range(3)}

    def plane(self, o, at, half=None):
        first, second, ring = ORDERS[o]
        spans = {first: (0, RING) if half is None else (2 * half, 2), second: (0, RING), ring: (at, 1)}
        return spans

    def push(self, r, o, event, spans, there, core=None, src=None):
        dst = self.block(r, o, spans, self.core)
        copy = pltpu.make_async_remote_copy(
            src_ref=dst if src is None else src,
            dst_ref=dst,
            send_sem=self.send_sem.at[r, o, event],
            recv_sem=self.recv_sem.at[r, o, event],
            device_id=device_at(there, self.core if core is None else core),
            device_id_type=MESH,
        )
        copy.start()
        return copy

    def landed(self, r, o, event, spans, core=None):
        dst = self.block(r, o, spans, self.core if core is None else core)
        pltpu.make_async_copy(dst, dst, self.recv_sem.at[r, o, event]).wait()

    def begin(self, r, o, src):
        first, second, ring = ORDERS[o]
        here = self.here(o)

        def one(k, _):
            there = moved(moved(self.spot, first, k % RING), second, k // RING)
            self.push(r, o, 0, here, there, src=src)
            return 0

        lax.fori_loop(1, 16, one, 0)

    def plane_done(self, r, o, sem):
        pltpu.make_async_copy(self.fifteen, self.fifteen, sem.at[r, o, 0]).wait()

    def planes(self, r, o):
        self.plane_done(r, o, self.recv_sem)
        self.share(r, o, 5, self.plane(o, self.spot[ORDERS[o][2]]))

    def ring(self, o):
        d = ORDERS[o][2]
        v = self.spot[d]
        up, down = moved(self.spot, d, 1), moved(self.spot, d, -1)
        return v, (v - 1) % RING, (v + 1) % RING, (v + 2) % RING, up, down

    def share(self, r, o, event, spans):
        self.sent.append(self.push(r, o, event, spans, self.spot, 1 - self.core))

    def spread(self, r, o, direct=False):
        v, low, high, far, up, down = self.ring(o)
        here = self.plane(o, v)
        self.sent.append(self.push(r, o, 1, here, up))
        self.sent.append(self.push(r, o, 2, here, down))
        if direct:
            self.sent.append(self.push(r, o, 3, here, moved(self.spot, ORDERS[o][2], 2)))

    def relay(self, r, o):
        v, low, high, far, up, down = self.ring(o)
        self.landed(r, o, 1, self.plane(o, low))
        self.sent.append(self.push(r, o, 3, self.plane(o, low, 0), up))
        self.landed(r, o, 2, self.plane(o, high))
        self.sent.append(self.push(r, o, 4, self.plane(o, high, 1), down))
        self.share(r, o, 6, self.plane(o, low))
        self.share(r, o, 7, self.plane(o, high))

    def finish(self, r, o):
        v, low, high, far, up, down = self.ring(o)
        self.landed(r, o, 3, self.plane(o, far, 0))
        self.landed(r, o, 4, self.plane(o, far, 1))
        self.share(r, o, 8, self.plane(o, far))

    def collect(self, r, o):
        v, low, high, far, up, down = self.ring(o)
        for k, at in enumerate((low, high, far)):
            self.landed(r, o, 1 + k, self.plane(o, at))
            self.share(r, o, 6 + k, self.plane(o, at))

    def shared_done(self, r, o):
        v, low, high, far, up, down = self.ring(o)
        for k, at in enumerate((v, low, high, far)):
            self.landed(r, o, 5 + k, self.plane(o, at), 1 - self.core)

    def drain(self, rounds):
        for r in range(rounds):
            for o in range(3):
                self.plane_done(r, o, self.send_sem)
        for copy in self.sent:
            copy.wait_send()


def mm(a, b):
    return jnp.dot(a, b, preferred_element_type=jnp.float32)


def mm_nt(a, b):
    return lax.dot_general(a, b, (((1,), (1,)), ((), ())), preferred_element_type=jnp.float32)


def mm_tn(a, b):
    return lax.dot_general(a, b, (((0,), (0,)), ((), ())), preferred_element_type=jnp.float32)


def head_mask():
    row = lax.broadcasted_iota(jnp.int32, (256, 256), 0) // HEAD_DIM
    col = lax.broadcasted_iota(jnp.int32, (256, 256), 1) // HEAD_DIM
    return row == col


def spread_heads(part, mask):
    four = jnp.concatenate([part] * 4, axis=0)
    return jnp.where(mask, four, jnp.zeros((), four.dtype))


def gather_heads(wide_part, mask):
    kept = jnp.where(mask, wide_part, 0.0)
    return (kept[:64] + kept[64:128]) + (kept[128:192] + kept[192:])


def panel(w, r, n2):
    c, o, x = n2 // 6, n2 // 2 % 3, n2 % 2 * 2
    pair = [w[r, c, o, x + k].reshape(768, 128) for k in range(2)]
    return jnp.concatenate(pair, axis=1)


def down_panel(w, cb, y):
    c, o = cb // 3, cb % 3
    return jnp.concatenate([w[2, c, o, x, y, z] for z in range(RING) for x in range(RING)], axis=0)


def split_low(value):
    high = value.astype(jnp.bfloat16)
    return high, (value - high.astype(jnp.float32)).astype(jnp.bfloat16)


def greet_all():
    barrier = pltpu.get_barrier_semaphore()
    me = lax.axis_index("wide") * 8 + lax.axis_index("narrow")

    def hello(k, _):
        there = (me + k) % 128
        pl.semaphore_signal(barrier, inc=1, device_id=(there // 8, there % 8), device_id_type=MESH)
        return 0

    lax.fori_loop(1, 128, hello, 0)
    return lambda: pl.semaphore_wait(barrier, 127)


def pack_rows(rows):
    n = rows.shape[0] // 8
    left, right = rows[:, :384].reshape(n, 8, 384), rows[:, 384:].reshape(n, 8, 384)
    return jnp.concatenate([left, right], axis=1).astype(jnp.bfloat16)


def unpack_rows(packed):
    wide_rows = packed.astype(jnp.float32)
    rows = jnp.concatenate([wide_rows[:, :8], wide_rows[:, 8:]], axis=2)
    return rows.reshape(-1, 768).astype(jnp.bfloat16)


def digits(value):
    high = jnp.floor(value * 0.015625)
    return high.astype(jnp.bfloat16), (value - 64.0 * high).astype(jnp.bfloat16)


def token_slots(ids_ref, table_rows):
    f32, bf = jnp.float32, jnp.bfloat16
    sents = jnp.concatenate([ids_ref[s // 2, s % 2 : s % 2 + 1, :] for s in range(8)], axis=0)
    row = lax.broadcasted_iota(jnp.int32, (512, 8), 0)
    col = lax.broadcasted_iota(jnp.int32, (512, 8), 1)
    member_of = (row // SEQ == col).astype(bf)
    wide_ids = jnp.zeros((512, SEQ), f32)
    for shift in (0, 7, 14):
        digit = ((sents >> shift) & 127).astype(f32).astype(bf)
        wide_ids = wide_ids + mm(member_of, digit) * float(1 << shift)
    row = lax.broadcasted_iota(jnp.int32, (512, SEQ), 0)
    col = lax.broadcasted_iota(jnp.int32, (512, SEQ), 1)
    name = jnp.sum(jnp.where(row % SEQ == col, wide_ids, 0.0), axis=1, keepdims=True)
    owner = jnp.floor((name + 0.5) * (1.0 / table_rows))
    local = name - owner * float(table_rows) + 1.0
    lane = lax.broadcasted_iota(jnp.int32, (512, 128), 1).astype(f32)
    hot = (lane == owner).astype(bf)
    row = lax.broadcasted_iota(jnp.int32, (512, 512), 0)
    col = lax.broadcasted_iota(jnp.int32, (512, 512), 1)
    before = mm((col < row).astype(bf), hot)
    rank = jnp.sum(jnp.where(lane == owner, before, 0.0), axis=1, keepdims=True)
    high, low = digits(jnp.broadcast_to(local, (512, 128)))
    zero = jnp.zeros((), bf)
    here = lane == rank
    both = mm_tn(hot, jnp.concatenate([jnp.where(here, high, zero), jnp.where(here, low, zero)], axis=1))
    return owner * 8.0 + rank, both[:, :128] * 64.0 + both[:, 128:]


def two_digits(value, base):
    high = jnp.floor((value + 0.5) * (1.0 / base))
    return high.astype(jnp.bfloat16), (value - base * high).astype(jnp.bfloat16)


def hot_tiles(high, low_hot, first, count):
    zero = jnp.zeros((), jnp.bfloat16)
    return [jnp.where(high == (first + i).astype(jnp.bfloat16), low_hot, zero) for i in range(count)]


def lane_names(rows):
    return lax.broadcasted_iota(jnp.int32, (rows, 128), 1).astype(jnp.float32).astype(jnp.bfloat16)


def slot_hot(slot_ref):
    high, low = two_digits(slot_ref[...], 128.0)
    zero = jnp.zeros((), jnp.bfloat16)
    low_hot = jnp.where(low == lane_names(512), jnp.ones((), jnp.bfloat16), zero)
    return jnp.concatenate(hot_tiles(high, low_hot, jnp.float32(0.0), 8), axis=1)


def forward_kernel(
    lens_ref, groups_ref, ids_ref, wq_ref, wo_ref, wu_ref, wd_ref, gains_ref, bias_ref, table_in,
    w_out, vec_out, h1_out, h2_out, inv_out, nl_out, act_out, gp_out, qkv_out, prob_out, ctx_out, x_out,
    dpool_out, loss_out, slot_out, asked_out,
    w, vecs, tiles, h1, h2, inv, nl, act, gp, qkv, prob, ctx, x_ref, resid, pooled, rnorm, pool_own, pool_swap, pool_all,
    left3, right3, stats, own, sent_ref, near, halves_ref, half_got, table, ids_out, ids_in, ids, asked, rows_out, rows_in,
    row_mat, units_size, pool_size,
    send_sem, recv_sem, local_sem, pool_send, pool_recv, tile_send, tile_recv, swap_sem, save_sem,
    near_send, near_recv, ids_sem, rows_sem, table_sem,
):
    spot, core = where_am_i()
    me = lax.axis_index("wide") * 8 + lax.axis_index("narrow")
    mine = spot[0] * 2 + core
    bf, f32 = jnp.bfloat16, jnp.float32
    all_here = greet_all()
    table_rows = table_in.shape[0]
    get_table = pltpu.make_async_copy(table_in, table.at[pl.ds(0, table_rows)], table_sem.at[0])
    get_table.start()
    table[pl.ds(table_rows, 4096 - table_rows), :] = jnp.zeros((4096 - table_rows, 768), bf)
    slot, wanted = token_slots(ids_ref, table_rows)
    slot_out[...] = jnp.broadcast_to(slot, (512, 128))
    ids[...] = wanted

    def row_out(i, _):
        ids_out[i] = ids[pl.ds(i, 1), :]
        return 0

    lax.fori_loop(0, 128, row_out, 0)

    for c in range(2):
        for o in range(3):
            for x in range(RING):
                n, j = c * 12 + o * 4 + x, 2 * x + c
                source = wq_ref if n < 18 else wo_ref
                cut = slice(128 * (n % 18), 128 * (n % 18) + 128)
                sent_ref[j, 6 * o : 6 * o + 6, :] = source[0, :, cut].astype(f32)
                sent_ref[j, 18 + 6 * o : 24 + 6 * o, :] = wu_ref[0, :, 128 * n : 128 * n + 128].astype(f32)
    lane = lax.broadcasted_iota(jnp.int32, (8, 128), 1)
    place = (lane == 6 * mine + lax.broadcasted_iota(jnp.int32, (8, 128), 0)).astype(bf)[0:6]
    named = jnp.zeros((1, 128), f32)
    for p in range(4):
        named = named + jnp.where(lane[0:1] == 64 + 4 * mine + p, groups_ref[p].astype(f32), 0.0)
    gain_rows, bias_rows = mm(gains_ref[0], place), mm_tn(bias_ref[0], place)
    for j in range(8):
        sent_ref[j, 36:38, :] = gain_rows
        sent_ref[j, 38:48, :] = bias_rows
        sent_ref[j, 36:37, :] = sent_ref[j, 36:37, :] + named
    for o in range(3):
        a, b = wd_ref[0, :, 128 * o : 128 * o + 128], wd_ref[0, :, 384 + 128 * o : 512 + 128 * o]
        a, b = a.astype(f32), b.astype(f32)
        halves_ref[0, o] = jnp.where(core == 0, a, b)
        halves_ref[1, o] = jnp.where(core == 0, b, a)
    all_here()

    sent = []
    for k in range(1, 8):
        there = (mine + k) % 8
        copy = pltpu.make_async_remote_copy(
            src_ref=sent_ref.at[there], dst_ref=near.at[mine], send_sem=near_send.at[k], recv_sem=near_recv.at[k],
            device_id=(lax.axis_index("wide"), there), device_id_type=MESH,
        )
        copy.start()
        sent.append(copy)
    copy = pltpu.make_async_remote_copy(
        src_ref=halves_ref.at[1], dst_ref=half_got, send_sem=near_send.at[0], recv_sem=near_recv.at[0],
        device_id=device_at(spot, 1 - core), device_id_type=MESH,
    )
    copy.start()
    sent.append(copy)

    def ask(k, _):
        there = (me + k) % 128
        pltpu.make_async_remote_copy(
            src_ref=ids_out.at[there], dst_ref=ids_in.at[(128 - k) % 128],
            send_sem=ids_sem.at[0], recv_sem=ids_sem.at[1],
            device_id=(there // 8, there % 8), device_id_type=MESH,
        ).start()
        return 0

    lax.fori_loop(1, 128, ask, 0)
    ids_in[0] = ids_out[me]
    near[mine] = sent_ref[mine]
    for k in range(1, 8):
        ref = near.at[(mine + 8 - k) % 8]
        pltpu.make_async_copy(ref, ref, near_recv.at[k]).wait()
    pltpu.make_async_copy(half_got, half_got, near_recv.at[0]).wait()
    row = lax.broadcasted_iota(jnp.int32, (288, 384), 0)
    col = lax.broadcasted_iota(jnp.int32, (288, 384), 1)
    unit, at = row // UNIT, row % UNIT
    pick = col == at // 6 * UNIT + unit * 6 + at % 6
    units = mm(pick.astype(bf), near[...].reshape(384, 128).astype(bf)).astype(bf)
    for r in range(2):
        for o in range(3):
            first_row = UNIT * (3 * r + o)
            own[r, o] = units[first_row : first_row + UNIT].reshape(1, 1, 1, UNIT, 128)
    for o in range(3):
        a, b = halves_ref[0, o], half_got[o]
        upper, lower = jnp.where(core == 0, a, b), jnp.where(core == 0, b, a)
        own[2, o] = jnp.concatenate([upper, lower], axis=0).astype(bf).reshape(1, 1, 1, UNIT, 128)
    small = jnp.zeros((16, 128), f32)
    for j in range(8):
        small = small + near[j, 32:48, :]
    tiles[pl.ds(spot[1], 1), pl.ds(spot[2], 1)] = small.astype(bf).reshape(1, 1, 16, 128)

    g = Gather(w, units_size, send_sem, recv_sem, spot, core, (0, 1, 2))
    every = [(r, o) for r in range(3) for o in range(3)]
    keep = []
    for r, o in every:
        copy = pltpu.make_async_copy(own.at[r, o], g.block(r, o, g.here(o), core), local_sem.at[r, o])
        copy.start()
        keep.append(copy)
        if r < 2:
            g.begin(r, o, own.at[r, o])

    def tile_push(event, at, there):
        ref = tiles.at[at]
        copy = pltpu.make_async_remote_copy(
            src_ref=ref, dst_ref=ref, send_sem=tile_send.at[event], recv_sem=tile_recv.at[event],
            device_id=device_at(there, core), device_id_type=MESH,
        )
        copy.start()
        sent.append(copy)

    def tile_at(phase, v):
        return (pl.ds(v, 1), pl.ds(spot[2], 1)) if phase == 0 else (pl.ds(0, RING), pl.ds(v, 1))

    def tile_spread(phase):
        for k, by in enumerate((1, 2, 3)):
            tile_push(3 * phase + k, tile_at(phase, spot[phase + 1]), moved(spot, phase + 1, by))

    def tile_landed(phase):
        for k, by in enumerate((1, 2, 3)):
            ref = tiles.at[tile_at(phase, (spot[phase + 1] + RING - by) % RING)]
            pltpu.make_async_copy(ref, ref, tile_recv.at[3 * phase + k]).wait()

    tile_spread(0)
    for copy in keep:
        copy.wait()

    others = ids_in.at[pl.ds(0, 127)]
    pltpu.make_async_copy(others, others, ids_sem.at[1]).wait()

    def row_in(i, _):
        ids[pl.ds(i, 1), :] = ids_in[i]
        return 0

    lax.fori_loop(0, 128, row_in, 0)
    high, low = digits(ids[...])
    row = lax.broadcasted_iota(jnp.int32, (1024, 128), 0)
    col = lax.broadcasted_iota(jnp.int32, (1024, 128), 1)
    member_of = (row // 8 == col).astype(bf)
    both = mm(member_of, high) * 64.0 + mm(member_of, low)
    asked_col = jnp.sum(jnp.where(col == row % 8, both, 0.0), axis=1, keepdims=True) - 1.0
    asked[...] = jnp.broadcast_to(asked_col, (1024, 128))
    row = lax.broadcasted_iota(jnp.int32, (128, 1024), 0)
    col = lax.broadcasted_iota(jnp.int32, (128, 1024), 1)
    member_of = (col // 8 == row).astype(bf)
    both = mm_tn(high, member_of) * 64.0 + mm_tn(low, member_of)
    asked_row = jnp.sum(jnp.where(row == col % 8, both, 0.0), axis=0, keepdims=True) - 1.0
    asked_out[...] = jnp.broadcast_to(asked_row, (8, 1024))
    get_table.wait()

    def find(half):
        high, low = two_digits(asked[512 * half : 512 * half + 512, :], 128.0)
        low_hot = jnp.where(low == lane_names(512), jnp.ones((), bf), jnp.zeros((), bf))

        def chunk(i, _):
            hot = jnp.concatenate(hot_tiles(high, low_hot, (4 * i).astype(f32), 4), axis=1)
            part = mm(hot, table[pl.ds(pl.multiple_of(i * 512, 512), 512), :])
            resid[...] = jnp.where(i == 0, part, resid[...] + part)
            return 0

        lax.fori_loop(0, 8, chunk, 0)
        for q in range(4):
            rows_out[64 * half + 16 * q : 64 * half + 16 * q + 16] = pack_rows(resid[128 * q : 128 * q + 128, :])

        def answer(k, _):
            there = (me + k) % 128
            pltpu.make_async_remote_copy(
                src_ref=rows_out.at[k], dst_ref=rows_in.at[me], send_sem=rows_sem.at[0], recv_sem=rows_sem.at[1],
                device_id=(there // 8, there % 8), device_id_type=MESH,
            ).start()
            return 0

        lax.fori_loop(max(1, 64 * half), 64 * half + 64, answer, 0)

    find(0)
    rows_in[me] = rows_out[0]
    tile_landed(0)
    tile_spread(1)
    for o in range(3):
        g.planes(0, o)
        g.spread(0, o)
    find(1)
    for o in range(3):
        g.relay(0, o)
    for o in range(3):
        g.planes(1, o)
    tile_landed(1)

    row_at = lax.broadcasted_iota(jnp.int32, (128, 768), 0)
    col_at = lax.broadcasted_iota(jnp.int32, (128, 768), 1)
    all_vec = jnp.zeros((16, 768), f32)
    all_grp = jnp.zeros((16, 512), f32)
    for slab in range(16):
        part = tiles[slab // RING, slab % RING]
        pick = (col_at == row_at + UNIT * slab) & (row_at < UNIT)
        all_vec = all_vec + mm(part, pick.astype(bf))
        pick = (col_at == row_at - 64 + 32 * slab) & (row_at >= 64) & (row_at < 96)
        all_grp = all_grp + mm(part, pick[:, :512].astype(bf))
    vecs[...] = jnp.concatenate([all_vec[4:16], all_vec[0:4]], axis=0)
    group_row = all_grp[4:5]
    saves = []

    def save(scratch, out, at):
        copy = pltpu.make_async_copy(scratch, out, save_sem.at[at])
        copy.start()
        saves.append(copy)

    def collect(r):
        for o in range(3):
            g.collect(r, o)

    def arrived(r):
        for o in range(3):
            g.shared_done(r, o)
        save(w.at[r], w_out.at[r], 11 + r)

    save(vecs, vec_out, 0)
    for o in range(3):
        g.finish(0, o)
    others = rows_in.at[pl.ds(0, 127)]
    pltpu.make_async_copy(others, others, rows_sem.at[1]).wait()
    for o in range(3):
        g.spread(1, o, True)
    for o in range(3):
        g.begin(2, o, own.at[2, o])
    for q in range(8):
        row_mat[128 * q : 128 * q + 128, :] = unpack_rows(rows_in[16 * q : 16 * q + 16])
    slots_hot = slot_hot(slot_out)
    for p in range(3):
        cut = slice(256 * p, 256 * p + 256)
        x_ref[:, cut] = mm(slots_hot, row_mat[:, cut]).astype(bf)
    save(x_ref, x_out, 10)
    arrived(0)
    mask = head_mask()

    def qkv_step(n2, _):
        kind, p = n2 // 3, n2 % 3
        rows = vecs[2:4, :]
        bias = jnp.where(kind == 0, rows[0:1], jnp.where(kind == 2, rows[1:2], 0.0))
        bias = jnp.where(p == 0, bias[:, :256], jnp.where(p == 1, bias[:, 256:512], bias[:, 512:]))
        qkv[n2] = (mm(x_ref[...], panel(w, 0, n2)) + bias).astype(bf)
        return 0

    lax.fori_loop(0, 9, qkv_step, 0)
    save(qkv, qkv_out, 1)

    def attend(s, _):
        rows = pl.ds(pl.multiple_of(s * SEQ, SEQ), SEQ)
        slot = lax.broadcasted_iota(jnp.int32, (SEQ, 256), 0)
        live = slot < lens_ref[s % 2, s // 2]
        for p in range(3):
            query, key_part, value = qkv[p, rows, :], qkv[3 + p, rows, :], qkv[6 + p, rows, :]
            scores = mm_nt(key_part, spread_heads(query, mask)) * 0.125
            scores = jnp.where(live, scores, far_low)
            powers = jnp.exp(scores - jnp.max(scores, axis=0, keepdims=True))
            probs = powers / jnp.sum(powers, axis=0, keepdims=True)
            prob[s, p] = probs
            ctx[p, rows, :] = gather_heads(mm_tn(probs.astype(bf), value), mask).astype(bf)
        return 0

    lax.fori_loop(0, 4, attend, 0)
    collect(1)
    for o in range(3):
        g.planes(2, o)
        g.spread(2, o, True)
    lax.fori_loop(4, 8, attend, 0)
    save(prob, prob_out, 2)
    save(ctx, ctx_out, 3)
    context = jnp.concatenate([ctx[0], ctx[1], ctx[2]], axis=1)
    for p in range(3):
        resid[:, 256 * p : 256 * p + 256] = mm(context, panel(w, 0, 9 + p))

    def norm_one_step(s, _):
        rows = pl.ds(pl.multiple_of(s * SEQ, SEQ), SEQ)
        value = x_ref[rows, :].astype(f32) + (resid[rows, :] + vecs[4:5, :])
        centred = value - jnp.mean(value, axis=1, keepdims=True)
        inverse = lax.rsqrt(jnp.mean(centred * centred, axis=1, keepdims=True) + norm_eps)
        scaled = centred * inverse
        h1[rows, :] = scaled
        inv[0, rows, :] = jnp.broadcast_to(inverse, (SEQ, 128))
        normed = scaled * vecs[0:1, :] + vecs[5:6, :]
        nl[rows, :] = normed.astype(bf)
        resid[rows, :] = normed + vecs[6:7, :]
        return 0

    lax.fori_loop(0, 8, norm_one_step, 0)
    save(h1, h1_out, 4)
    save(nl, nl_out, 5)
    arrived(1)

    def up_step(n2, _):
        weight = panel(w, 1, n2)
        q, p = n2 // 3, n2 % 3
        rows = vecs[8:12, :]
        bias = jnp.where(q == 0, rows[0:1], jnp.where(q == 1, rows[1:2], jnp.where(q == 2, rows[2:3], rows[3:4])))
        bias = jnp.where(p == 0, bias[:, :256], jnp.where(p == 1, bias[:, 256:512], bias[:, 512:]))
        for half in range(4):
            part = pl.ds(128 * half, 128)
            pre = mm(nl[part, :], weight) + bias
            upper = 0.5 + 0.5 * lax.erf(pre * 0.7071067811865476)
            act[n2, part, :] = (pre * upper).astype(bf)
            gp[n2, part, :] = upper + pre * (jnp.exp(-0.5 * pre * pre) * 0.3989422804014327)
        return 0

    lax.fori_loop(0, 4, up_step, 0)
    collect(2)
    lax.fori_loop(4, 12, up_step, 0)
    save(act, act_out, 6)
    save(gp, gp_out, 7)
    arrived(2)

    def down_step(y, _):
        hidden = jnp.concatenate([act[3 * y], act[3 * y + 1], act[3 * y + 2]], axis=1)
        for p in range(3):
            weight = jnp.concatenate([down_panel(w, 2 * p, y), down_panel(w, 2 * p + 1, y)], axis=1)
            cols = slice(256 * p, 256 * p + 256)
            resid[:, cols] = resid[:, cols] + mm(hidden, weight)
        return 0

    lax.fori_loop(0, RING, down_step, 0)

    def norm_two_step(s, _):
        rows = pl.ds(pl.multiple_of(s * SEQ, SEQ), SEQ)
        value = resid[rows, :]
        centred = value - jnp.mean(value, axis=1, keepdims=True)
        inverse = lax.rsqrt(jnp.mean(centred * centred, axis=1, keepdims=True) + norm_eps)
        scaled = centred * inverse
        h2[rows, :] = scaled
        inv[1, rows, :] = jnp.broadcast_to(inverse, (SEQ, 128))
        state = scaled * vecs[1:2, :] + vecs[7:8, :]
        live = lax.broadcasted_iota(jnp.int32, (SEQ, 768), 0) < lens_ref[s % 2, s // 2]
        mean_vec = jnp.sum(jnp.where(live, state, 0.0), axis=0, keepdims=True) / lens_ref[s % 2, s // 2].astype(f32)
        r = lax.rsqrt(jnp.sum(mean_vec * mean_vec, axis=1, keepdims=True) + pool_eps)
        pooled[s] = mean_vec * r
        rnorm[s] = jnp.broadcast_to(r, (1, 768))
        return 0

    lax.fori_loop(0, 8, norm_two_step, 0)
    save(h2, h2_out, 8)
    save(inv, inv_out, 9)

    sources = jnp.concatenate([pooled[2 * i] for i in range(4)], axis=0)
    targets = jnp.concatenate([pooled[2 * i + 1] for i in range(4)], axis=0)
    first = core == 0
    pad = jnp.zeros((4, 768), f32)
    pool_own[0] = jnp.concatenate([jnp.where(first, targets, sources), pad], axis=0)
    swap = pltpu.make_async_remote_copy(
        src_ref=pool_own.at[0], dst_ref=pool_swap, send_sem=swap_sem.at[0], recv_sem=swap_sem.at[1],
        device_id=device_at(spot, 1 - core), device_id_type=MESH,
    )
    swap.start()
    swap.wait()
    got = pool_swap[0:4, :]
    kind = jnp.concatenate(
        [jnp.where(first, sources, got), jnp.where(first, got, targets)], axis=0
    )
    q = Gather(pool_all, pool_size, pool_send, pool_recv, spot, core, (1, 2, 0))
    for o in range(3):
        unit = jnp.concatenate([kind[:, 256 * o : 256 * o + 128], kind[:, 256 * o + 128 : 256 * o + 256]], axis=0)
        here = (pl.ds(spot[1], 1), pl.ds(spot[2], 1), pl.ds(spot[0], 1))
        pool_all[(0, core, o) + here] = unit.reshape(1, 1, 1, 16, 128)
    for o in range(3):
        q.begin(0, o, None)
    for o in range(3):
        q.planes(0, o)
        q.spread(0, o, True)
    for o in range(3):
        q.collect(0, o)
    for o in range(3):
        q.shared_done(0, o)

    for k, out in ((0, left3), (1, right3)):
        for o in range(3):
            for h in range(2):
                block = pool_all[0, k, o, :, :, :, 8 * h : 8 * h + 8, :].reshape(512, 128)
                high, low = split_low(block)
                at = 256 * o + 128 * h
                parts = (high, high, low) if k == 0 else (high, low, high)
                for i in range(3):
                    out[:, 768 * i + at : 768 * i + at + 128] = parts[i]
    pair_row = lax.broadcasted_iota(jnp.int32, (512, 256), 0)
    pair_col = lax.broadcasted_iota(jnp.int32, (512, 256), 1)
    names = lax.broadcasted_iota(jnp.int32, (16, 512), 0).astype(f32)
    member = (names == group_row).astype(bf)

    def column_lse(rows3, cols3, into):
        for p in range(2):
            cut = slice(256 * p, 256 * p + 256)
            scores = logit_scale * mm_nt(rows3[...], cols3[cut, :])
            scores = scores - jnp.where(pair_row == pair_col + 256 * p, logit_scale * margin, 0.0)
            alike = mm_tn(member, member[:, cut]) > 0.5
            scores = jnp.where(alike, scores, far_low)
            peak = jnp.max(scores, axis=0, keepdims=True)
            total = jnp.sum(jnp.exp(scores - peak), axis=0, keepdims=True)
            stats[into : into + 1, cut] = peak + jnp.log(total)

    column_lse(left3, right3, 0)
    column_lse(right3, left3, 1)
    chip = (spot[1] * RING + spot[2]) * RING + spot[0]
    mine = pl.ds(pl.multiple_of(chip * 8, 8), 8)
    weight = 1.0 / 1024.0
    at_row = lax.broadcasted_iota(jnp.int32, (8, 512), 0) + chip * 8
    at_col = lax.broadcasted_iota(jnp.int32, (8, 512), 1)
    own_pair = at_row == at_col
    pick = (lax.broadcasted_iota(jnp.int32, (8, 512), 1) == at_row).astype(bf)
    own_member = mm_nt(pick, member)
    alike = mm(own_member.astype(bf), member) > 0.5
    grads = []
    terms = []
    for k, (rows3, cols3) in enumerate(((left3, right3), (right3, left3))):
        block = pool_all[0, k, :, pl.ds(spot[1], 1), pl.ds(spot[2], 1), pl.ds(spot[0], 1)]
        cut = [block[o, 0, 0, 0, 8 * h : 8 * h + 8, :] for o in range(3) for h in range(2)]
        own8 = jnp.concatenate(cut, axis=1)
        high, low = split_low(own8)
        parts = (high, high, low) if k == 0 else (high, low, high)
        scores = logit_scale * mm_nt(jnp.concatenate(parts, axis=1), cols3[...])
        scores = scores - jnp.where(own_pair, logit_scale * margin, 0.0)
        diagonal = jnp.sum(jnp.where(own_pair, scores, 0.0), axis=1, keepdims=True)
        scores = jnp.where(alike, scores, far_low)
        peak = jnp.max(scores, axis=1, keepdims=True)
        lse = peak + jnp.log(jnp.sum(jnp.exp(scores - peak), axis=1, keepdims=True))
        other = stats[k : k + 1, :]
        mix = weight * (jnp.exp(scores - lse) + jnp.exp(scores - other))
        mix = mix - jnp.where(own_pair, 2.0 * weight, 0.0)
        mix_high, mix_low = split_low(mix)
        high_at, low_at = (0, 768) if k == 0 else (0, 1536)
        high_cols, low_cols = cols3[:, high_at : high_at + 768], cols3[:, low_at : low_at + 768]
        grad = mm(mix_high, high_cols) + mm(mix_high, low_cols) + mm(mix_low, high_cols)
        grads.append(logit_scale * jnp.where(first, grad[0:4], grad[4:8]))
        terms.append(jnp.where(first, (lse - diagonal)[0:4], (lse - diagonal)[4:8]))
    row = lax.broadcasted_iota(jnp.int32, (4, 128), 0)
    lane = lax.broadcasted_iota(jnp.int32, (4, 128), 1)
    rows = [jnp.sum(jnp.where(row == lane, terms[k], 0.0), axis=0, keepdims=True) for k in range(2)]
    loss_out[...] = jnp.concatenate(rows + [jnp.zeros((6, 128), f32)], axis=0)
    for s in range(8):
        d_row = grads[s % 2][s // 2 : s // 2 + 1, :]
        row = pooled[s]
        inner = jnp.sum(row * d_row, axis=1, keepdims=True)
        dpool_out[s] = rnorm[s] * (d_row - row * inner) / lens_ref[s % 2, s // 2].astype(f32)
    g.drain(3)
    q.drain(1)
    for copy in sent:
        copy.wait_send()
    for sem, ref in ((ids_sem, ids_in), (rows_sem, rows_in)):
        others = ref.at[pl.ds(0, 127)]
        pltpu.make_async_copy(others, others, sem.at[0]).wait()
    for copy in saves:
        copy.wait()


def forward_pass(lengths, groups, ids, w_qkv, w_out, w_up, w_down, gains, biases, table):
    bf, f32 = jnp.bfloat16, jnp.float32
    shapes = [
        ((3, 2, 3, RING, RING, RING, UNIT, 128), bf),
        ((16, 768), f32),
        ((512, 768), f32),
        ((512, 768), f32),
        ((2, 512, 128), f32),
        ((512, 768), bf),
        ((12, 512, 256), bf),
        ((12, 512, 256), f32),
        ((9, 512, 256), bf),
        ((8, 3, SEQ, 256), f32),
        ((3, 512, 256), bf),
        ((512, 768), bf),
        ((8, 1, 768), f32),
        ((8, 128), f32),
        ((512, 128), f32),
        ((8, 1024), f32),
    ]
    anywhere = pl.BlockSpec(memory_space=pl.ANY)
    vmem = pl.BlockSpec(memory_space=pltpu.VMEM)
    dma = pltpu.SemaphoreType.DMA
    return pl.pallas_call(
        forward_kernel,
        out_shape=[jax.ShapeDtypeStruct(*s) for s in shapes],
        in_specs=[pl.BlockSpec(memory_space=pltpu.SMEM)] * 2 + [vmem] * 7 + [anywhere],
        out_specs=[anywhere] * 12 + [vmem] * 4,
        scratch_shapes=[
            pltpu.VMEM(*shapes[0]),
            pltpu.VMEM(*shapes[1]),
            pltpu.VMEM((RING, RING, 16, 128), bf),
            *[pltpu.VMEM(*s) for s in shapes[2:12]],
            pltpu.VMEM((512, 768), f32),
            pltpu.VMEM((8, 1, 768), f32),
            pltpu.VMEM((8, 1, 768), f32),
            pltpu.VMEM((1, 8, 768), f32),
            pltpu.VMEM((8, 768), f32),
            pltpu.VMEM((1, 2, 3, RING, RING, RING, 16, 128), f32),
            pltpu.VMEM((512, 2304), bf),
            pltpu.VMEM((512, 2304), bf),
            pltpu.VMEM((8, 512), f32),
            pltpu.VMEM((3, 3, 1, 1, 1, UNIT, 128), bf),
            pltpu.VMEM((8, UNIT, 128), f32),
            pltpu.VMEM((8, UNIT, 128), f32),
            pltpu.VMEM((2, 3, 24, 128), f32),
            pltpu.VMEM((3, 24, 128), f32),
            pltpu.VMEM((4096, 768), bf),
            pltpu.VMEM((128, 1, 128), f32),
            pltpu.VMEM((128, 1, 128), f32),
            pltpu.VMEM((128, 128), f32),
            pltpu.VMEM((1024, 128), f32),
            pltpu.VMEM((128, 16, 384), bf),
            pltpu.VMEM((128, 16, 384), bf),
            pltpu.VMEM((1024, 768), bf),
            pltpu.VMEM((15, UNIT, 128), bf),
            pltpu.VMEM((15, 16, 128), f32),
            dma((3, 3, 9)),
            dma((3, 3, 9)),
            dma((3, 3)),
            dma((1, 3, 9)),
            dma((1, 3, 9)),
            dma((6,)),
            dma((6,)),
            dma((2,)),
            dma((14,)),
            dma((8,)),
            dma((8,)),
            dma((2,)),
            dma((2,)),
            dma((1,)),
        ],
        compiler_params=pltpu.CompilerParams(
            collective_id=1, has_side_effects=True, vmem_limit_bytes=62 * 1024 * 1024
        ),
        name="forward_pass",
    )(lengths, groups, ids, w_qkv, w_out, w_up, w_down, gains, biases, table)


class Reduce:
    def __init__(self, parts, bufs, plane, out, send_sem, recv_sem, spot, core):
        self.parts, self.bufs, self.plane_in, self.out = parts, bufs, plane, out
        self.send_sem, self.recv_sem = send_sem, recv_sem
        self.spot, self.core = spot, core
        self.sent = []

    def copy(self, src, dst, r, o, event, there):
        copy = pltpu.make_async_remote_copy(
            src_ref=src,
            dst_ref=dst,
            send_sem=self.send_sem.at[r, o, event],
            recv_sem=self.recv_sem.at[r, o, event],
            device_id=device_at(there, self.core),
            device_id_type=MESH,
        )
        copy.start()
        return copy

    def landed(self, dst, r, o, event):
        pltpu.make_async_copy(dst, dst, self.recv_sem.at[r, o, event]).wait()

    def spans(self, o, at, half=None):
        ring, first, second = ORDERS[o]
        return {ring: (at, 1), first: (0, RING) if half is None else (2 * half, 2), second: (0, RING)}

    def mine(self, r, o, spans):
        return block_of(self.parts, r, self.core, o, spans)

    def slot(self, r, o, which):
        return self.bufs[o * 2].at[r, which] if which < 3 else self.bufs[o * 2 + 1].at[0, which - 3]

    def add_into(self, into, others):
        sizes = into.shape[:3]

        def one(i, _):
            at = (i // sizes[1], i % sizes[1])
            if len(others) == 1:
                into[at] = into[at] + others[0][at]
            else:
                value = into[at].astype(jnp.float32)
                for other in others:
                    value = value + other[at].astype(jnp.float32)
                into[at] = value.astype(jnp.bfloat16)
            return 0

        lax.fori_loop(0, sizes[0] * sizes[1], one, 0)

    def first(self, r, o):
        d = ORDERS[o][0]
        if True:
            for by in (1, 3, 2):
                there = moved(self.spot, d, by)
                src = self.mine(r, o, self.spans(o, there[d]))
                self.sent.append(self.copy(src, self.slot(r, o, by - 1), r, o, by - 1, there))
            return
        across = (self.spot[d] + 2) % RING
        for half, by in ((0, 1), (1, -1)):
            src = self.mine(r, o, self.spans(o, across, half))
            self.sent.append(self.copy(src, self.slot(r, o, 3 + half), r, o, 2 + 3 * half, moved(self.spot, d, by)))

    def second(self, r, o):
        d = ORDERS[o][0]
        for half, by in ((0, 1), (1, -1)):
            at = (self.spot[d] + by) % RING
            view = self.slot(r, o, 3 + half)
            self.landed(view, r, o, 2 + 3 * half)
            self.add_into(self.mine(r, o, self.spans(o, at, half)), [view])
            src = self.mine(r, o, self.spans(o, at))
            self.sent.append(self.copy(src, self.slot(r, o, half), r, o, half, moved(self.spot, d, by)))

    def third(self, r, o):
        ring, first, second = ORDERS[o]
        views = [self.slot(r, o, k) for k in range(3)]
        for k, view in enumerate(views):
            self.landed(view, r, o, k)
        self.add_into(self.mine(r, o, self.spans(o, self.spot[ring])), views)

        def one(k, _):
            there = moved(moved(self.spot, first, k % RING), second, k // RING)
            src = self.mine(r, o, {d: (there[d], 1) for d in range(3)})
            self.copy(src, self.plane_in.at[r, o, pl.ds(k, 1), pl.ds(0, 1), pl.ds(0, 1)], r, o, 4, there)
            return 0

        lax.fori_loop(1, 16, one, 0)

    def fourth(self, r, o):
        others = self.plane_in.at[r, o, pl.ds(1, 15)]
        self.landed(others, r, o, 4)
        here = self.mine(r, o, {d: (self.spot[d], 1) for d in range(3)})
        total = here[0, 0, 0].astype(jnp.float32)
        for k in range(1, 16):
            total = total + self.plane_in[r, o, k, 0, 0].astype(jnp.float32)
        self.out[r, o] = total

    def drain(self):
        for r in range(3):
            for o in range(3):
                others = self.plane_in.at[r, o, pl.ds(1, 15)]
                pltpu.make_async_copy(others, others, self.send_sem.at[r, o, 4]).wait()
        for copy in self.sent:
            copy.wait_send()


def reduce_buffers(rounds):
    bufs = []
    for o in range(3):
        ring, first, second = ORDERS[o]
        sizes = [RING] * 3
        sizes[ring] = 1
        half = list(sizes)
        half[first] = 2
        bufs.append(pltpu.VMEM((rounds, 3, *sizes, UNIT, 128), jnp.bfloat16))
        bufs.append(pltpu.VMEM((1, 2, *half, UNIT, 128), jnp.bfloat16))
    return bufs


TABLE_STEP = 784
TABLE_BASE = 112


def asked_digits(asked_ref):
    high, low = two_digits(jnp.broadcast_to(asked_ref[0:1, :], (TABLE_BASE, 1024)), float(TABLE_BASE))
    name = lax.broadcasted_iota(jnp.int32, (TABLE_BASE, 1024), 0).astype(jnp.float32).astype(jnp.bfloat16)
    return high, jnp.where(low == name, jnp.ones((), jnp.bfloat16), jnp.zeros((), jnp.bfloat16))


def norm_back(grad, scaled, inverse, gain):
    e = grad * gain
    mean_e = jnp.mean(e, axis=1, keepdims=True)
    mean_eh = jnp.mean(e * scaled, axis=1, keepdims=True)
    return inverse * (e - mean_e - scaled * mean_eh)


def backward_kernel(
    lens_ref, vec_ref, dpool_ref, x_ref, slot_ref,
    w_in, h1_in, h2_in, inv_in, nl_in, act_in, gp_in, qkv_in, prob_in, ctx_in,
    token_out, rows_in, qkv_out, out_out, up_out, down_out, vec_out,
    w, h1, h2, inv, nl, act, gp, qkv, prob, ctx, parts, d2d, d_res, d_low, turned, dvec, vec_slots, red_out, near_out, near_in, half_in, rows_out, *rest,
):
    bufs, plane_in, rest = rest[:6], rest[6], rest[7:]
    send_sem, recv_sem, swap_send, swap_recv, free_sem, vec_send, vec_recv, load_sem, gp_sem, w_sem, near_send, near_recv, rows_sem = rest
    me = lax.axis_index("wide") * 8 + lax.axis_index("narrow")
    spot, core = where_am_i()
    bf, f32 = jnp.bfloat16, jnp.float32

    def load(src, dst, at):
        copy = pltpu.make_async_copy(src, dst, load_sem.at[at])
        copy.start()
        return copy

    def load_w(r, at):
        copy = pltpu.make_async_copy(w_in.at[r], w.at[at], w_sem.at[r])
        copy.start()
        return copy

    def load_gp(y, at):
        return pltpu.make_async_copy(gp_in.at[pl.ds(3 * y, 3)], gp.at[at], gp_sem.at[at])

    get_h2, get_inv = load(h2_in, h2, 0), load(inv_in, inv, 1)
    get_act = load(act_in, act, 2)
    get_w2 = load_w(2, 0)
    load_gp(0, 0).start()
    load_gp(1, 1).start()
    get_nl = load(nl_in, nl, 3)
    get_w1 = load_w(1, 1)
    get_h1, get_ctx = load(h1_in, h1, 4), load(ctx_in, ctx, 5)
    get_qkv, get_prob = load(qkv_in, qkv, 6), load(prob_in, prob, 7)
    all_here = greet_all()
    red = Reduce(parts, bufs, plane_in, red_out, send_sem, recv_sem, spot, core)
    swaps = {}

    def give(r):
        if r == 0:
            pl.semaphore_wait(free_sem, 1)
        for o in range(3):
            copy = pltpu.make_async_remote_copy(
                src_ref=parts.at[r, 1 - core, o], dst_ref=d2d.at[r % 2, o],
                send_sem=swap_send.at[r, o], recv_sem=swap_recv.at[r, o],
                device_id=device_at(spot, 1 - core), device_id_type=MESH,
            )
            copy.start()
            red.sent.append(copy)

    def take(r):
        for o in range(3):
            view = d2d.at[r % 2, o]
            pltpu.make_async_copy(view, view, swap_recv.at[r, o]).wait()
            red.add_into(parts.at[r, core, o], [view])
            red.first(r, o)
        if r == 2:
            pl.semaphore_signal(free_sem, inc=1, device_id=device_at(spot, 1 - core), device_id_type=MESH)

    def second(r):
        for o in range(3):
            red.second(r, o)

    def third(r):
        for o in range(3):
            red.third(r, o)

    def fourth(r):
        for o in range(3):
            red.fourth(r, o)

    dvec[0] = jnp.zeros((16, 768), f32)

    def add_vec(row, value):
        dvec[0, row : row + 1, :] = dvec[0, row : row + 1, :] + value

    def total(value):
        return jnp.sum(value, axis=0, keepdims=True)

    get_h2.wait()
    get_inv.wait()

    def norm_two_step(s, _):
        rows = pl.ds(pl.multiple_of(s * SEQ, SEQ), SEQ)
        live = lax.broadcasted_iota(jnp.int32, (SEQ, 768), 0) < lens_ref[s % 2, s // 2]
        grad = jnp.where(live, jnp.broadcast_to(dpool_ref[s], (SEQ, 768)), 0.0)
        scaled = h2[rows, :]
        inverse = inv[1, rows, 0:1]
        back = norm_back(grad, scaled, inverse, vec_ref[1:2, :])
        low = back.astype(bf)
        d_res[rows, :] = back
        d_low[rows, :] = low
        add_vec(1, total(grad * scaled))
        add_vec(7, total(grad))
        add_vec(6, total(low.astype(f32)))
        return 0

    lax.fori_loop(0, 8, norm_two_step, 0)
    get_act.wait()

    def down_step(y, _):
        hidden = jnp.concatenate([act[3 * y], act[3 * y + 1], act[3 * y + 2]], axis=1)
        turned[...] = hidden.T
        for p in range(3):
            block = mm(turned[...], d_low[:, 256 * p : 256 * p + 256]).astype(bf)
            for k in range(2):
                cb = 2 * p + k
                for z in range(RING):
                    for x in range(RING):
                        at = UNIT * (RING * z + x)
                        parts[2, cb // 3, cb % 3, x, y, z] = block[at : at + UNIT, 128 * k : 128 * k + 128]
        return 0

    lax.fori_loop(0, RING, down_step, 0)
    all_here()
    give(2)
    get_w2.wait()

    def pre_step(y, _):
        at = y % 2
        load_gp(y, at).wait()
        columns = [
            jnp.concatenate([w[0, cb // 3, cb % 3, x, y, z] for z in range(RING) for x in range(RING)], axis=0)
            for cb in range(6)
        ]
        weight = jnp.concatenate(columns, axis=1)
        for j in range(3):
            grad = mm_nt(d_low[...], weight[256 * j : 256 * j + 256, :]) * gp[at, j]
            low = grad.astype(bf)
            act[3 * y + j] = low
            cut = slice(256 * j, 256 * j + 256)
            dvec[0, pl.ds(8 + y, 1), cut] = total(low.astype(f32))

        @pl.when(y < 2)
        def _():
            load_gp(y + 2, at).start()

        return 0

    lax.fori_loop(0, RING, pre_step, 0)
    get_w0 = load_w(0, 0)
    get_nl.wait()
    turned_nl = nl[...].T
    turned[:, :] = turned_nl

    def up_step(n2, _):
        block = mm(turned[...], act[n2]).astype(bf)
        c, o, x = n2 // 6, n2 // 2 % 3, n2 % 2 * 2
        for k in range(2):
            parts[1, c, o, x + k] = block[:, 128 * k : 128 * k + 128].reshape(RING, RING, UNIT, 128)
        return 0

    lax.fori_loop(0, 12, up_step, 0, unroll=3)
    give(1)
    take(2)
    get_w1.wait()

    def six_blocks(at, n):
        blocks = []
        for k in range(6):
            m = n + k
            blocks.append(w[at, m // 12, m // 4 % 3, m % 4].reshape(768, 128))
        return jnp.concatenate(blocks, axis=1)

    def up_back_step(t, _):
        low = jnp.concatenate([act[3 * t], act[3 * t + 1], act[3 * t + 2]], axis=1)
        weight = six_blocks(1, 6 * t)
        for p in range(3):
            cut = slice(256 * p, 256 * p + 256)
            d_res[:, cut] = d_res[:, cut] + mm_nt(low, weight[cut, :])
        return 0

    lax.fori_loop(0, RING, up_back_step, 0)
    get_h1.wait()

    def norm_one_step(s, _):
        rows = pl.ds(pl.multiple_of(s * SEQ, SEQ), SEQ)
        grad, scaled = d_res[rows, :], h1[rows, :]
        back = norm_back(grad, scaled, inv[0, rows, 0:1], vec_ref[0:1, :])
        low = back.astype(bf)
        d_res[rows, :] = back
        d_low[rows, :] = low
        add_vec(0, total(grad * scaled))
        add_vec(5, total(grad))
        add_vec(4, total(low.astype(f32)))
        return 0

    lax.fori_loop(0, 8, norm_one_step, 0)
    take(1)
    get_ctx.wait()
    turned[...] = jnp.concatenate([ctx[0], ctx[1], ctx[2]], axis=1).T
    get_w0.wait()
    weight = six_blocks(0, 18)
    for p in range(3):
        cut = slice(256 * p, 256 * p + 256)
        block = mm(turned[...], d_low[:, cut]).astype(bf)
        for k in range(2):
            n = 18 + 2 * p + k
            parts[0, n // 12, n // 4 % 3, n % 4] = block[:, 128 * k : 128 * k + 128].reshape(RING, RING, UNIT, 128)
        ctx[p] = mm_nt(d_low[...], weight[cut, :]).astype(bf)
    get_qkv.wait()
    get_prob.wait()
    mask = head_mask()

    def attend_back(s, _):
        rows = pl.ds(pl.multiple_of(s * SEQ, SEQ), SEQ)
        for p in range(3):
            query, key_part, value = qkv[p, rows, :], qkv[3 + p, rows, :], qkv[6 + p, rows, :]
            wide_grad = spread_heads(ctx[p, rows, :], mask)
            probs = prob[s, p]
            d_value = mm(probs.astype(bf), wide_grad)
            d_probs = mm_nt(value, wide_grad)
            centre = jnp.sum(probs * d_probs, axis=0, keepdims=True)
            d_scores = (probs * (d_probs - centre)).astype(bf)
            d_query = gather_heads(mm_tn(d_scores, key_part), mask) * 0.125
            d_key = mm(d_scores, spread_heads(query, mask)) * 0.125
            low_query, low_value = d_query.astype(bf), d_value.astype(bf)
            qkv[p, rows, :] = low_query
            qkv[3 + p, rows, :] = d_key.astype(bf)
            qkv[6 + p, rows, :] = low_value
            cut = slice(256 * p, 256 * p + 256)
            dvec[0, 2:3, cut] = dvec[0, 2:3, cut] + total(low_query.astype(f32))
            dvec[0, 3:4, cut] = dvec[0, 3:4, cut] + total(low_value.astype(f32))
        return 0

    lax.fori_loop(0, 4, attend_back, 0)
    third(2)
    lax.fori_loop(4, 8, attend_back, 0)
    vec_sent = []

    def vec_push(event, src, there, c):
        copy = pltpu.make_async_remote_copy(
            src_ref=src, dst_ref=vec_slots.at[event], send_sem=vec_send.at[event], recv_sem=vec_recv.at[event],
            device_id=device_at(there, c), device_id_type=MESH,
        )
        copy.start()
        vec_sent.append(copy)

    def vec_landed(event):
        ref = vec_slots.at[event]
        pltpu.make_async_copy(ref, ref, vec_recv.at[event]).wait()

    def vec_start(d):
        for by in (1, 2, 3):
            vec_push(3 * d + by, dvec.at[d + 1], moved(spot, d, by), core)

    def vec_add(d):
        for by in (1, 2, 3):
            vec_landed(3 * d + by)
        sides = vec_slots[1 + 3 * d] + vec_slots[3 + 3 * d]
        dvec[d + 2] = (dvec[d + 1] + sides) + vec_slots[2 + 3 * d]

    vec_push(0, dvec.at[0], spot, 1 - core)

    third(1)
    def input_step(t, _):
        low = jnp.concatenate([qkv[3 * t], qkv[3 * t + 1], qkv[3 * t + 2]], axis=1)
        weight = six_blocks(0, 6 * t)
        for p in range(3):
            cut = slice(256 * p, 256 * p + 256)
            d_res[:, cut] = d_res[:, cut] + mm_nt(low, weight[cut, :])
        return 0

    lax.fori_loop(0, 3, input_step, 0)
    token_copy = pltpu.make_async_copy(d_res, token_out, load_sem.at[8])
    token_copy.start()
    d_low[...] = d_res[...].astype(bf)
    slots_hot = slot_hot(slot_ref)
    for q in range(4):
        rows = mm_tn(slots_hot[:, 256 * q : 256 * q + 256], d_low[...])
        rows_out[32 * q : 32 * q + 32] = pack_rows(rows)

    def hand_back(k, _):
        there = (me + k) % 128
        pltpu.make_async_remote_copy(
            src_ref=rows_out.at[there], dst_ref=rows_in.at[(128 - k) % 128],
            send_sem=rows_sem.at[0], recv_sem=rows_sem.at[1],
            device_id=(there // 8, there % 8), device_id_type=MESH,
        ).start()
        return 0

    lax.fori_loop(1, 128, hand_back, 0)
    keep_rows = pltpu.make_async_copy(rows_out.at[me], rows_in.at[0], load_sem.at[9])
    keep_rows.start()
    turned[...] = x_ref[...].T

    def qkv_step(i, _):
        n2 = (i + 6 * (1 - core)) % 9
        block = mm(turned[...], qkv[n2]).astype(bf)
        c, o, x = n2 // 6, n2 // 2 % 3, n2 % 2 * 2
        for k in range(2):
            parts[0, c, o, x + k] = block[:, 128 * k : 128 * k + 128].reshape(RING, RING, UNIT, 128)
        return 0

    lax.fori_loop(0, 6, qkv_step, 0, unroll=3)
    give(0)
    lax.fori_loop(6, 9, qkv_step, 0, unroll=3)
    vec_landed(0)
    dvec[1] = dvec[0] + vec_slots[0]
    vec_start(0)
    fourth(2)
    take(0)
    vec_add(0)
    vec_start(1)
    fourth(1)
    vec_add(1)
    vec_start(2)
    third(0)
    vec_add(2)
    vec_out[...] = dvec[4]
    fourth(0)

    mine = spot[0] * 2 + core
    for j in range(8):
        for r in range(2):
            for o in range(3):
                at = 6 * (3 * r + o)
                near_out[j, at : at + 6, :] = red_out[r, o, 6 * j : 6 * j + 6, :]
    for k in range(1, 8):
        there = (mine + k) % 8
        copy = pltpu.make_async_remote_copy(
            src_ref=near_out.at[there], dst_ref=near_in.at[mine], send_sem=near_send.at[k], recv_sem=near_recv.at[k],
            device_id=(lax.axis_index("wide"), there), device_id_type=MESH,
        )
        copy.start()
        vec_sent.append(copy)
    theirs = pl.ds(pl.multiple_of(24 * (1 - core), 8), 24)
    copy = pltpu.make_async_remote_copy(
        src_ref=red_out.at[2, :, theirs], dst_ref=half_in, send_sem=near_send.at[0], recv_sem=near_recv.at[0],
        device_id=device_at(spot, 1 - core), device_id_type=MESH,
    )
    copy.start()
    vec_sent.append(copy)
    near_in[mine] = near_out[mine]
    for k in range(1, 8):
        ref = near_in.at[(mine + 8 - k) % 8]
        pltpu.make_async_copy(ref, ref, near_recv.at[k]).wait()
    pltpu.make_async_copy(half_in, half_in, near_recv.at[0]).wait()
    for c in range(2):
        for o in range(3):
            for x in range(RING):
                n, j = c * 12 + o * 4 + x, 2 * x + c
                block = near_in[j, 6 * o : 6 * o + 6, :]
                if n < 18:
                    qkv_out[:, 128 * n : 128 * n + 128] = block
                else:
                    out_out[:, 128 * (n - 18) : 128 * (n - 18) + 128] = block
                up_out[:, 128 * n : 128 * n + 128] = near_in[j, 18 + 6 * o : 24 + 6 * o, :]
    ours = pl.ds(pl.multiple_of(24 * core, 8), 24)
    for o in range(3):
        a, b = red_out[2, o, ours, :], half_in[o]
        down_out[:, 128 * o : 128 * o + 128] = jnp.where(core == 0, a, b)
        down_out[:, 384 + 128 * o : 512 + 128 * o] = jnp.where(core == 0, b, a)
    others = rows_in.at[pl.ds(0, 127)]
    pltpu.make_async_copy(others, others, rows_sem.at[1]).wait()
    pltpu.make_async_copy(others, others, rows_sem.at[0]).wait()
    token_copy.wait()
    keep_rows.wait()
    red.drain()
    for copy in vec_sent:
        copy.wait_send()


def backward_pass(lens, vectors, d_pool, x, slots, w, h1, h2, inv, nl, act, gp, qkv, prob, ctx):
    bf, f32 = jnp.bfloat16, jnp.float32
    anywhere = pl.BlockSpec(memory_space=pl.ANY)
    vmem = pl.BlockSpec(memory_space=pltpu.VMEM)
    dma = pltpu.SemaphoreType.DMA
    scratch = [
        pltpu.VMEM((2, *w.shape[1:]), bf),
        pltpu.VMEM(h1.shape, f32),
        pltpu.VMEM(h2.shape, f32),
        pltpu.VMEM(inv.shape, f32),
        pltpu.VMEM(nl.shape, bf),
        pltpu.VMEM(act.shape, bf),
        pltpu.VMEM((2, 3, 512, 256), f32),
        pltpu.VMEM(qkv.shape, bf),
        pltpu.VMEM(prob.shape, f32),
        pltpu.VMEM(ctx.shape, bf),
        pltpu.VMEM(w.shape, bf),
        pltpu.VMEM((2, *w.shape[2:]), bf),
        pltpu.VMEM((512, 768), f32),
        pltpu.VMEM((512, 768), bf),
        pltpu.VMEM((768, 512), bf),
        pltpu.VMEM((5, 16, 768), f32),
        pltpu.VMEM((10, 16, 768), f32),
        pltpu.VMEM((3, 3, UNIT, 128), f32),
        pltpu.VMEM((8, 40, 128), f32),
        pltpu.VMEM((8, 40, 128), f32),
        pltpu.VMEM((3, 24, 128), f32),
        pltpu.VMEM((128, 16, 384), bf),
        *reduce_buffers(3),
        pltpu.VMEM((3, 3, 16, 1, 1, UNIT, 128), bf),
        dma((3, 3, 6)),
        dma((3, 3, 6)),
        dma((3, 3)),
        dma((3, 3)),
        pltpu.SemaphoreType.REGULAR,
        dma((10,)),
        dma((10,)),
        dma((10,)),
        dma((2,)),
        dma((3,)),
        dma((8,)),
        dma((8,)),
        dma((2,)),
    ]
    shapes = [
        ((512, 768), f32),
        ((128, 16, 384), bf),
        ((6, 2304), f32),
        ((6, 768), f32),
        ((6, 3072), f32),
        ((24, 768), f32),
        ((16, 768), f32),
    ]
    return pl.pallas_call(
        backward_kernel,
        out_shape=[jax.ShapeDtypeStruct(*s) for s in shapes],
        in_specs=[pl.BlockSpec(memory_space=pltpu.SMEM)] + [vmem] * 4 + [anywhere] * 10,
        out_specs=[anywhere] * 2 + [vmem] * 5,
        scratch_shapes=scratch,
        compiler_params=pltpu.CompilerParams(
            collective_id=2, has_side_effects=True, vmem_limit_bytes=64 * 1024 * 1024 - 65536
        ),
        name="backward_pass",
    )(lens, vectors, d_pool, x, slots, w, h1, h2, inv, nl, act, gp, qkv, prob, ctx)


def table_kernel(
    rows_ref, asked_ref, qkv_ref, out_ref, up_ref, down_ref, vec_ref, loss_ref, token_ref,
    table_out, token_out, qkv_out, proj_out, up_out, down_out, gain_out, bias_out, loss_out, rows,
):
    at = pl.program_id(0)
    token_out[...] = token_ref[...]

    @pl.when(at == 0)
    def _():
        for q in range(8):
            rows[128 * q : 128 * q + 128, :] = unpack_rows(rows_ref[16 * q : 16 * q + 16])
        for i in range(6):
            qkv_out[i] = qkv_ref[i : i + 1, :]
            proj_out[i] = out_ref[i : i + 1, :]
            up_out[i] = up_ref[i : i + 1, :]
        down_out[0] = down_ref[...]
        me = lax.axis_index("wide") * 8 + lax.axis_index("narrow")
        turned = pltpu.roll(vec_ref[...], 768 - 6 * me, 1)[:, :128]
        gain_out[0] = turned[0:2, 0:6]
        across = turned.T
        for i in range(6):
            bias_out[i] = across[i : i + 1, 2:12]
        loss_out[...] = loss_ref[0:2, 0:4]

    high, low_hot = asked_digits(asked_ref)
    first = (at * (TABLE_STEP // TABLE_BASE)).astype(jnp.float32)
    hot = jnp.concatenate(hot_tiles(high, low_hot, first, TABLE_STEP // TABLE_BASE), axis=0)
    table_out[...] = mm(hot, rows[...])


def table_sums(rows, asked, d_qkv, d_out, d_up, d_down, vectors, loss, tokens, table_rows):
    f32 = jnp.float32
    ins = (rows, asked, d_qkv, d_out, d_up, d_down, vectors, loss)
    outs = [(6, 1, 2304), (6, 1, 768), (6, 1, 3072), (1, 24, 768), (1, 2, 6), (6, 1, 10), (2, 4)]
    steps = table_rows // TABLE_STEP
    token_step = -(-512 // steps // 8) * 8

    def whole(shape):
        return pl.BlockSpec(shape, lambda i: (0,) * len(shape))

    token_block = pl.BlockSpec((token_step, 768), lambda i: (i, 0))
    return pl.pallas_call(
        table_kernel,
        out_shape=[jax.ShapeDtypeStruct(s, f32) for s in [(table_rows, 768), (512, 768)] + outs],
        grid=(steps,),
        in_specs=[whole(v.shape) for v in ins] + [token_block],
        out_specs=[pl.BlockSpec((TABLE_STEP, 768), lambda i: (i, 0)), token_block] + [whole(s) for s in outs],
        scratch_shapes=[pltpu.VMEM((1024, 768), jnp.bfloat16)],
        compiler_params=pltpu.CompilerParams(vmem_limit_bytes=63 * 1024 * 1024),
        name="table_sums",
    )(*ins, tokens)


def shards(token_ids, lengths, groups, table, w_qkv, w_out, w_up, w_down, gains, biases):
    lens = lengths.T
    kept = forward_pass(lens, groups, token_ids, w_qkv, w_out, w_up, w_down, gains, jnp.swapaxes(biases, 1, 2), table)
    w, vecs, h1, h2, inv, nl, act, gate, qkv, prob, ctx, x, d_pool, loss_tile, slots, asked = kept
    token_grads, row_grads, d_qkv, d_out, d_up, d_down, d_vectors = backward_pass(
        lens, vecs, d_pool, x, slots, w, h1, h2, inv, nl, act, gate, qkv, prob, ctx
    )
    table_rows = table.shape[0]
    sums = table_sums(row_grads, asked, d_qkv, d_out, d_up, d_down, d_vectors, loss_tile, token_grads, table_rows)
    table_grads, token_grads, d_qkv, d_out, d_up, d_down, d_gains, d_biases, loss_terms = sums
    return (
        loss_terms.T,
        token_grads.reshape(token_ids.shape + (768,)),
        table_grads,
        jnp.swapaxes(d_qkv, 0, 1),
        jnp.swapaxes(d_out, 0, 1),
        jnp.swapaxes(d_up, 0, 1),
        d_down,
        d_gains,
        jnp.transpose(d_biases, (1, 2, 0)),
    )


def solution(mesh):
    in_specs = (
        P(("wide", "narrow"), None, None),
        P(("wide", "narrow"), None),
        P(("wide", "narrow")),
        P(("wide", "narrow"), None),
        P(None, ("wide", "narrow"), None),
        P(None, ("wide", "narrow"), None),
        P(None, ("wide", "narrow"), None),
        P(None, ("wide", "narrow"), None),
        P(None, None, ("wide", "narrow")),
        P(None, None, ("wide", "narrow")),
    )
    out_specs = (
        P(("wide", "narrow"), None),
        P(("wide", "narrow"), None, None, None),
        P(("wide", "narrow"), None),
        P(None, ("wide", "narrow"), None),
        P(None, ("wide", "narrow"), None),
        P(None, ("wide", "narrow"), None),
        P(None, ("wide", "narrow"), None),
        P(None, None, ("wide", "narrow")),
        P(None, None, ("wide", "narrow")),
    )
    return jax.shard_map(shards, mesh=mesh, in_specs=in_specs, out_specs=out_specs, check_vma=False)
```
